32 devices in a mesh: tower: 2 (over core), dp: 16 (over z, y, x).
Axes of the slice: x: 2, y: 2, z: 4, core: 2. Of those that a mesh axis runs over, the one named last changes fastest.
Arguments:
- block_input: bfloat16 [2, 17280, 768], P('tower', 'dp'), may hold values from -6 to 6
- segments: int32 [224, 77], P('dp'), may hold values from 0 to 19, as said below
- caption_ends: int32 [320], P('dp'), may hold values from 15 to 1077, as said below
- pair_flags: int32 [320], replicated, may hold values from 0 to 1, as said below
- attention_gain: float32 [2, 768], P('tower'), may hold values from 0.1 to 1.9
- attention_bias: float32 [2, 768], P('tower'), may hold values from -3 to 3
- triple_weight: bfloat16 [2, 3, 768, 768], P('tower'), may hold values from -0.21875 to 0.21875
- triple_bias: float32 [2, 2, 768], P('tower'), may hold values from -3 to 3
- mixer_weight: bfloat16 [2, 768, 768], P('tower'), may hold values from -1.25 to 1.25
- mixer_bias: float32 [2, 768], P('tower'), may hold values from -3 to 3
- feed_gain: float32 [2, 768], P('tower'), may hold values from 0.1 to 1.9
- feed_bias: float32 [2, 768], P('tower'), may hold values from -3 to 3
- widen_weight: bfloat16 [2, 768, 3072], P('tower'), may hold values from -0.21875 to 0.21875
- widen_bias: float32 [2, 3072], P('tower'), may hold values from -3 to 3
- narrow_weight: bfloat16 [2, 3072, 768], P('tower'), may hold values from -0.15625 to 0.15625
- narrow_bias: float32 [2, 768], P('tower'), may hold values from -3 to 3
- final_gain: float32 [2, 768], P('tower'), may hold values from 0.1 to 1.9
- final_bias: float32 [2, 768], P('tower'), may hold values from -3 to 3
- embed_weight: bfloat16 [2, 768, 512], P('tower'), may hold values from -0.21875 to 0.21875
- logit_scale: float32 [], replicated, may hold values from 3.6 to 4.4
- loss_scale: float32 [], replicated, may hold values from 160 to 640
Outputs:
- mean_loss: float32 [], replicated
- accuracy: float32 [], replicated
- block_input_gradient: float32 [2, 17280, 768], P('tower', 'dp')
- attention_gain_gradient: float32 [2, 768], P('tower', 'dp')
- attention_bias_gradient: float32 [2, 768], P('tower', 'dp')
- triple_weight_gradient: float32 [2, 3, 768, 768], P('tower', None, 'dp')
- triple_bias_gradient: float32 [2, 2, 768], P('tower', None, 'dp')
- mixer_weight_gradient: float32 [2, 768, 768], P('tower', 'dp')
- mixer_bias_gradient: float32 [2, 768], P('tower', 'dp')
- feed_gain_gradient: float32 [2, 768], P('tower', 'dp')
- feed_bias_gradient: float32 [2, 768], P('tower', 'dp')
- widen_weight_gradient: float32 [2, 768, 3072], P('tower', None, 'dp')
- widen_bias_gradient: float32 [2, 3072], P('tower', 'dp')
- narrow_weight_gradient: float32 [2, 3072, 768], P('tower', 'dp')
- narrow_bias_gradient: float32 [2, 768], P('tower', 'dp')
- final_gain_gradient: float32 [2, 768], P('tower', 'dp')
- final_bias_gradient: float32 [2, 768], P('tower', 'dp')
- embed_weight_gradient: float32 [2, 768, 512], P('tower', 'dp')
- logit_scale_gradient: float32 [], replicated
The draws below stay inside these ranges and needn't reach their ends.
Inputs may be any that keep to these rules, and one draw needn't show every extreme that they name: `segments`: the 14 caption rows of each dp index hold captions 0 to 19 in order, one or two whole captions a row, each of 16 to 77 tokens; caption k of dp index d is pair d * 20 + k. caption_ends[c] is the last position, counted over the 1078 tokens of its dp index, where segments holds c mod 20. `pair_flags`: the last pair is real.
All inputs are finite; a program needn't handle non-finite values.
Results may differ from the reference program's by a relative error of at most 0.024.
Values may be sent and summed in bfloat16 or wider, within the bound.
No kernel may reach another device: no remote copies, remote signals or barrier semaphores. Data moves between devices by JAX's collectives and lax.ppermute only.
A program may use at most 256 MiB of HBM per device.

```python
import math
import jax
import jax.numpy as jnp
from jax import lax

D_IMG = 768
MLP_IMG = 3072
D_TXT = 512
MLP_TXT = 2048
EMB = 512
HEAD = 64
IMG_TOK = 50
CTX = 77
IMG_DEV = 20
TXT_ROWS = 14
TOK_PAD = 1080
PAIRS = 320
N_DP = 16


def caption_layout(key):
    folded = jax.random.fold_in(key, 17)
    device_keys = jax.random.split(folded, N_DP)

    def one_device(device_key):
        first_key, second_key = jax.random.split(device_key)
        shuffled = jax.random.permutation(first_key, TXT_ROWS)
        double = shuffled < IMG_DEV - TXT_ROWS
        split_at = jax.random.randint(second_key, (TXT_ROWS,), 16, CTX - 16)
        per_row = 1 + double.astype(jnp.int32)
        row_start = jnp.cumsum(per_row) - per_row
        positions = lax.iota(jnp.int32, CTX)
        later = (double[:, None] & (positions[None, :] >= split_at[:, None])).astype(jnp.int32)
        segment_rows = row_start[:, None] + later
        row_base = lax.iota(jnp.int32, TXT_ROWS) * CTX
        first_end = jnp.where(double, row_base + split_at - 1, row_base + CTX - 1)
        second_slot = jnp.where(double, row_start + 1, IMG_DEV)
        end_rows = jnp.zeros((IMG_DEV,), jnp.int32).at[row_start].set(first_end)
        end_rows = end_rows.at[second_slot].set(row_base + CTX - 1, mode='drop')
        return (segment_rows, end_rows)
    segment_rows, end_rows = jax.vmap(one_device)(device_keys)
    return (segment_rows.reshape(N_DP * TXT_ROWS, CTX), end_rows.reshape(PAIRS))


def draw_segments(key, part):
    return caption_layout(key)[0]


def draw_caption_ends(key, part):
    return caption_layout(key)[1]


def draw_pair_flags(key, part):
    folded = jax.random.fold_in(key, 29)
    ticket = jax.random.randint(folded, (PAIRS,), 0, 1000)
    limit = 250 + 600 * lax.iota(jnp.int32, PAIRS) // PAIRS
    flags = (ticket < limit).astype(jnp.int32)
    return flags.at[PAIRS - 1].set(1)


def levels(rng, shape, shards, low, top_value):
    def one(position, shards_of):
        steps = jax.random.uniform(jax.random.fold_in(jax.random.fold_in(rng, 6), position), (shards_of,), jnp.float32, low / len(shards), top_value / len(shards))
        return jnp.repeat(jnp.exp(steps), shape[position] // shards_of).reshape((-1,) + (1,) * (len(shape) - position - 1))

    level = one(*shards[0])
    for cut in shards[1:]:
        level = level * one(*cut)
    return level


def normal_values(key, extent, deviation, reach, shards=(), kind=jnp.bfloat16):
    drawn = deviation * jax.random.normal(key, extent, jnp.float32)
    if shards:
        drawn = drawn * levels(key, extent, shards, -0.22, 0.18)
    return jnp.clip(drawn, -reach, reach).astype(kind)


def setup_inputs(seed: int = 0) -> dict:
    seeds = jax.random.split(jax.random.key(seed), 22)
    block_input = normal_values(seeds[0], (2, N_DP * TOK_PAD, D_IMG), 1.0, 6.0, ((0, 2), (1, 16)))
    segments = draw_segments(jax.random.fold_in(seeds[21], 71), 0)
    caption_ends = draw_caption_ends(jax.random.fold_in(seeds[21], 71), 0)
    pair_flags = draw_pair_flags(jax.random.fold_in(seeds[21], 71), 0)
    attention_gain = jnp.clip(1.0 + 0.18 * jax.random.normal(seeds[4], (2, D_IMG), jnp.float32), 0.1, 1.9)
    attention_bias = normal_values(seeds[5], (2, D_IMG), 0.3, 3.0, ((0, 2),), jnp.float32)
    triple_weight = normal_values(seeds[6], (2, 3, D_IMG, D_IMG), D_IMG ** -0.5, 0.21875, ((0, 2),))
    triple_bias = normal_values(seeds[7], (2, 2, D_IMG), 0.3, 3.0, ((0, 2),), jnp.float32)
    mixer_weight = normal_values(seeds[8], (2, D_IMG, D_IMG), (D_IMG // 36) ** -0.5, 1.25, ((0, 2),))
    mixer_bias = normal_values(seeds[9], (2, D_IMG), 0.3, 3.0, ((0, 2),), jnp.float32)
    feed_gain = jnp.clip(1.0 + 0.18 * jax.random.normal(seeds[10], (2, D_IMG), jnp.float32), 0.1, 1.9)
    feed_bias = normal_values(seeds[11], (2, D_IMG), 0.3, 3.0, ((0, 2),), jnp.float32)
    widen_weight = normal_values(seeds[12], (2, D_IMG, MLP_IMG), D_IMG ** -0.5, 0.21875, ((0, 2),))
    widen_bias = normal_values(seeds[13], (2, MLP_IMG), 0.3, 3.0, ((0, 2),), jnp.float32)
    narrow_weight = normal_values(seeds[14], (2, MLP_IMG, D_IMG), (MLP_IMG // 2) ** -0.5, 0.15625, ((0, 2),))
    narrow_bias = normal_values(seeds[15], (2, D_IMG), 0.3, 3.0, ((0, 2),), jnp.float32)
    final_gain = jnp.clip(1.0 + 0.18 * jax.random.normal(seeds[16], (2, D_IMG), jnp.float32), 0.1, 1.9)
    final_bias = normal_values(seeds[17], (2, D_IMG), 0.3, 3.0, ((0, 2),), jnp.float32)
    embed_weight = normal_values(seeds[18], (2, D_IMG, EMB), D_IMG ** -0.5, 0.21875, ((0, 2),))
    logit_scale = jnp.clip(jax.random.uniform(seeds[19], (), jnp.float32, 3.6, 4.4), 3.6, 4.4)
    loss_scale = jnp.clip(jnp.exp(jax.random.uniform(seeds[20], (), jnp.float32, math.log(160.0), math.log(640.0))), 160.0, 640.0)
    return {"block_input": block_input, "segments": segments, "caption_ends": caption_ends, "pair_flags": pair_flags, "attention_gain": attention_gain, "attention_bias": attention_bias, "triple_weight": triple_weight, "triple_bias": triple_bias, "mixer_weight": mixer_weight, "mixer_bias": mixer_bias, "feed_gain": feed_gain, "feed_bias": feed_bias, "widen_weight": widen_weight, "widen_bias": widen_bias, "narrow_weight": narrow_weight, "narrow_bias": narrow_bias, "final_gain": final_gain, "final_bias": final_bias, "embed_weight": embed_weight, "logit_scale": logit_scale, "loss_scale": loss_scale}


precise = lax.Precision.HIGHEST

@jax.custom_vjp
def low(v):
    return lax.optimization_barrier(v.astype(jnp.bfloat16)).astype(jnp.float32)

@jax.custom_vjp
def low_back(v):
    return v

def low_keep(v):
    return (low(v), None)

def low_pass(kept, grad):
    return (grad,)

def back_keep(v):
    return (v, None)

def back_low(kept, grad):
    return (low(grad),)
low.defvjp(low_keep, low_pass)
low_back.defvjp(back_keep, back_low)

def layer_norm(stream, norm_gain, norm_offset):
    centre = stream - lax.optimization_barrier(jnp.mean(stream, axis=-1, keepdims=True))
    invert = lax.rsqrt(lax.optimization_barrier(jnp.mean(centre * centre, axis=-1, keepdims=True)) + 1e-05)
    return centre * invert * norm_gain + norm_offset

def product(left, right):
    return jnp.dot(left, right, precision=precise)

def crop_params(weights, which, width, hidden):
    return (weights[0][which, :width], weights[1][which, :width], weights[2][which, :, :width, :width], weights[3][which, :, :width], weights[4][which, :width, :width], weights[5][which, :width], weights[6][which, :width], weights[7][which, :width], weights[8][which, :width, :hidden], weights[9][which, :hidden], weights[10][which, :hidden, :width], weights[11][which, :width], weights[12][which, :width], weights[13][which, :width], weights[14][which, :width])

def tower_pass(stream, params, heads, allowed, pooling):
    groups, length, width = stream.shape
    attention_gain, attention_bias, triple_weight, triple_bias, mixer_weight, mixer_bias, feed_gain, feed_bias, widen_weight, widen_bias, narrow_weight, narrow_bias, final_gain, final_bias, embed_weight = params
    normed_one = low(layer_norm(stream, attention_gain, attention_bias))
    query = low(low_back(product(normed_one, triple_weight[0]) + triple_bias[0]))
    key_rows = low(low_back(product(normed_one, triple_weight[1])))
    values = low(low_back(product(normed_one, triple_weight[2]) + triple_bias[1]))
    shaped = (groups, length, heads, HEAD)
    scores = jnp.einsum('gqhd,gkhd->ghqk', query.reshape(shaped), key_rows.reshape(shaped), precision=precise) * 0.125
    scores = low_back(jnp.where(allowed, scores, -1e+30))
    weights_low = low(jax.nn.softmax(scores, axis=-1))
    mixed = jnp.einsum('ghqk,gkhd->gqhd', weights_low, values.reshape(shaped), precision=precise)
    mixed = low(low_back(mixed.reshape(groups, length, width)))
    middle = stream + low_back(product(mixed, mixer_weight) + mixer_bias)
    normed_two = low(layer_norm(middle, feed_gain, feed_bias))
    hidden_pre = low_back(product(normed_two, widen_weight) + widen_bias)
    activated = low(hidden_pre * jax.nn.sigmoid(1.702 * hidden_pre))
    output = middle + low_back(product(activated, narrow_weight) + narrow_bias)
    pooled = pooling(output)
    normed_three = low(layer_norm(pooled, final_gain, final_bias))
    embedded = low_back(product(normed_three, embed_weight))
    return low(embedded * lax.rsqrt(lax.optimization_barrier(jnp.sum(embedded * embedded, axis=-1, keepdims=True)) + 1e-06))

def contrast(own_rows, other_rows, factor, live_flags):
    logits = low_back(factor * jnp.dot(own_rows, other_rows.T, precision=precise))
    masked = jnp.where(live_flags[None, :] > 0.5, logits, -1e+30)
    log_total = jax.nn.logsumexp(masked, axis=-1)
    matched = jnp.diagonal(logits)
    return (jnp.sum(live_flags * (log_total - matched)), jnp.sum(live_flags * jnp.exp(matched - log_total)))

def reference(block_input, segments, caption_ends, pair_flags, attention_gain, attention_bias, triple_weight, triple_bias, mixer_weight, mixer_bias, feed_gain, feed_bias, widen_weight, widen_bias, narrow_weight, narrow_bias, final_gain, final_bias, embed_weight, logit_scale, loss_scale):
    weights_in = tuple((member.astype(jnp.float32) for member in (attention_gain, attention_bias, triple_weight, triple_bias, mixer_weight, mixer_bias, feed_gain, feed_bias, widen_weight, widen_bias, narrow_weight, narrow_bias, final_gain, final_bias, embed_weight)))
    block_float = block_input.astype(jnp.float32)
    live_flags = (pair_flags > 0).astype(jnp.float32)
    live_pairs = jnp.sum(live_flags)
    positions = lax.iota(jnp.int32, CTX)
    causal = positions[None, :] <= positions[:, None]
    allowed_text = (causal[None] & (segments[:, :, None] == segments[:, None, :]))[:, None]
    allowed_image = jnp.ones((1, 1, IMG_TOK, IMG_TOK), dtype=jnp.bool_)
    owner_rows = lax.iota(jnp.int32, PAIRS) // IMG_DEV

    def text_pool(output):
        flat_rows = output.reshape(N_DP, TXT_ROWS * CTX, D_TXT)
        return flat_rows[owner_rows, caption_ends]

    def objective(block, weights, scale_log):
        image_params = crop_params(weights, 0, D_IMG, MLP_IMG)
        text_params = crop_params(weights, 1, D_TXT, MLP_TXT)
        image_stream = block[0].reshape(N_DP, TOK_PAD, D_IMG)[:, :IMG_DEV * IMG_TOK].reshape(PAIRS, IMG_TOK, D_IMG)
        text_stream = block[1].reshape(N_DP, TOK_PAD, D_IMG)[:, :TXT_ROWS * CTX, :D_TXT].reshape(N_DP * TXT_ROWS, CTX, D_TXT)
        image_units = tower_pass(image_stream, image_params, D_IMG // HEAD, allowed_image, lambda output: output[:, 0])
        text_units = tower_pass(text_stream, text_params, D_TXT // HEAD, allowed_text, text_pool)
        factor = jnp.exp(scale_log)
        loss_one, hits_one = contrast(image_units, text_units, factor, live_flags)
        loss_two, hits_two = contrast(text_units, image_units, factor, live_flags)
        return ((loss_one + loss_two) / (2.0 * live_pairs), (hits_one + hits_two) / (2.0 * live_pairs))
    mean_loss, pullback, accuracy = jax.vjp(objective, block_float, weights_in, logit_scale.astype(jnp.float32), has_aux=True)
    block_grad, weight_grads, scale_grad = pullback(loss_scale.astype(jnp.float32))
    return (mean_loss, accuracy, block_grad, weight_grads[0], weight_grads[1], weight_grads[2], weight_grads[3], weight_grads[4], weight_grads[5], weight_grads[6], weight_grads[7], weight_grads[8], weight_grads[9], weight_grads[10], weight_grads[11], weight_grads[12], weight_grads[13], weight_grads[14], scale_grad)
```

```python
from functools import partial

import jax
import jax.numpy as jnp
from jax import lax
from jax.experimental import pallas as pl
from jax.experimental.pallas import tpu as pltpu
from jax.sharding import PartitionSpec as P

D_TXT = 512
MLP_TXT = 2048
HEAD = 64
IMG_TOK = 50
CTX = 77
F32 = jnp.float32
BF16 = jnp.bfloat16
VMEM_LIMIT = 60 * 1024 * 1024
CHUNK = 1024
NORM_ROWS = 272
PROJECT_ROWS = 1088
WINDOW = 256


def dot_dims(left, right, left_dim, right_dim, precision=None):
    return lax.dot_general(
        left,
        right,
        (((left_dim,), (right_dim,)), ((), ())),
        preferred_element_type=F32,
        precision=precision,
    )


def mm(left, right):
    return dot_dims(left, right, 1, 0)


def mm_nt(left, right):
    return dot_dims(left, right, 1, 1)


def mm_tn(left, right):
    return dot_dims(left, right, 0, 0)


def iota(shape, dim):
    return lax.broadcasted_iota(jnp.int32, shape, dim)


def sigmoid(rows):
    return 1.0 / (1.0 + jnp.exp(-rows))


def one_hot(condition):
    return condition.astype(F32).astype(BF16)


def normed(rows, mask, width):
    mean = jnp.sum(rows * mask, axis=-1, keepdims=True) / width
    centre = (rows - mean) * mask
    invert = lax.rsqrt(jnp.sum(centre * centre, axis=-1, keepdims=True) / width + 1e-05)
    return centre * invert, invert


def norm_back(rows_hat, invert, gain, upward, mask, width):
    scaled = upward * gain
    mean = jnp.sum(scaled, axis=-1, keepdims=True) / width
    along = jnp.sum(scaled * rows_hat, axis=-1, keepdims=True) / width
    return invert * (scaled - mean * mask - rows_hat * along)


def sums_of(rows):
    return jnp.sum(rows, axis=0, keepdims=True)


def head_mask(rows, pairs, width):
    row = iota((rows, width), 0)
    first = lax.shift_right_logical(iota((rows, width), 1), 6) * pairs
    return (row >= first) & (row < first + pairs)


def repeat_rows(rows, pairs):
    row = iota((rows, pairs), 0)
    return one_hot(lax.rem(row, pairs) == iota((rows, pairs), 1))


def tower_sizes(full_width, full_hidden):
    is_text = lax.axis_index("tower") != 0
    width = jnp.where(is_text, D_TXT, full_width)
    mask = (iota((1, full_width), 1) < width).astype(F32)
    return is_text, width.astype(F32), mask


def fetch(source, target, semaphore):
    copy = pltpu.make_async_copy(source, target, semaphore)
    copy.start()
    return copy


def three_parts(rows):
    parts = []
    for _ in range(3):
        part = rows.astype(BF16).astype(F32)
        parts.append(part)
        rows = rows - part
    return jnp.concatenate(parts, axis=0).astype(BF16)


def over_tokens(tokens, size, step):
    for at in range(0, tokens, size):
        step(at, min(size, tokens - at))


def across(lane_sums, full_width):
    return jnp.concatenate([lane_sums] * (full_width // 128), axis=1)


def pooled_spots(ends_ref, is_text, pairs, copies):
    pair = lax.rem(iota((copies * pairs, pairs), 0), pairs)
    ends = jnp.where(pair == iota((copies * pairs, pairs), 1), ends_ref[...], 0).astype(F32)
    ends = jnp.sum(ends, axis=1, keepdims=True)
    firsts = (lax.rem(iota((copies * pairs, 1), 0), pairs) * IMG_TOK).astype(F32)
    return jnp.where(is_text, ends, firsts)


def embed_back(embedded, grad_unit):
    inv_norm = lax.rsqrt(jnp.sum(embedded * embedded, axis=-1, keepdims=True) + 1e-06)
    along = jnp.sum(embedded * grad_unit, axis=-1, keepdims=True)
    return (inv_norm * grad_unit - inv_norm * inv_norm * inv_norm * embedded * along).astype(BF16)


class Hidden:
    def __init__(self, widen_hbm, narrow_hbm, s_widen, s_narrow, sems, chunks):
        self.pairs = (
            (lambda at: widen_hbm.at[0, :, pl.ds(at, CHUNK)], lambda at: s_widen.at[:, pl.ds(at, CHUNK)]),
            (lambda at: narrow_hbm.at[0, pl.ds(at, CHUNK), :], lambda at: s_narrow.at[pl.ds(at, CHUNK), :]),
        )
        self.sems = sems
        self.chunks = chunks

    def copy(self, which, chunk):
        source, target = self.pairs[which]
        at = chunk * CHUNK
        return pltpu.make_async_copy(source(at), target(at), self.sems.at[which, chunk])

    def start(self, order):
        for chunk in range(self.chunks):
            for which in order:
                self.copy(which, chunk).start()

    def each(self, step):
        for chunk in range(self.chunks):
            self.copy(0, chunk).wait()
            self.copy(1, chunk).wait()
            step(slice(chunk * CHUNK, (chunk + 1) * CHUNK))


def attend_kernel(
    dims,
    ends_ref,
    x_hbm,
    ag,
    ab,
    triple_hbm,
    triple_bias,
    wo_hbm,
    bo,
    fg,
    fb,
    ww_hbm,
    bw,
    wn_hbm,
    bn,
    lg,
    lb,
    we_hbm,
    unit_ref,
    early_ref,
    hat_hbm,
    inv_hbm,
    probs_hbm,
    keys_ref,
    embedded_ref,
    pooled_ref,
    middle_ref,
    slope_ref,
    hat_rows_ref,
    s_x,
    s_one,
    s_hat,
    s_inv,
    s_probs,
    s_key,
    s_value,
    s_triple,
    s_wo,
    s_ww,
    s_wn,
    s_we,
    s_low,
    sems,
    hidden_sems,
):
    pairs, tokens, full_width, full_hidden = dims
    is_text, width, mask = tower_sizes(full_width, full_hidden)
    rows = full_width // HEAD * pairs
    get_x = fetch(x_hbm.at[0], s_x, sems.at[0])
    get_triple = fetch(triple_hbm.at[0], s_triple, sems.at[1])
    gain, shift = ag[...] * mask, ab[...] * mask
    ones = one_hot((iota((full_width, 128), 0)).astype(F32) < width)
    hidden = Hidden(ww_hbm, wn_hbm, s_ww, s_wn, hidden_sems, full_hidden // CHUNK)
    get_x.wait()
    get_wo = fetch(wo_hbm.at[0], s_wo, sems.at[2])
    hidden.start((0, 1))
    get_we = fetch(we_hbm.at[0], s_we, sems.at[3])

    def norm_rows(at, count):
        here = pl.ds(at, count)
        low = s_x[here, :]
        mean = mm(low, ones) / width
        centre = (low.astype(F32) - across(mean, full_width)) * mask
        square = centre * centre
        high = square.astype(BF16)
        low = (square - high.astype(F32)).astype(BF16)
        invert = lax.rsqrt((mm(high, ones) + mm(low, ones)) / width + 1e-05)
        hat = centre * across(invert, full_width)
        s_hat[here, :] = hat.astype(BF16)
        s_one[here, :] = (hat * gain + shift).astype(BF16)
        s_inv[here, :] = invert

    over_tokens(tokens, NORM_ROWS, norm_rows)
    put_hat = fetch(s_hat, hat_hbm, sems.at[4])
    put_inv = fetch(s_inv, inv_hbm, sems.at[5])
    pick = one_hot(iota((pairs, tokens), 1).astype(F32) == pooled_spots(ends_ref, is_text, pairs, 1))
    stream_rows = mm(pick, s_x[...]) * mask
    one = mm(pick, s_one[...]).astype(BF16)
    get_triple.wait()
    query = ((mm(one, s_triple[0]) + triple_bias[0, 0:1, :]) * (mask * 0.125)).astype(BF16)
    repeat = repeat_rows(rows, pairs)
    heads = head_mask(rows, pairs, full_width)
    wide = jnp.where(heads, mm(repeat, query), 0.0).astype(BF16)

    def project(at, count):
        here = pl.ds(at, count)
        s_key[here, :] = mm(s_one[here, :], s_triple[1]).astype(BF16)
        s_value[here, :] = (mm(s_one[here, :], s_triple[2]) + triple_bias[0, 1:2, :]).astype(BF16)

    over_tokens(tokens, PROJECT_ROWS, project)
    s_probs[...] = mm_nt(wide, s_key[...])
    last = pooled_spots(ends_ref, is_text, pairs, rows // pairs)
    pair = lax.rem(iota((rows, 1), 0), pairs)
    stops = jnp.where(
        pair - 1 == iota((rows, pairs), 1), ends_ref[...] + 1, 0
    ).astype(F32)
    first = jnp.where(is_text, jnp.sum(stops, axis=1, keepdims=True), last)
    last = jnp.where(is_text, last, last + (IMG_TOK - 1.0))
    step_rows = 48
    for at in range(0, rows, step_rows):
        here = slice(at, at + step_rows)
        place = iota((step_rows, tokens), 1).astype(F32)
        allowed = (place >= first[here]) & (place <= last[here])
        scores = jnp.where(allowed, s_probs[here, :], -1e30)
        powers = jnp.exp(scores - jnp.max(scores, axis=1, keepdims=True))
        probs = powers * (1.0 / jnp.sum(powers, axis=1, keepdims=True))
        s_probs[here, :] = probs
        s_low[here, :] = probs.astype(BF16)
    put_probs = fetch(s_probs, probs_hbm, sems.at[6])
    mixed_wide = mm(s_low[...], s_value[...])
    mixed = mm_tn(repeat, jnp.where(heads, mixed_wide, 0.0).astype(BF16))
    mixed = (mixed * mask).astype(BF16)
    early_ref[:, 0:full_width] = mixed
    early_ref[:, full_width : 2 * full_width] = stream_rows.astype(BF16)
    get_wo.wait()
    middle = stream_rows + mm(mixed, s_wo[...]) + bo[...]
    middle_ref[...] = middle
    mid_hat, _ = normed(middle, mask, width)
    two = ((mid_hat * fg[...] + fb[...]) * mask).astype(BF16)
    pooled_ref[...] = middle + bn[...]
    hidden_width = jnp.where(is_text, MLP_TXT, full_hidden)
    hidden_mask = (iota((1, full_hidden), 1) < hidden_width).astype(F32)

    def forward(at):
        pre = mm(two, s_ww[:, at]) + bw[:, at]
        gate = sigmoid(1.702 * pre)
        active = pre * gate * hidden_mask[:, at]
        slope_ref[:, at] = (gate + 1.702 * active * (1.0 - gate)) * hidden_mask[:, at]
        pooled_ref[...] += mm(active.astype(BF16), s_wn[at, :])

    hidden.each(forward)
    out_hat, out_inv = normed(pooled_ref[...], mask, width)
    early_ref[:, 2 * full_width : 3 * full_width] = out_hat.astype(BF16)
    lane = iota((pairs, 128), 1)
    numbers = jnp.zeros((pairs, 128), F32)
    for place in range(3):
        part = out_inv.astype(BF16).astype(F32)
        numbers = jnp.where(lane == place, part, numbers)
        out_inv = out_inv - part
    early_ref[:, 3 * full_width :] = numbers.astype(BF16)
    three = ((out_hat * lg[...] + lb[...]) * mask).astype(BF16)
    get_we.wait()
    embedded = mm(three, s_we[...])
    embedded_ref[...] = embedded
    unit_ref[...] = (
        embedded * lax.rsqrt(jnp.sum(embedded * embedded, axis=-1, keepdims=True) + 1e-06)
    ).astype(BF16)
    keys_ref[...] = mm_nt(wide, s_triple[1]).astype(BF16)
    hat_rows_ref[...] = mm(pick, s_hat[...]).astype(BF16)
    for copy in (put_hat, put_inv, put_probs):
        copy.wait()


def means_kernel(dims, ag, ab, hat_ref, probs_ref, turned_ref, spread_ref, s_turn):
    pairs, tokens, full_width, full_hidden = dims
    _, width, mask = tower_sizes(full_width, full_hidden)
    rows = probs_ref.shape[0]
    low = probs_ref[...].astype(BF16)
    spread = mm(low, hat_ref[...])
    spread_ref[...] = spread
    total = jnp.sum(low.astype(F32), axis=1, keepdims=True)
    s_turn[rows:, :] = jnp.zeros((s_turn.shape[0] - rows, full_width), F32)
    s_turn[0:rows, :] = (spread * ag[...] + total * ab[...]) * mask
    turned_ref[...] = s_turn[...].T.astype(BF16)


def in_order(pieces, stages, pairs, block, at):
    here = lax.axis_index("dp")
    row = at + iota((block, 1), 0)
    owner = lax.div(row, pairs)
    apart = lax.bitwise_xor(owner, here)
    place = jnp.zeros_like(owner)
    weight = 1
    for shift, bits in stages:
        digit = lax.bitwise_and(lax.shift_right_logical(apart, shift), (1 << bits) - 1)
        place = place + digit * weight
        weight = weight << bits
    column = place * pairs + row - owner * pairs
    total = None
    first = 0
    for piece in pieces:
        count = piece.shape[0]
        part = mm(one_hot(iota((block, count), 1) + first == column), piece[...])
        total = part if total is None else total + part
        first += count
    return total.astype(BF16)


def over_blocks(count, step):
    if count == 1:
        step(0)
    else:

        def one(index, carry):
            step(index)
            return carry

        lax.fori_loop(0, count, one, 0)


def block_rows(total):
    return 320 if total % 320 == 0 else total


def loss_kernel(
    dims,
    own_rel,
    other_rel,
    flags_ref,
    logit_scale,
    loss_scale,
    ag,
    ab,
    triple_hbm,
    triple_bias,
    wo_hbm,
    fg,
    ww_hbm,
    wn_hbm,
    lg,
    we_hbm,
    hat_hbm,
    probs_hbm,
    spread_ref,
    keys_ref,
    embedded_ref,
    pooled_ref,
    middle_ref,
    slope_ref,
    hat_rows_ref,
    turned_ref,
    loss_ref,
    hits_ref,
    scale_ref,
    grad_all_ref,
    late_ref,
    rows_ref,
    back_ref,
    values_ref,
    rows_one_ref,
    rows_mid_ref,
    s_own,
    s_other,
    s_triple,
    s_wo,
    s_ww,
    s_wn,
    s_we,
    s_hat,
    s_probs,
    s_rows,
    s_two,
    s_turn,
    sems,
    hidden_sems,
):
    pairs, tokens, full_width, full_hidden, stages = dims
    all_pairs = own_rel.shape[0]
    block = block_rows(all_pairs)
    here = lax.axis_index("dp")
    is_text, width, mask = tower_sizes(full_width, full_hidden)
    rows = full_width // HEAD * pairs
    get_we = fetch(we_hbm.at[0], s_we, sems.at[0])
    hidden = Hidden(ww_hbm, wn_hbm, s_ww, s_wn, hidden_sems, full_hidden // CHUNK)
    hidden.start((1, 0))
    get_wo = fetch(wo_hbm.at[0], s_wo, sems.at[1])
    get_triple = fetch(triple_hbm.at[0], s_triple, sems.at[2])
    get_hat = fetch(hat_hbm, s_hat, sems.at[3])
    get_probs = fetch(probs_hbm, s_probs, sems.at[4])

    def place(index):
        at = pl.multiple_of(index * block, block)
        s_own[pl.ds(at, block), :] = in_order([own_rel], stages, pairs, block, at)
        s_other[pl.ds(at, block), :] = in_order([other_rel], stages, pairs, block, at)

    over_blocks(all_pairs // block, place)
    live = (flags_ref[...] > 0).astype(F32)
    live_pairs = jnp.sum(live, axis=1, keepdims=True)
    factor = jnp.exp(logit_scale[...])
    row_weight = loss_scale[...] / (2.0 * live_pairs)
    loss_ref[...] = jnp.zeros_like(loss_ref)
    hits_ref[...] = jnp.zeros_like(hits_ref)
    scale_ref[...] = jnp.zeros_like(scale_ref)
    grad_all_ref[...] = jnp.zeros_like(grad_all_ref)

    def part(index):
        at = pl.multiple_of(index * block, block)
        eye = at + iota((block, all_pairs), 0) == iota((block, all_pairs), 1)
        live_rows = jnp.sum(jnp.where(eye, live, 0.0), axis=1, keepdims=True)

        def one_way(left, right):
            logits = mm_nt(left, right) * factor
            masked = jnp.where(live > 0.5, logits, -1e30)
            peak = jnp.max(masked, axis=1, keepdims=True)
            powers = jnp.exp(masked - peak)
            total = jnp.sum(powers, axis=1, keepdims=True)
            log_total = peak + jnp.log(total)
            matched = jnp.sum(jnp.where(eye, logits, 0.0), axis=1, keepdims=True)
            gap = jnp.where(live_rows > 0.5, log_total - matched, 0.0)
            grads = (
                (powers / total - eye.astype(F32)) * (live_rows * row_weight)
            ).astype(BF16)
            loss = jnp.sum(live_rows * gap, axis=0, keepdims=True)
            hits = jnp.sum(live_rows * jnp.exp(-gap), axis=0, keepdims=True)
            scale = jnp.sum(
                jnp.sum(grads.astype(F32) * logits, axis=1, keepdims=True),
                axis=0,
                keepdims=True,
            )
            return grads, loss, hits, scale

        own = s_own[pl.ds(at, block), :]
        other = s_other[pl.ds(at, block), :]
        grads, loss_one, hits_one, scale_one = one_way(own, s_other[...])
        grad_all_ref[pl.ds(at, block), :] += factor * mm(grads, s_other[...])
        grads, loss_two, hits_two, scale_two = one_way(other, s_own[...])
        grad_all_ref[...] += factor * mm_tn(grads, other)
        loss_ref[...] += loss_one + loss_two
        hits_ref[...] += hits_one + hits_two
        scale_ref[...] += scale_one + scale_two

    over_blocks(all_pairs // block, part)
    loss_ref[...] = loss_ref[...] / (2.0 * live_pairs)
    hits_ref[...] = hits_ref[...] / (2.0 * live_pairs)

    for pair in range(pairs):
        s_rows[pair : pair + 1, :] = grad_all_ref[pl.ds(here * pairs + pair, 1), :]

    gain, shift = ag[...] * mask, ab[...] * mask
    grad_embed = embed_back(embedded_ref[...], s_rows[...])
    get_we.wait()
    grad_three = mm_nt(grad_embed, s_we[...])
    out_hat, out_inv = normed(pooled_ref[...], mask, width)
    grad_pooled = norm_back(out_hat, out_inv, lg[...] * mask, grad_three, mask, width)
    branch = grad_pooled.astype(BF16)
    s_two[...] = jnp.zeros_like(s_two)

    def backward(at):
        grad_active = mm_nt(branch, s_wn[at, :])
        grad_hidden = (grad_active * slope_ref[:, at]).astype(BF16)
        s_two[...] += mm_nt(grad_hidden, s_ww[:, at])

    hidden.each(backward)
    mid_hat, mid_inv = normed(middle_ref[...], mask, width)
    grad_two = s_two[...] * mask
    grad_middle = grad_pooled + norm_back(mid_hat, mid_inv, fg[...] * mask, grad_two, mask, width)
    rows_mid_ref[...] = grad_middle
    attention = grad_middle.astype(BF16)
    rows_ref[:, full_width:] = attention
    get_wo.wait()
    grad_mixed = (mm_nt(attention, s_wo[...]) * mask).astype(BF16)
    repeat = repeat_rows(rows, pairs)
    heads = head_mask(rows, pairs, full_width)
    wide = jnp.where(heads, mm(repeat, grad_mixed), 0.0)
    get_triple.wait()
    along = mm_nt(wide.astype(BF16), s_triple[2])
    values_low = along.astype(BF16)
    values_ref[...] = values_low
    offset = jnp.sum(along * shift, axis=1, keepdims=True) + jnp.sum(
        wide * triple_bias[0, 1:2, :], axis=1, keepdims=True
    )
    get_hat.wait()
    get_probs.wait()
    grad_probs = mm_nt((along * gain).astype(BF16), s_hat[...]) + offset
    probs = s_probs[...]
    inner = jnp.sum(grad_probs * probs, axis=1, keepdims=True)
    back = (probs * (grad_probs - inner)).astype(BF16)
    back_ref[...] = back
    spread = mm(back, s_hat[...])
    total = jnp.sum(back.astype(F32), axis=1, keepdims=True)
    means = (spread * gain + total * shift).astype(BF16)
    query_wide = mm(means, s_triple[1]) * 0.125
    grad_query = mm_tn(repeat, jnp.where(heads, query_wide, 0.0).astype(BF16)).astype(BF16)
    rows_ref[:, 0:full_width] = grad_query
    rows_one = mm_nt(grad_query, s_triple[0]) * mask
    rows_one_ref[...] = rows_one
    values_wide = values_low.astype(F32)
    keys_wide = keys_ref[...].astype(F32)
    prob_total = jnp.sum(probs.astype(BF16).astype(F32), axis=1, keepdims=True)
    gain_sum = (
        sums_of(values_wide * spread_ref[...])
        + sums_of(keys_wide * spread)
        + sums_of(rows_one * hat_rows_ref[...].astype(F32))
    )
    shift_sum = (
        sums_of(values_wide * prob_total) + sums_of(keys_wide * total) + sums_of(rows_one)
    ) * mask
    s_turn[rows:, :] = jnp.zeros((s_turn.shape[0] - rows, full_width), F32)
    s_turn[0:rows, :] = means.astype(F32)
    slot = rows
    for vector in (gain_sum, shift_sum, sums_of(grad_two * mid_hat), sums_of(grad_two)):
        for _ in range(3):
            low = vector.astype(BF16).astype(F32)
            s_turn[slot : slot + 1, :] = low
            vector = vector - low
            slot += 1
    late_ref[:, 0 : s_turn.shape[0]] = s_turn[...].T.astype(BF16)
    late_ref[:, s_turn.shape[0] :] = turned_ref[...]


def stream_kernel(
    dims,
    ends_ref,
    ag,
    hat_hbm,
    inv_hbm,
    probs_hbm,
    back_ref,
    values_ref,
    keys_ref,
    rows_one_ref,
    rows_mid_ref,
    out_hbm,
    s_hat,
    s_inv,
    s_probs,
    s_left,
    s_right,
    s_out,
    sems,
    out_sems,
):
    pairs, tokens, full_width, full_hidden = dims
    is_text, width, mask = tower_sizes(full_width, full_hidden)
    rows = full_width // HEAD * pairs
    get_probs = fetch(probs_hbm, s_probs, sems.at[0])
    get_hat = fetch(hat_hbm, s_hat, sems.at[1])
    get_inv = fetch(inv_hbm, s_inv, sems.at[2])
    gain = ag[...] * mask
    s_left[rows : 2 * rows, :] = back_ref[...]
    s_right[0:rows, :] = values_ref[...]
    s_right[rows : 2 * rows, :] = keys_ref[...]
    spots = pooled_spots(ends_ref, is_text, pairs, 3)
    s_left[2 * rows :, :] = one_hot(iota((3 * pairs, tokens), 1).astype(F32) == spots)
    s_right[2 * rows :, :] = three_parts(rows_one_ref[...])
    middle_parts = three_parts(rows_mid_ref[...])
    ones = one_hot(iota((full_width, 128), 0).astype(F32) < width)
    get_probs.wait()
    s_left[0:rows, :] = s_probs[...].astype(BF16)
    get_hat.wait()
    get_inv.wait()

    def put(at, count):
        spot = pl.ds(at, count)
        return pltpu.make_async_copy(
            s_out.at[spot, :], out_hbm.at[0, spot, :], out_sems.at[at // NORM_ROWS]
        )

    def norm_rows(at, count):
        spot = pl.ds(at, count)
        upward = mm_tn(s_left[:, spot], s_right[...])
        hat = s_hat[spot, :].astype(F32)
        scaled = upward * gain
        mean = mm(scaled.astype(BF16), ones) / width
        along = mm((scaled * hat).astype(BF16), ones) / width
        s_out[spot, :] = across(s_inv[spot, :], full_width) * (
            scaled - across(mean, full_width) * mask - hat * across(along, full_width)
        ) + mm_tn(s_left[2 * rows :, spot], middle_parts)
        put(at, count).start()

    over_tokens(tokens, NORM_ROWS, norm_rows)
    over_tokens(tokens, NORM_ROWS, lambda at, count: put(at, count).wait())


def window_of(slice_hidden, full_hidden):
    here = lax.axis_index("dp")
    first = jnp.minimum(lax.div(here * slice_hidden, 128) * 128, full_hidden - WINDOW)
    return pl.multiple_of(first, 128)


def rows_kernel(dims, *refs):
    pairs, full_width, full_hidden, slice_width, slice_hidden, stages, pieces = dims
    early = refs[:pieces]
    (
        grad_ref,
        ag,
        ab,
        triple_hbm,
        triple_bias,
        wo_hbm,
        bo,
        fg,
        fb,
        ww_hbm,
        bw_hbm,
        wn_hbm,
        lg,
        lb,
        we_hbm,
        ones_ref,
        queries_ref,
        mixed_ref,
        embed_ref,
        narrow_ref,
        widen_ref,
        final_gain_ref,
        final_bias_ref,
        narrow_bias_ref,
        widen_bias_ref,
        s_triple,
        s_wo,
        s_ww,
        s_wn,
        s_we,
        s_bw,
        s_vectors,
        sems,
    ) = refs[pieces:]
    all_pairs = grad_ref.shape[0]
    block = block_rows(all_pairs)
    here = lax.axis_index("dp")
    is_text, width, mask = tower_sizes(full_width, full_hidden)
    first = window_of(slice_hidden, full_hidden)
    window = pl.ds(first, WINDOW)
    copies = [
        fetch(triple_hbm.at[0, 0], s_triple, sems.at[0]),
        fetch(wo_hbm.at[0], s_wo, sems.at[1]),
        fetch(we_hbm.at[0], s_we, sems.at[2]),
        fetch(ww_hbm.at[0, :, window], s_ww, sems.at[3]),
        fetch(wn_hbm.at[0, window, :], s_wn, sems.at[4]),
        fetch(bw_hbm.at[:, window], s_bw, sems.at[5]),
    ]
    for ref in (embed_ref, narrow_ref, widen_ref, widen_bias_ref, s_vectors):
        ref[...] = jnp.zeros_like(ref)
    lane = iota((full_width, slice_width), 0)
    pick = one_hot(
        (lane == here * slice_width + iota((full_width, slice_width), 1))
        & (lane.astype(F32) < width)
    )
    unit = first + iota((WINDOW, slice_hidden), 0)
    hidden = jnp.where(is_text, MLP_TXT, full_hidden)
    chosen = one_hot(
        (unit == here * slice_hidden + iota((WINDOW, slice_hidden), 1)) & (unit < hidden)
    )
    gain, shift = lg[...] * mask, lb[...] * mask
    for copy in copies:
        copy.wait()

    def part(index):
        at = pl.multiple_of(index * block, block)
        here_rows = pl.ds(at, block)
        arrived = in_order(early, stages, pairs, block, at)
        mixed = arrived[:, 0:full_width]
        stream_rows = arrived[:, full_width : 2 * full_width].astype(F32)
        out_hat = arrived[:, 2 * full_width : 3 * full_width].astype(F32)
        out_inv = jnp.sum(arrived[:, 3 * full_width :].astype(F32), axis=1, keepdims=True)
        rows_hat, _ = normed(stream_rows, mask, width)
        one = ((rows_hat * ag[...] + ab[...]) * mask).astype(BF16)
        ones_ref[here_rows, :] = mm(one, pick).astype(BF16)
        query = (mm(one, s_triple[...]) + triple_bias[0, 0:1, :]) * mask
        queries_ref[here_rows, :] = query.astype(BF16)
        mixed_ref[here_rows, :] = mm(mixed, pick).astype(BF16)
        middle = stream_rows + mm(mixed, s_wo[...]) + bo[...]
        mid_hat, _ = normed(middle, mask, width)
        two = ((mid_hat * fg[...] + fb[...]) * mask).astype(BF16)
        pre = mm(two, s_ww[...]) + s_bw[...]
        gate = sigmoid(1.702 * pre)
        active = pre * gate
        slope = gate + 1.702 * active * (1.0 - gate)
        three = (out_hat * gain + shift).astype(BF16)
        grad_embed = embed_back(mm(three, s_we[...]), grad_ref[here_rows, :])
        embed_ref[0] += mm_tn(mm(three, pick).astype(BF16), grad_embed)
        grad_three = mm_nt(grad_embed, s_we[...])
        s_vectors[0:1, :] += sums_of(grad_three * out_hat)
        s_vectors[1:2, :] += sums_of(grad_three)
        branch = norm_back(out_hat, out_inv, gain, grad_three, mask, width).astype(BF16)
        s_vectors[2:3, :] += sums_of(branch.astype(F32))
        narrow_ref[0] += mm_tn(mm(active.astype(BF16), chosen).astype(BF16), branch)
        grad_hidden = (mm_nt(branch, s_wn[...]) * slope).astype(BF16)
        hidden_slice = mm(grad_hidden, chosen)
        widen_ref[0] += mm_tn(hidden_slice.astype(BF16), two)
        widen_bias_ref[...] += sums_of(hidden_slice)

    over_blocks(all_pairs // block, part)
    vectors = dot_dims(s_vectors[...], pick.astype(F32), 1, 0, lax.Precision.HIGHEST)
    for slot, ref in enumerate((final_gain_ref, final_bias_ref, narrow_bias_ref)):
        ref[...] = vectors[slot : slot + 1, :]


def last_kernel(dims, *refs):
    pairs, full_width, full_hidden, slice_width, stages, pieces = dims
    arrived = refs[:pieces]
    (
        late_ref,
        ones_ref,
        queries_ref,
        mixed_ref,
        wo_hbm,
        triple_ref,
        mixer_ref,
        gain_ref,
        shift_ref,
        feed_gain_ref,
        feed_bias_ref,
        mixer_bias_ref,
        bias_ref,
        s_keys,
        s_means,
        s_late,
        s_values,
        s_sums,
        s_wo,
        sems,
    ) = refs[pieces:]
    here = lax.axis_index("dp")
    is_text, width, mask = tower_sizes(full_width, full_hidden)
    get_wo = fetch(wo_hbm.at[0], s_wo, sems.at[0])
    count = late_ref.shape[0]
    lanes = late_ref.shape[2] // 2
    heads = full_width // HEAD
    rows = heads * pairs
    all_pairs = queries_ref.shape[0]
    block = block_rows(all_pairs)
    triple_ref[0, 0] = jnp.zeros((slice_width, full_width), F32)
    mixer_ref[...] = jnp.zeros_like(mixer_ref)
    s_late[...] = jnp.zeros_like(s_late)
    s_sums[...] = jnp.zeros_like(s_sums)
    get_wo.wait()

    def part(index):
        at = pl.multiple_of(index * block, block)
        here_rows = pl.ds(at, block)
        now = in_order(arrived, stages, pairs, block, at)
        grad_query = now[:, 0:full_width]
        attention = now[:, full_width:]
        triple_ref[0, 0] += mm_tn(ones_ref[here_rows, :], grad_query)
        mixer_ref[0] += mm_tn(mixed_ref[here_rows, :], attention)
        grad_mixed = (mm_nt(attention, s_wo[...]) * mask).astype(BF16)
        s_values[here_rows, :] = grad_mixed
        for slot, vector in enumerate((grad_query, grad_mixed, attention)):
            s_sums[slot : slot + 1, :] += sums_of(vector.astype(F32))

    over_blocks(all_pairs // block, part)
    if slice_width % 16 == 0 and count <= 16:
        for source in range(count):
            now = late_ref[source]
            s_late[...] += now[:, 0:lanes].astype(F32)
            across_now = slice(source * pairs, (source + 1) * pairs)
            for head in range(heads):
                down = slice(head * slice_width, (head + 1) * slice_width)
                lane = head * pairs
                s_keys[down, across_now] = now[:, lane : lane + pairs]
                s_means[down, across_now] = now[:, lanes + lane : lanes + lane + pairs]
        left = iota((slice_width, 2 * HEAD), 1) < HEAD
        for two in range(heads // 2):
            down = slice(two * 2 * slice_width, (two + 1) * 2 * slice_width)
            lane = slice(two * 2 * HEAD, (two + 1) * 2 * HEAD)
            both = mm(s_keys[down, :], queries_ref[:, lane]) * 0.125
            triple_ref[0, 1, :, lane] = jnp.where(left, both[0:slice_width], both[slice_width:])
            both = mm(s_means[down, :], s_values[:, lane])
            triple_ref[0, 2, :, lane] = jnp.where(left, both[0:slice_width], both[slice_width:])
    else:
        triple_ref[0, 1] = jnp.zeros((slice_width, full_width), F32)
        triple_ref[0, 2] = jnp.zeros((slice_width, full_width), F32)
        head = head_mask(lanes, pairs, full_width)

        def one(source, carry):
            now = late_ref[source]
            s_late[...] += now[:, 0:lanes].astype(F32)
            row = iota((lanes, all_pairs), 0)
            column = iota((lanes, all_pairs), 1)
            repeat = one_hot((column == source * pairs + lax.rem(row, pairs)) & (row < rows))
            for which, origin in ((1, queries_ref), (2, s_values)):
                wide = jnp.where(head, mm(repeat, origin[...]), 0.0).astype(BF16)
                first = (which - 1) * lanes
                triple_ref[0, which] += mm(now[:, first : first + lanes], wide)
            return carry

        lax.fori_loop(0, count, one, 0)
        triple_ref[0, 1] = triple_ref[0, 1] * 0.125
    lane = iota((8, lanes), 1)
    row = iota((8, lanes), 0)
    slot = rows + row * 3
    chosen = ((lane >= slot) & (lane < slot + 3) & (row < 4)).astype(F32)
    from_late = dot_dims(chosen, s_late[...], 1, 1, lax.Precision.HIGHEST)
    for slot, ref in enumerate((gain_ref, shift_ref, feed_gain_ref, feed_bias_ref)):
        ref[...] = from_late[slot : slot + 1, :]
    pick = (
        iota((full_width, slice_width), 0)
        == here * slice_width + iota((full_width, slice_width), 1)
    ).astype(F32)
    sums = dot_dims(s_sums[...], pick, 1, 0, lax.Precision.HIGHEST)
    bias_ref[0] = sums[0:2, :]
    mixer_bias_ref[...] = sums[2:3, :]


def stages_of(count):
    bits = count.bit_length() - 1
    stages = []
    while bits > 0:
        take = 2 if bits >= 2 else 1
        bits -= take
        stages.append((bits, take))
    return tuple(stages)


def exchange(block, axis, stage):
    count = lax.axis_size(axis)
    shift, bits = stage
    parts = [block]
    for apart in range(1, 1 << bits):
        route = [(low, low ^ (apart << shift)) for low in range(count)]
        parts.append(lax.ppermute(block, axis, route))
    return parts


def call(kernel, ins, outs, scratch, in_hbm=(), out_hbm=(), cost=None):
    vmem = pl.BlockSpec(memory_space=pltpu.VMEM)
    anywhere = pl.BlockSpec(memory_space=pl.ANY)
    specs = [anywhere if index in in_hbm else vmem for index in range(len(ins))]
    out_specs = [anywhere if index in out_hbm else vmem for index in range(len(outs))]
    flops, moved = cost
    return pl.pallas_call(
        kernel,
        out_shape=[jax.ShapeDtypeStruct(shape, kind) for shape, kind in outs],
        in_specs=specs,
        out_specs=out_specs,
        scratch_shapes=scratch,
        compiler_params=pltpu.CompilerParams(vmem_limit_bytes=VMEM_LIMIT),
        cost_estimate=pl.CostEstimate(flops=flops, bytes_accessed=moved, transcendentals=0),
    )(*ins)


def body(
    block_input,
    segments,
    caption_ends,
    pair_flags,
    attention_gain,
    attention_bias,
    triple_weight,
    triple_bias,
    mixer_weight,
    mixer_bias,
    feed_gain,
    feed_bias,
    widen_weight,
    widen_bias,
    narrow_weight,
    narrow_bias,
    final_gain,
    final_bias,
    embed_weight,
    logit_scale,
    loss_scale,
):
    tokens, width = block_input.shape[1:]
    hidden = widen_weight.shape[2]
    emb = embed_weight.shape[2]
    pairs = caption_ends.shape[0]
    count = lax.axis_size("dp")
    all_pairs = pair_flags.shape[0]
    heads = width // HEAD
    rows = heads * pairs
    lanes = -(-(rows + 12) // 128) * 128
    slice_width = width // count
    slice_hidden = hidden // count
    stages = stages_of(count)
    ends = caption_ends.reshape(1, pairs)
    dma = pltpu.SemaphoreType.DMA
    weights_scratch = [
        pltpu.VMEM((3, width, width), BF16),
        pltpu.VMEM((width, width), BF16),
        pltpu.VMEM((width, hidden), BF16),
        pltpu.VMEM((hidden, width), BF16),
        pltpu.VMEM((width, emb), BF16),
    ]
    dims = (pairs, tokens, width, hidden)
    chunk_count = hidden // CHUNK
    (
        unit,
        early,
        hat,
        invert,
        probs,
        keys,
        embedded,
        pooled,
        middle,
        slope,
        hat_rows,
    ) = call(
        partial(attend_kernel, dims),
        (
            ends,
            block_input,
            attention_gain,
            attention_bias,
            triple_weight,
            triple_bias,
            mixer_weight,
            mixer_bias,
            feed_gain,
            feed_bias,
            widen_weight,
            widen_bias,
            narrow_weight,
            narrow_bias,
            final_gain,
            final_bias,
            embed_weight,
        ),
        [
            ((pairs, emb), BF16),
            ((pairs, 3 * width + 128), BF16),
            ((tokens, width), BF16),
            ((tokens, 128), F32),
            ((rows, tokens), F32),
            ((rows, width), BF16),
            ((pairs, emb), F32),
            ((pairs, width), F32),
            ((pairs, width), F32),
            ((pairs, hidden), F32),
            ((pairs, width), BF16),
        ],
        [
            pltpu.VMEM((tokens, width), BF16),
            pltpu.VMEM((tokens, width), BF16),
            pltpu.VMEM((tokens, width), BF16),
            pltpu.VMEM((tokens, 128), F32),
            pltpu.VMEM((rows, tokens), F32),
            pltpu.VMEM((tokens, width), BF16),
            pltpu.VMEM((tokens, width), BF16),
        ]
        + weights_scratch
        + [
            pltpu.VMEM((rows, tokens), BF16),
            dma((7,)),
            dma((2, chunk_count)),
        ],
        in_hbm=(1, 4, 6, 10, 12, 16),
        out_hbm=(2, 3, 4),
        cost=(10**9, 20 * 10**6),
    )
    turned, spread = call(
        partial(means_kernel, dims),
        (attention_gain, attention_bias, hat, probs),
        [((width, lanes), BF16), ((rows, width), F32)],
        [pltpu.VMEM((lanes, width), F32)],
        cost=(10**9, 5 * 10**6),
    )
    early_pieces = [early]
    own_rel = unit
    for index, stage in enumerate(stages):
        own_parts = exchange(own_rel, "dp", stage)
        if index + 1 < len(stages):
            early_parts = exchange(jnp.concatenate(early_pieces, axis=0), "dp", stage)
            own_parts, early_pieces, turned, spread = lax.optimization_barrier(
                (own_parts, early_parts, turned, spread)
            )
        own_rel = jnp.concatenate(own_parts, axis=0)
    other_rel = lax.ppermute(own_rel, "tower", [(0, 1), (1, 0)])
    early_pieces = exchange(jnp.concatenate(early_pieces, axis=0), "dp", stages[-1])
    (
        loss,
        hits,
        scale,
        grad_all,
        late,
        late_rows,
        back,
        values,
        rows_one,
        rows_mid,
    ) = call(
        partial(loss_kernel, dims + (stages,)),
        (
            own_rel,
            other_rel,
            pair_flags.reshape(1, all_pairs),
            logit_scale.reshape(1, 1),
            loss_scale.reshape(1, 1),
            attention_gain,
            attention_bias,
            triple_weight,
            triple_bias,
            mixer_weight,
            feed_gain,
            widen_weight,
            narrow_weight,
            final_gain,
            embed_weight,
            hat,
            probs,
            spread,
            keys,
            embedded,
            pooled,
            middle,
            slope,
            hat_rows,
            turned,
        ),
        [
            ((1, 1), F32),
            ((1, 1), F32),
            ((1, 1), F32),
            ((all_pairs, emb), F32),
            ((width, 2 * lanes), BF16),
            ((pairs, 2 * width), BF16),
            ((rows, tokens), BF16),
            ((rows, width), BF16),
            ((pairs, width), F32),
            ((pairs, width), F32),
        ],
        [pltpu.VMEM((all_pairs, emb), BF16), pltpu.VMEM((all_pairs, emb), BF16)]
        + weights_scratch
        + [
            pltpu.VMEM((tokens, width), BF16),
            pltpu.VMEM((rows, tokens), F32),
            pltpu.VMEM((pairs, emb), F32),
            pltpu.VMEM((pairs, width), F32),
            pltpu.VMEM((lanes, width), F32),
            dma((5,)),
            dma((2, chunk_count)),
        ],
        in_hbm=(7, 9, 11, 12, 14, 15, 16),
        cost=(10**9, 20 * 10**6),
    )
    early_pieces, late, late_rows = lax.optimization_barrier((early_pieces, late, late_rows))
    late_all = lax.all_to_all(late, "dp", 0, 0, tiled=True).reshape(
        count, slice_width, 2 * lanes
    )
    late_pieces = [late_rows]
    for stage in stages:
        late_pieces = exchange(jnp.concatenate(late_pieces, axis=0), "dp", stage)
    (block_grad,) = call(
        partial(stream_kernel, dims),
        (ends, attention_gain, hat, invert, probs, back, values, keys, rows_one, rows_mid),
        [((1, tokens, width), F32)],
        [
            pltpu.VMEM((tokens, width), BF16),
            pltpu.VMEM((tokens, 128), F32),
            pltpu.VMEM((rows, tokens), F32),
            pltpu.VMEM((2 * rows + 3 * pairs, tokens), BF16),
            pltpu.VMEM((2 * rows + 3 * pairs, width), BF16),
            pltpu.VMEM((tokens, width), F32),
            dma((3,)),
            dma((-(-tokens // NORM_ROWS),)),
        ],
        in_hbm=(2, 3, 4),
        out_hbm=(0,),
        cost=(2 * 10**9, 10 * 10**6),
    )
    ahead = len(early_pieces)
    vector = ((1, slice_width), F32)
    (
        ones,
        query_rows,
        mixed_slice,
        grad_embed,
        grad_narrow,
        grad_widen,
        grad_final_gain,
        grad_final_bias,
        grad_narrow_bias,
        grad_widen_bias,
    ) = call(
        partial(rows_kernel, (pairs, width, hidden, slice_width, slice_hidden, stages, ahead)),
        tuple(early_pieces)
        + (
            grad_all,
            attention_gain,
            attention_bias,
            triple_weight,
            triple_bias,
            mixer_weight,
            mixer_bias,
            feed_gain,
            feed_bias,
            widen_weight,
            widen_bias,
            narrow_weight,
            final_gain,
            final_bias,
            embed_weight,
        ),
        [
            ((all_pairs, slice_width), BF16),
            ((all_pairs, width), BF16),
            ((all_pairs, slice_width), BF16),
            ((1, slice_width, emb), F32),
            ((1, slice_hidden, width), F32),
            ((1, slice_hidden, width), F32),
            vector,
            vector,
            vector,
            ((1, slice_hidden), F32),
        ],
        [
            pltpu.VMEM((width, width), BF16),
            pltpu.VMEM((width, width), BF16),
            pltpu.VMEM((width, WINDOW), BF16),
            pltpu.VMEM((WINDOW, width), BF16),
            pltpu.VMEM((width, emb), BF16),
            pltpu.VMEM((1, WINDOW), F32),
            pltpu.VMEM((8, width), F32),
            dma((6,)),
        ],
        in_hbm=tuple(ahead + index for index in (3, 5, 9, 10, 11, 14)),
        cost=(3 * 10**9, 10 * 10**6),
    )
    (
        grad_triple,
        grad_mixer,
        grad_gain,
        grad_bias,
        grad_feed_gain,
        grad_feed_bias,
        grad_mixer_bias,
        grad_triple_bias,
    ) = call(
        partial(last_kernel, (pairs, width, hidden, slice_width, stages, len(late_pieces))),
        tuple(late_pieces) + (late_all, ones, query_rows, mixed_slice, mixer_weight),
        [
            ((1, 3, slice_width, width), F32),
            ((1, slice_width, width), F32),
            vector,
            vector,
            vector,
            vector,
            vector,
            ((1, 2, slice_width), F32),
        ],
        [
            pltpu.VMEM((width // HEAD * slice_width, all_pairs), BF16),
            pltpu.VMEM((width // HEAD * slice_width, all_pairs), BF16),
            pltpu.VMEM((slice_width, lanes), F32),
            pltpu.VMEM((all_pairs, width), BF16),
            pltpu.VMEM((8, width), F32),
            pltpu.VMEM((width, width), BF16),
            dma((1,)),
        ],
        in_hbm=(len(late_pieces) + 4,),
        cost=(10**9, 10 * 10**6),
    )
    return (
        loss[0, 0],
        hits[0, 0],
        block_grad,
        grad_gain,
        grad_bias,
        grad_triple,
        grad_triple_bias,
        grad_mixer,
        grad_mixer_bias,
        grad_feed_gain,
        grad_feed_bias,
        jnp.swapaxes(grad_widen, 1, 2),
        grad_widen_bias,
        grad_narrow,
        grad_narrow_bias,
        grad_final_gain,
        grad_final_bias,
        grad_embed,
        scale[0, 0],
    )


def solution(mesh):
    in_specs = (
        P("tower", "dp", None),
        P("dp", None),
        P("dp"),
        P(),
        P("tower", None),
        P("tower", None),
        P("tower", None, None, None),
        P("tower", None, None),
        P("tower", None, None),
        P("tower", None),
        P("tower", None),
        P("tower", None),
        P("tower", None, None),
        P("tower", None),
        P("tower", None, None),
        P("tower", None),
        P("tower", None),
        P("tower", None),
        P("tower", None, None),
        P(),
        P(),
    )
    out_specs = (
        P(),
        P(),
        P("tower", "dp", None),
        P("tower", "dp"),
        P("tower", "dp"),
        P("tower", None, "dp", None),
        P("tower", None, "dp"),
        P("tower", "dp", None),
        P("tower", "dp"),
        P("tower", "dp"),
        P("tower", "dp"),
        P("tower", None, "dp"),
        P("tower", "dp"),
        P("tower", "dp", None),
        P("tower", "dp"),
        P("tower", "dp"),
        P("tower", "dp"),
        P("tower", "dp", None),
        P(),
    )
    return jax.shard_map(body, mesh=mesh, in_specs=in_specs, out_specs=out_specs, check_vma=False)
```

```python
from functools import partial

import jax
import jax.numpy as jnp
from jax import lax
from jax.experimental import pallas as pl
from jax.experimental.pallas import tpu as pltpu
from jax.sharding import PartitionSpec as P

D_TXT = 512
MLP_TXT = 2048
HEAD = 64
IMG_TOK = 50
CTX = 77
F32 = jnp.float32
BF16 = jnp.bfloat16
VMEM_LIMIT = 62 * 1024 * 1024
CHUNK = 1024
NORM_ROWS = 272
PROJECT_ROWS = 1088


def dot_dims(left, right, left_dim, right_dim, precision=None):
    return lax.dot_general(
        left,
        right,
        (((left_dim,), (right_dim,)), ((), ())),
        preferred_element_type=F32,
        precision=precision,
    )


def mm(left, right):
    return dot_dims(left, right, 1, 0)


def mm_nt(left, right):
    return dot_dims(left, right, 1, 1)


def mm_tn(left, right):
    return dot_dims(left, right, 0, 0)


def iota(shape, dim):
    return lax.broadcasted_iota(jnp.int32, shape, dim)


def sigmoid(rows):
    return 1.0 / (1.0 + jnp.exp(-rows))


def one_hot(condition):
    return condition.astype(F32).astype(BF16)


def normed(rows, mask, width):
    mean = jnp.sum(rows * mask, axis=-1, keepdims=True) / width
    centre = (rows - mean) * mask
    invert = lax.rsqrt(jnp.sum(centre * centre, axis=-1, keepdims=True) / width + 1e-05)
    return centre * invert, invert


def norm_back(rows_hat, invert, gain, upward, mask, width):
    scaled = upward * gain
    mean = jnp.sum(scaled, axis=-1, keepdims=True) / width
    along = jnp.sum(scaled * rows_hat, axis=-1, keepdims=True) / width
    return invert * (scaled - mean * mask - rows_hat * along)


def sums_of(rows):
    return jnp.sum(rows, axis=0, keepdims=True)


def head_mask(rows, pairs, width):
    row = iota((rows, width), 0)
    first = lax.shift_right_logical(iota((rows, width), 1), 6) * pairs
    return (row >= first) & (row < first + pairs)


def repeat_rows(rows, pairs):
    row = iota((rows, pairs), 0)
    return one_hot(lax.rem(row, pairs) == iota((rows, pairs), 1))


def tower_sizes(full_width, full_hidden):
    is_text = lax.axis_index("tower") != 0
    width = jnp.where(is_text, D_TXT, full_width)
    mask = (iota((1, full_width), 1) < width).astype(F32)
    return is_text, width.astype(F32), mask


def fetch(source, target, semaphore):
    copy = pltpu.make_async_copy(source, target, semaphore)
    copy.start()
    return copy


def three_parts(rows):
    parts = []
    for _ in range(3):
        part = rows.astype(BF16).astype(F32)
        parts.append(part)
        rows = rows - part
    return jnp.concatenate(parts, axis=0).astype(BF16)


def over_tokens(tokens, size, step):
    for at in range(0, tokens, size):
        step(at, min(size, tokens - at))


def across(lane_sums, full_width):
    return jnp.concatenate([lane_sums] * (full_width // 128), axis=1)


def pooled_spots(ends_ref, is_text, pairs, copies):
    pair = lax.rem(iota((copies * pairs, pairs), 0), pairs)
    ends = jnp.where(pair == iota((copies * pairs, pairs), 1), ends_ref[...], 0).astype(F32)
    ends = jnp.sum(ends, axis=1, keepdims=True)
    firsts = (lax.rem(iota((copies * pairs, 1), 0), pairs) * IMG_TOK).astype(F32)
    return jnp.where(is_text, ends, firsts)


def embed_back(embedded, grad_unit):
    inv_norm = lax.rsqrt(jnp.sum(embedded * embedded, axis=-1, keepdims=True) + 1e-06)
    along = jnp.sum(embedded * grad_unit, axis=-1, keepdims=True)
    return (inv_norm * grad_unit - inv_norm * inv_norm * inv_norm * embedded * along).astype(BF16)


class Hidden:
    def __init__(self, widen_hbm, narrow_hbm, s_widen, s_narrow, sems, chunks):
        self.pairs = (
            (lambda at: widen_hbm.at[0, :, pl.ds(at, CHUNK)], lambda at: s_widen.at[:, pl.ds(at, CHUNK)]),
            (lambda at: narrow_hbm.at[0, pl.ds(at, CHUNK), :], lambda at: s_narrow.at[pl.ds(at, CHUNK), :]),
        )
        self.sems = sems
        self.chunks = chunks

    def copy(self, which, chunk):
        source, target = self.pairs[which]
        at = chunk * CHUNK
        return pltpu.make_async_copy(source(at), target(at), self.sems.at[which, chunk])

    def start(self, order):
        for chunk in range(self.chunks):
            for which in order:
                self.copy(which, chunk).start()

    def wait(self, chunk):
        self.copy(0, chunk).wait()
        self.copy(1, chunk).wait()

    def each(self, step):
        for chunk in range(self.chunks):
            self.wait(chunk)
            step(slice(chunk * CHUNK, (chunk + 1) * CHUNK))


def attend_kernel(
    dims,
    ends_ref,
    x_hbm,
    ag,
    ab,
    triple_hbm,
    triple_bias,
    wo_hbm,
    bo,
    fg,
    fb,
    ww_hbm,
    bw,
    wn_hbm,
    bn,
    lg,
    lb,
    we_hbm,
    unit_ref,
    early_ref,
    hat_hbm,
    inv_hbm,
    probs_hbm,
    query_ref,
    embedded_ref,
    pooled_ref,
    middle_ref,
    slope_ref,
    s_x,
    s_one,
    s_hat,
    s_inv,
    s_probs,
    s_key,
    s_value,
    s_triple,
    s_wo,
    s_ww,
    s_wn,
    s_we,
    s_low,
    sems,
    hidden_sems,
):
    pairs, tokens, full_width, full_hidden = dims
    is_text, width, mask = tower_sizes(full_width, full_hidden)
    rows = full_width // HEAD * pairs
    get_x = fetch(x_hbm.at[0], s_x, sems.at[0])
    get_triple = fetch(triple_hbm.at[0], s_triple, sems.at[1])
    gain, shift = ag[...] * mask, ab[...] * mask
    ones = one_hot((iota((full_width, 128), 0)).astype(F32) < width)
    hidden = Hidden(ww_hbm, wn_hbm, s_ww, s_wn, hidden_sems, full_hidden // CHUNK)
    get_x.wait()
    get_wo = fetch(wo_hbm.at[0], s_wo, sems.at[2])
    hidden.start((0, 1))
    get_we = fetch(we_hbm.at[0], s_we, sems.at[3])

    def norm_rows(at, count):
        here = pl.ds(at, count)
        low = s_x[here, :]
        mean = mm(low, ones) / width
        centre = (low.astype(F32) - across(mean, full_width)) * mask
        square = centre * centre
        high = square.astype(BF16)
        low = (square - high.astype(F32)).astype(BF16)
        invert = lax.rsqrt((mm(high, ones) + mm(low, ones)) / width + 1e-05)
        hat = centre * across(invert, full_width)
        s_hat[here, :] = hat.astype(BF16)
        s_one[here, :] = (hat * gain + shift).astype(BF16)
        s_inv[here, :] = invert

    over_tokens(tokens, NORM_ROWS, norm_rows)
    put_hat = fetch(s_hat, hat_hbm, sems.at[4])
    put_inv = fetch(s_inv, inv_hbm, sems.at[5])
    pick = one_hot(iota((pairs, tokens), 1).astype(F32) == pooled_spots(ends_ref, is_text, pairs, 1))
    stream_rows = mm(pick, s_x[...]) * mask
    one = mm(pick, s_one[...]).astype(BF16)
    get_triple.wait()
    query = ((mm(one, s_triple[0]) + triple_bias[0, 0:1, :]) * (mask * 0.125)).astype(BF16)
    repeat = repeat_rows(rows, pairs)
    heads = head_mask(rows, pairs, full_width)
    wide = jnp.where(heads, mm(repeat, query), 0.0).astype(BF16)

    def project(at, count):
        here = pl.ds(at, count)
        s_key[here, :] = mm(s_one[here, :], s_triple[1]).astype(BF16)
        s_value[here, :] = (mm(s_one[here, :], s_triple[2]) + triple_bias[0, 1:2, :]).astype(BF16)

    over_tokens(tokens, PROJECT_ROWS, project)
    s_probs[...] = mm_nt(wide, s_key[...])
    last = pooled_spots(ends_ref, is_text, pairs, rows // pairs)
    pair = lax.rem(iota((rows, 1), 0), pairs)
    stops = jnp.where(
        pair - 1 == iota((rows, pairs), 1), ends_ref[...] + 1, 0
    ).astype(F32)
    first = jnp.where(is_text, jnp.sum(stops, axis=1, keepdims=True), last)
    last = jnp.where(is_text, last, last + (IMG_TOK - 1.0))
    step_rows = 48
    for at in range(0, rows, step_rows):
        here = slice(at, at + step_rows)
        place = iota((step_rows, tokens), 1).astype(F32)
        allowed = (place >= first[here]) & (place <= last[here])
        scores = jnp.where(allowed, s_probs[here, :], -1e30)
        powers = jnp.exp(scores - jnp.max(scores, axis=1, keepdims=True))
        probs = powers * (1.0 / jnp.sum(powers, axis=1, keepdims=True))
        s_probs[here, :] = probs
        s_low[here, :] = probs.astype(BF16)
    put_probs = fetch(s_probs, probs_hbm, sems.at[6])
    mixed_wide = mm(s_low[...], s_value[...])
    mixed = mm_tn(repeat, jnp.where(heads, mixed_wide, 0.0).astype(BF16))
    mixed = (mixed * mask).astype(BF16)
    early_ref[:, 0:full_width] = mixed
    early_ref[:, full_width : 2 * full_width] = stream_rows.astype(BF16)
    get_wo.wait()
    middle = stream_rows + mm(mixed, s_wo[...]) + bo[...]
    middle_ref[...] = middle
    mid_hat, _ = normed(middle, mask, width)
    two = ((mid_hat * fg[...] + fb[...]) * mask).astype(BF16)
    pooled_ref[...] = middle + bn[...]
    hidden_width = jnp.where(is_text, MLP_TXT, full_hidden)
    hidden_mask = (iota((1, full_hidden), 1) < hidden_width).astype(F32)

    def forward(at):
        pre = mm(two, s_ww[:, at]) + bw[:, at]
        gate = sigmoid(1.702 * pre)
        active = pre * gate * hidden_mask[:, at]
        slope_ref[:, at] = (gate + 1.702 * active * (1.0 - gate)) * hidden_mask[:, at]
        pooled_ref[...] += mm(active.astype(BF16), s_wn[at, :])

    hidden.each(forward)
    out_hat, out_inv = normed(pooled_ref[...], mask, width)
    early_ref[:, 2 * full_width : 3 * full_width] = out_hat.astype(BF16)
    lane = iota((pairs, 128), 1)
    numbers = jnp.zeros((pairs, 128), F32)
    for place in range(3):
        part = out_inv.astype(BF16).astype(F32)
        numbers = jnp.where(lane == place, part, numbers)
        out_inv = out_inv - part
    early_ref[:, 3 * full_width :] = numbers.astype(BF16)
    three = ((out_hat * lg[...] + lb[...]) * mask).astype(BF16)
    get_we.wait()
    embedded = mm(three, s_we[...])
    embedded_ref[...] = embedded
    unit_ref[...] = (
        embedded * lax.rsqrt(jnp.sum(embedded * embedded, axis=-1, keepdims=True) + 1e-06)
    ).astype(BF16)
    query_ref[...] = query
    for copy in (put_hat, put_inv, put_probs):
        copy.wait()


def means_kernel(
    dims,
    ends_ref,
    ag,
    ab,
    hat_ref,
    probs_ref,
    query_ref,
    triple_hbm,
    turned_ref,
    spread_ref,
    keys_ref,
    hat_rows_ref,
    s_weight,
    s_turn,
    sems,
):
    pairs, tokens, full_width, full_hidden = dims
    is_text, width, mask = tower_sizes(full_width, full_hidden)
    get_weight = fetch(triple_hbm.at[0, 1], s_weight, sems.at[0])
    rows = probs_ref.shape[0]
    low = probs_ref[...].astype(BF16)
    spread = mm(low, hat_ref[...])
    spread_ref[...] = spread
    total = jnp.sum(low.astype(F32), axis=1, keepdims=True)
    s_turn[rows:, :] = jnp.zeros((s_turn.shape[0] - rows, full_width), F32)
    s_turn[0:rows, :] = (spread * ag[...] + total * ab[...]) * mask
    turned_ref[...] = s_turn[...].T.astype(BF16)
    pick = one_hot(iota((pairs, tokens), 1).astype(F32) == pooled_spots(ends_ref, is_text, pairs, 1))
    hat_rows_ref[...] = mm(pick, hat_ref[...]).astype(BF16)
    wide = mm(repeat_rows(rows, pairs), query_ref[...])
    wide = jnp.where(head_mask(rows, pairs, full_width), wide, 0.0).astype(BF16)
    get_weight.wait()
    keys_ref[...] = mm_nt(wide, s_weight[...]).astype(BF16)


def in_order(pieces, stages, pairs, block, at):
    here = lax.axis_index("dp")
    row = at + iota((block, 1), 0)
    owner = lax.div(row, pairs)
    apart = lax.bitwise_xor(owner, here)
    place = jnp.zeros_like(owner)
    weight = 1
    for shift, bits in stages:
        digit = lax.bitwise_and(lax.shift_right_logical(apart, shift), (1 << bits) - 1)
        place = place + digit * weight
        weight = weight << bits
    column = place * pairs + row - owner * pairs
    total = None
    first = 0
    for piece in pieces:
        count = piece.shape[0]
        part = mm(one_hot(iota((block, count), 1) + first == column), piece[...])
        total = part if total is None else total + part
        first += count
    return total.astype(BF16)


def over_blocks(count, step):
    if count == 1:
        step(0)
    else:

        def one(index, carry):
            step(index)
            return carry

        lax.fori_loop(0, count, one, 0)


def block_rows(total):
    return 320 if total % 320 == 0 else total


def loss_kernel(
    dims,
    own_rel,
    other_rel,
    flags_ref,
    logit_scale,
    loss_scale,
    ag,
    ab,
    triple_hbm,
    triple_bias,
    wo_hbm,
    fg,
    ww_hbm,
    wn_hbm,
    lg,
    we_hbm,
    hat_hbm,
    probs_hbm,
    spread_ref,
    keys_ref,
    embedded_ref,
    pooled_ref,
    middle_ref,
    slope_ref,
    hat_rows_ref,
    loss_ref,
    hits_ref,
    scale_ref,
    grad_all_ref,
    late_ref,
    queries_ref,
    back_ref,
    values_ref,
    rows_one_ref,
    rows_mid_ref,
    s_own,
    s_other,
    s_triple,
    s_wo,
    s_ww,
    s_wn,
    s_we,
    s_hat,
    s_probs,
    s_rows,
    s_two,
    s_turn,
    s_slab,
    sems,
    hidden_sems,
):
    pairs, tokens, full_width, full_hidden, stages = dims
    all_pairs = own_rel.shape[0]
    block = block_rows(all_pairs)
    here = lax.axis_index("dp")
    is_text, width, mask = tower_sizes(full_width, full_hidden)
    rows = full_width // HEAD * pairs
    get_we = fetch(we_hbm.at[0], s_we, sems.at[0])
    hidden = Hidden(ww_hbm, wn_hbm, s_ww, s_wn, hidden_sems, full_hidden // CHUNK)
    hidden.start((1, 0))
    get_wo = fetch(wo_hbm.at[0], s_wo, sems.at[1])
    get_triple = fetch(triple_hbm.at[0], s_triple, sems.at[2])
    get_hat = fetch(hat_hbm, s_hat, sems.at[3])
    get_probs = fetch(probs_hbm, s_probs, sems.at[4])

    def place(index):
        at = pl.multiple_of(index * block, block)
        s_own[pl.ds(at, block), :] = in_order([own_rel], stages, pairs, block, at)
        s_other[pl.ds(at, block), :] = in_order([other_rel], stages, pairs, block, at)

    over_blocks(all_pairs // block, place)
    live = (flags_ref[...] > 0).astype(F32)
    live_pairs = jnp.sum(live, axis=1, keepdims=True)
    factor = jnp.exp(logit_scale[...])
    row_weight = loss_scale[...] / (2.0 * live_pairs)
    loss_ref[...] = jnp.zeros_like(loss_ref)
    hits_ref[...] = jnp.zeros_like(hits_ref)
    scale_ref[...] = jnp.zeros_like(scale_ref)
    grad_all_ref[...] = jnp.zeros_like(grad_all_ref)

    def part(index):
        at = pl.multiple_of(index * block, block)
        eye = at + iota((block, all_pairs), 0) == iota((block, all_pairs), 1)
        live_rows = jnp.sum(jnp.where(eye, live, 0.0), axis=1, keepdims=True)

        def one_way(left, right):
            logits = mm_nt(left, right) * factor
            masked = jnp.where(live > 0.5, logits, -1e30)
            peak = jnp.max(masked, axis=1, keepdims=True)
            powers = jnp.exp(masked - peak)
            total = jnp.sum(powers, axis=1, keepdims=True)
            log_total = peak + jnp.log(total)
            matched = jnp.sum(jnp.where(eye, logits, 0.0), axis=1, keepdims=True)
            gap = jnp.where(live_rows > 0.5, log_total - matched, 0.0)
            grads = (
                (powers / total - eye.astype(F32)) * (live_rows * row_weight)
            ).astype(BF16)
            loss = jnp.sum(live_rows * gap, axis=0, keepdims=True)
            hits = jnp.sum(live_rows * jnp.exp(-gap), axis=0, keepdims=True)
            scale = jnp.sum(
                jnp.sum(grads.astype(F32) * logits, axis=1, keepdims=True),
                axis=0,
                keepdims=True,
            )
            return grads, loss, hits, scale

        own = s_own[pl.ds(at, block), :]
        other = s_other[pl.ds(at, block), :]
        grads, loss_one, hits_one, scale_one = one_way(own, s_other[...])
        grad_all_ref[pl.ds(at, block), :] += factor * mm(grads, s_other[...])
        grads, loss_two, hits_two, scale_two = one_way(other, s_own[...])
        grad_all_ref[...] += factor * mm_tn(grads, other)
        loss_ref[...] += loss_one + loss_two
        hits_ref[...] += hits_one + hits_two
        scale_ref[...] += scale_one + scale_two

    over_blocks(all_pairs // block, part)
    loss_ref[...] = loss_ref[...] / (2.0 * live_pairs)
    hits_ref[...] = hits_ref[...] / (2.0 * live_pairs)

    for pair in range(pairs):
        s_rows[pair : pair + 1, :] = grad_all_ref[pl.ds(here * pairs + pair, 1), :]

    gain, shift = ag[...] * mask, ab[...] * mask
    grad_embed = embed_back(embedded_ref[...], s_rows[...])
    get_we.wait()
    grad_three = mm_nt(grad_embed, s_we[...])
    out_hat, out_inv = normed(pooled_ref[...], mask, width)
    grad_pooled = norm_back(out_hat, out_inv, lg[...] * mask, grad_three, mask, width)
    branch = grad_pooled.astype(BF16)
    s_two[...] = jnp.zeros_like(s_two)

    def backward(at):
        grad_active = mm_nt(branch, s_wn[at, :])
        grad_hidden = (grad_active * slope_ref[:, at]).astype(BF16)
        s_two[...] += mm_nt(grad_hidden, s_ww[:, at])

    hidden.each(backward)
    mid_hat, mid_inv = normed(middle_ref[...], mask, width)
    grad_two = s_two[...] * mask
    grad_middle = grad_pooled + norm_back(mid_hat, mid_inv, fg[...] * mask, grad_two, mask, width)
    rows_mid_ref[...] = grad_middle
    attention = grad_middle.astype(BF16)
    get_wo.wait()
    grad_mixed = (mm_nt(attention, s_wo[...]) * mask).astype(BF16)
    repeat = repeat_rows(rows, pairs)
    heads = head_mask(rows, pairs, full_width)
    wide = jnp.where(heads, mm(repeat, grad_mixed), 0.0)
    get_triple.wait()
    along = mm_nt(wide.astype(BF16), s_triple[2])
    values_low = along.astype(BF16)
    values_ref[...] = values_low
    offset = jnp.sum(along * shift, axis=1, keepdims=True) + jnp.sum(
        wide * triple_bias[0, 1:2, :], axis=1, keepdims=True
    )
    get_hat.wait()
    get_probs.wait()
    grad_probs = mm_nt((along * gain).astype(BF16), s_hat[...]) + offset
    probs = s_probs[...]
    inner = jnp.sum(grad_probs * probs, axis=1, keepdims=True)
    back = (probs * (grad_probs - inner)).astype(BF16)
    back_ref[...] = back
    spread = mm(back, s_hat[...])
    total = jnp.sum(back.astype(F32), axis=1, keepdims=True)
    means = (spread * gain + total * shift).astype(BF16)
    query_wide = mm(means, s_triple[1]) * 0.125
    grad_query = mm_tn(repeat, jnp.where(heads, query_wide, 0.0).astype(BF16)).astype(BF16)
    queries_ref[...] = grad_query
    rows_one = mm_nt(grad_query, s_triple[0]) * mask
    rows_one_ref[...] = rows_one
    values_wide = values_low.astype(F32)
    keys_wide = keys_ref[...].astype(F32)
    prob_total = jnp.sum(probs.astype(BF16).astype(F32), axis=1, keepdims=True)
    gain_sum = (
        sums_of(values_wide * spread_ref[...])
        + sums_of(keys_wide * spread)
        + sums_of(rows_one * hat_rows_ref[...].astype(F32))
    )
    shift_sum = (
        sums_of(values_wide * prob_total) + sums_of(keys_wide * total) + sums_of(rows_one)
    ) * mask
    s_turn[rows:, :] = jnp.zeros((s_turn.shape[0] - rows, full_width), F32)
    s_turn[0:rows, :] = means.astype(F32)
    slot = rows
    for vector in (gain_sum, shift_sum):
        for _ in range(3):
            low = vector.astype(BF16).astype(F32)
            s_turn[slot : slot + 1, :] = low
            vector = vector - low
            slot += 1
    lanes = s_turn.shape[0]
    late_ref[:, 0:lanes] = s_turn[...].T.astype(BF16)
    if late_ref.shape[1] > lanes:
        turned = grad_query.astype(F32).T
        slab = s_slab.shape[0]
        s_slab[...] = jnp.zeros_like(s_slab)
        for place in range(full_width // slab):
            down = slice(place * slab, (place + 1) * slab)
            s_slab[:, place * pairs : (place + 1) * pairs] = turned[down, :]
        slab_low = s_slab[...].astype(BF16)
        for place in range(full_width // slab):
            late_ref[place * slab : (place + 1) * slab, lanes:] = slab_low


def rows_kernel(dims, *refs):
    pairs, tokens, full_width, full_hidden, slice_width, slice_hidden, stages, pieces = dims
    early = refs[:pieces]
    (
        ends_ref,
        hat_hbm,
        inv_hbm,
        probs_hbm,
        back_ref,
        value_factors_ref,
        keys_ref,
        rows_one_ref,
        rows_mid_ref,
        grad_ref,
        ag,
        ab,
        triple_hbm,
        triple_bias,
        wo_hbm,
        bo,
        fg,
        fb,
        ww_hbm,
        bw,
        wn_hbm,
        lg,
        lb,
        we_hbm,
        out_hbm,
        ones_ref,
        queries_ref,
        values_ref,
        embed_ref,
        narrow_ref,
        widen_ref,
        mixer_ref,
        final_gain_ref,
        final_bias_ref,
        feed_gain_ref,
        feed_bias_ref,
        narrow_bias_ref,
        mixer_bias_ref,
        value_bias_ref,
        widen_bias_ref,
        s_triple,
        s_wo,
        s_ww,
        s_wn,
        s_we,
        s_vectors,
        s_hat,
        s_inv,
        s_probs,
        s_left,
        s_right,
        s_out,
        sems,
        hidden_sems,
        out_sems,
    ) = refs[pieces:]
    all_pairs = grad_ref.shape[0]
    block = block_rows(all_pairs)
    here = lax.axis_index("dp")
    is_text, width, mask = tower_sizes(full_width, full_hidden)
    get_probs = fetch(probs_hbm, s_probs, sems.at[3])
    get_hat = fetch(hat_hbm, s_hat, sems.at[4])
    get_inv = fetch(inv_hbm, s_inv, sems.at[5])
    get_wo = fetch(wo_hbm.at[0], s_wo, sems.at[1])
    get_we = fetch(we_hbm.at[0], s_we, sems.at[2])
    hidden = Hidden(ww_hbm, wn_hbm, s_ww, s_wn, hidden_sems, full_hidden // CHUNK)
    hidden.start((0, 1))
    get_triple = fetch(triple_hbm.at[0, 0], s_triple, sems.at[0])
    rows = full_width // HEAD * pairs
    token_gain = ag[...] * mask
    s_left[rows : 2 * rows, :] = back_ref[...]
    s_right[0:rows, :] = value_factors_ref[...]
    s_right[rows : 2 * rows, :] = keys_ref[...]
    spots = pooled_spots(ends_ref, is_text, pairs, 3)
    s_left[2 * rows :, :] = one_hot(iota((3 * pairs, tokens), 1).astype(F32) == spots)
    s_right[2 * rows :, :] = three_parts(rows_one_ref[...])
    middle_parts = three_parts(rows_mid_ref[...])
    ones = one_hot(iota((full_width, 128), 0).astype(F32) < width)
    get_probs.wait()
    s_left[0:rows, :] = s_probs[...].astype(BF16)
    get_hat.wait()
    get_inv.wait()

    def put(at, count):
        spot = pl.ds(at, count)
        return pltpu.make_async_copy(
            s_out.at[spot, :], out_hbm.at[0, spot, :], out_sems.at[at // NORM_ROWS]
        )

    def norm_rows(at, count):
        spot = pl.ds(at, count)
        upward = mm_tn(s_left[:, spot], s_right[...])
        hat = s_hat[spot, :].astype(F32)
        scaled = upward * token_gain
        mean = mm(scaled.astype(BF16), ones) / width
        along = mm((scaled * hat).astype(BF16), ones) / width
        s_out[spot, :] = across(s_inv[spot, :], full_width) * (
            scaled - across(mean, full_width) * mask - hat * across(along, full_width)
        ) + mm_tn(s_left[2 * rows :, spot], middle_parts)
        put(at, count).start()

    over_tokens(tokens, NORM_ROWS, norm_rows)
    for ref in (embed_ref, narrow_ref, widen_ref, mixer_ref, widen_bias_ref, s_vectors):
        ref[...] = jnp.zeros_like(ref)
    lane = iota((full_width, slice_width), 0)
    pick = one_hot(
        (lane == here * slice_width + iota((full_width, slice_width), 1))
        & (lane.astype(F32) < width)
    )
    hidden_width = jnp.where(is_text, MLP_TXT, full_hidden)
    hidden_mask = (iota((1, full_hidden), 1) < hidden_width).astype(F32)
    gain, shift = lg[...] * mask, lb[...] * mask
    feed_gain = fg[...] * mask
    get_wo.wait()
    get_we.wait()

    def part(index):
        at = pl.multiple_of(index * block, block)
        here_rows = pl.ds(at, block)
        arrived = in_order(early, stages, pairs, block, at)
        mixed = arrived[:, 0:full_width]
        stream_rows = arrived[:, full_width : 2 * full_width].astype(F32)
        out_hat = arrived[:, 2 * full_width : 3 * full_width].astype(F32)
        out_inv = jnp.sum(arrived[:, 3 * full_width :].astype(F32), axis=1, keepdims=True)
        three = (out_hat * gain + shift).astype(BF16)
        grad_embed = embed_back(mm(three, s_we[...]), grad_ref[here_rows, :])
        embed_ref[0] += mm_tn(mm(three, pick).astype(BF16), grad_embed)
        grad_three = mm_nt(grad_embed, s_we[...])
        s_vectors[0:1, :] += sums_of(grad_three * out_hat)
        s_vectors[1:2, :] += sums_of(grad_three)
        grad_pooled = norm_back(out_hat, out_inv, gain, grad_three, mask, width)
        branch = grad_pooled.astype(BF16)
        s_vectors[2:3, :] += sums_of(branch.astype(F32))
        middle = stream_rows + mm(mixed, s_wo[...]) + bo[...]
        mid_hat, mid_inv = normed(middle, mask, width)
        two = ((mid_hat * fg[...] + fb[...]) * mask).astype(BF16)
        grad_two = jnp.zeros((block, full_width), F32)
        active_slice = jnp.zeros((block, slice_hidden), F32)
        hidden_slice = jnp.zeros((block, slice_hidden), F32)
        for first in range(0, full_hidden, CHUNK):
            lanes = slice(first, first + CHUNK)
            if all_pairs == block:
                hidden.wait(first // CHUNK)
            pre = mm(two, s_ww[:, lanes]) + bw[:, lanes]
            gate = sigmoid(1.702 * pre)
            active = pre * gate
            slope = (gate + 1.702 * active * (1.0 - gate)) * hidden_mask[:, lanes]
            grad_hidden = (mm_nt(branch, s_wn[lanes, :]) * slope).astype(BF16)
            grad_two = grad_two + mm_nt(grad_hidden, s_ww[:, lanes])
            row = first + iota((CHUNK, slice_hidden), 0)
            chosen = one_hot(
                (row == here * slice_hidden + iota((CHUNK, slice_hidden), 1))
                & (row < hidden_width)
            )
            active_slice = active_slice + mm(active.astype(BF16), chosen)
            hidden_slice = hidden_slice + mm(grad_hidden, chosen)
        narrow_ref[0] += mm_tn(active_slice.astype(BF16), branch)
        widen_ref[0] += mm_tn(hidden_slice.astype(BF16), two)
        widen_bias_ref[...] += sums_of(hidden_slice)
        s_vectors[3:4, :] += sums_of(grad_two * mid_hat)
        s_vectors[4:5, :] += sums_of(grad_two)
        grad_middle = grad_pooled + norm_back(mid_hat, mid_inv, feed_gain, grad_two, mask, width)
        attention = grad_middle.astype(BF16)
        s_vectors[5:6, :] += sums_of(attention.astype(F32))
        mixer_ref[0] += mm_tn(mm(mixed, pick).astype(BF16), attention)
        grad_mixed = (mm_nt(attention, s_wo[...]) * mask).astype(BF16)
        values_ref[here_rows, :] = grad_mixed
        s_vectors[6:7, :] += sums_of(grad_mixed.astype(F32))
        rows_hat, _ = normed(stream_rows, mask, width)
        one = ((rows_hat * ag[...] + ab[...]) * mask).astype(BF16)
        ones_ref[here_rows, :] = mm(one, pick).astype(BF16)
        if all_pairs == block:
            get_triple.wait()
        query = (mm(one, s_triple[...]) + triple_bias[0, 0:1, :]) * mask
        queries_ref[here_rows, :] = query.astype(BF16)

    if all_pairs != block:
        get_triple.wait()
        for chunk in range(full_hidden // CHUNK):
            hidden.wait(chunk)
    over_blocks(all_pairs // block, part)
    over_tokens(tokens, NORM_ROWS, lambda at, count: put(at, count).wait())
    vectors = dot_dims(s_vectors[...], pick.astype(F32), 1, 0, lax.Precision.HIGHEST)
    for slot, ref in enumerate(
        (
            final_gain_ref,
            final_bias_ref,
            narrow_bias_ref,
            feed_gain_ref,
            feed_bias_ref,
            mixer_bias_ref,
            value_bias_ref,
        )
    ):
        ref[...] = vectors[slot : slot + 1, :]


def last_kernel(dims, *refs):
    pairs, full_width, full_hidden, slice_width, stages, pieces = dims
    arrived = refs[:pieces]
    (
        late_ref,
        means_ref,
        ones_ref,
        queries_ref,
        values_ref,
        value_bias_ref,
        triple_ref,
        gain_ref,
        shift_ref,
        bias_ref,
        s_keys,
        s_means,
        s_turned,
        s_late,
        s_sums,
    ) = refs[pieces:]
    here = lax.axis_index("dp")
    count = late_ref.shape[0]
    lanes = means_ref.shape[2]
    heads = full_width // HEAD
    rows = heads * pairs
    all_pairs = queries_ref.shape[0]
    s_late[...] = jnp.zeros_like(s_late)
    if not arrived:
        for source in range(count):
            now = late_ref[source]
            s_late[...] += now[:, 0:lanes].astype(F32)
            means = means_ref[source]
            across_now = slice(source * pairs, (source + 1) * pairs)
            for head in range(heads):
                down = slice(head * slice_width, (head + 1) * slice_width)
                lane = slice(head * pairs, (head + 1) * pairs)
                s_keys[down, across_now] = now[:, lane]
                s_means[down, across_now] = means[:, lane]
            for slab in range(count):
                down = slice(slab * slice_width, (slab + 1) * slice_width)
                first = lanes + slab * pairs
                s_turned[down, across_now] = now[:, first : first + pairs]
        left = iota((slice_width, 2 * HEAD), 1) < HEAD
        for two in range(heads // 2):
            down = slice(two * 2 * slice_width, (two + 1) * 2 * slice_width)
            lane = slice(two * 2 * HEAD, (two + 1) * 2 * HEAD)
            both = mm(s_keys[down, :], queries_ref[:, lane]) * 0.125
            triple_ref[0, 1, :, lane] = jnp.where(left, both[0:slice_width], both[slice_width:])
            both = mm(s_means[down, :], values_ref[:, lane])
            triple_ref[0, 2, :, lane] = jnp.where(left, both[0:slice_width], both[slice_width:])
        triple_ref[0, 0] = mm(s_turned[...], ones_ref[...]).T
        mine = s_turned[pl.ds(pl.multiple_of(here * slice_width, slice_width), slice_width), :]
        sums = mm_nt(jnp.ones((8, all_pairs), BF16), mine)
    else:
        block = block_rows(all_pairs)
        triple_ref[...] = jnp.zeros_like(triple_ref)
        s_sums[...] = jnp.zeros_like(s_sums)

        def part(index):
            at = pl.multiple_of(index * block, block)
            grad_query = in_order(arrived, stages, pairs, block, at)
            triple_ref[0, 0] += mm_tn(ones_ref[pl.ds(at, block), :], grad_query)
            s_sums[0:1, :] += sums_of(grad_query.astype(F32))

        over_blocks(all_pairs // block, part)
        head = head_mask(lanes, pairs, full_width)

        def one(source, carry):
            now = late_ref[source]
            s_late[...] += now.astype(F32)
            row = iota((lanes, all_pairs), 0)
            column = iota((lanes, all_pairs), 1)
            repeat = one_hot((column == source * pairs + lax.rem(row, pairs)) & (row < rows))
            means = means_ref[source]
            for which, left, origin in ((1, now, queries_ref), (2, means, values_ref)):
                wide = jnp.where(head, mm(repeat, origin[...]), 0.0).astype(BF16)
                triple_ref[0, which] += mm(left, wide)
            return carry

        lax.fori_loop(0, count, one, 0)
        triple_ref[0, 1] = triple_ref[0, 1] * 0.125
        pick = (
            iota((full_width, slice_width), 0)
            == here * slice_width + iota((full_width, slice_width), 1)
        ).astype(F32)
        sums = dot_dims(s_sums[...], pick, 1, 0, lax.Precision.HIGHEST)
    lane = iota((8, lanes), 1)
    row = iota((8, lanes), 0)
    slot = rows + row * 3
    chosen = ((lane >= slot) & (lane < slot + 3) & (row < 2)).astype(F32)
    from_late = dot_dims(chosen, s_late[...], 1, 1, lax.Precision.HIGHEST)
    gain_ref[...] = from_late[0:1, :]
    shift_ref[...] = from_late[1:2, :]
    bias_ref[0, 0:1, :] = sums[0:1, :]
    bias_ref[0, 1:2, :] = value_bias_ref[...]


def stages_of(count):
    bits = count.bit_length() - 1
    stages = []
    while bits > 0:
        take = 2 if bits >= 2 else 1
        bits -= take
        stages.append((bits, take))
    return tuple(stages)


def exchange(block, axis, stage):
    count = lax.axis_size(axis)
    shift, bits = stage
    parts = [block]
    for apart in range(1, 1 << bits):
        route = [(low, low ^ (apart << shift)) for low in range(count)]
        parts.append(lax.ppermute(block, axis, route))
    return parts


def call(kernel, ins, outs, scratch, in_hbm=(), out_hbm=(), cost=None):
    vmem = pl.BlockSpec(memory_space=pltpu.VMEM)
    anywhere = pl.BlockSpec(memory_space=pl.ANY)
    specs = [anywhere if index in in_hbm else vmem for index in range(len(ins))]
    out_specs = [anywhere if index in out_hbm else vmem for index in range(len(outs))]
    flops, moved = cost
    return pl.pallas_call(
        kernel,
        out_shape=[jax.ShapeDtypeStruct(shape, kind) for shape, kind in outs],
        in_specs=specs,
        out_specs=out_specs,
        scratch_shapes=scratch,
        compiler_params=pltpu.CompilerParams(vmem_limit_bytes=VMEM_LIMIT),
        cost_estimate=pl.CostEstimate(flops=flops, bytes_accessed=moved, transcendentals=0),
    )(*ins)


def body(
    block_input,
    segments,
    caption_ends,
    pair_flags,
    attention_gain,
    attention_bias,
    triple_weight,
    triple_bias,
    mixer_weight,
    mixer_bias,
    feed_gain,
    feed_bias,
    widen_weight,
    widen_bias,
    narrow_weight,
    narrow_bias,
    final_gain,
    final_bias,
    embed_weight,
    logit_scale,
    loss_scale,
):
    tokens, width = block_input.shape[1:]
    hidden = widen_weight.shape[2]
    emb = embed_weight.shape[2]
    pairs = caption_ends.shape[0]
    count = lax.axis_size("dp")
    all_pairs = pair_flags.shape[0]
    heads = width // HEAD
    rows = heads * pairs
    lanes = -(-(rows + 12) // 128) * 128
    slice_width = width // count
    slice_hidden = hidden // count
    stages = stages_of(count)
    compact = count <= 16 and slice_width % 16 == 0
    slab_lanes = -(-all_pairs // 128) * 128
    ends = caption_ends.reshape(1, pairs)
    dma = pltpu.SemaphoreType.DMA
    weights_scratch = [
        pltpu.VMEM((3, width, width), BF16),
        pltpu.VMEM((width, width), BF16),
        pltpu.VMEM((width, hidden), BF16),
        pltpu.VMEM((hidden, width), BF16),
        pltpu.VMEM((width, emb), BF16),
    ]
    dims = (pairs, tokens, width, hidden)
    chunk_count = hidden // CHUNK
    (
        unit,
        early,
        hat,
        invert,
        probs,
        query,
        embedded,
        pooled,
        middle,
        slope,
    ) = call(
        partial(attend_kernel, dims),
        (
            ends,
            block_input,
            attention_gain,
            attention_bias,
            triple_weight,
            triple_bias,
            mixer_weight,
            mixer_bias,
            feed_gain,
            feed_bias,
            widen_weight,
            widen_bias,
            narrow_weight,
            narrow_bias,
            final_gain,
            final_bias,
            embed_weight,
        ),
        [
            ((pairs, emb), BF16),
            ((pairs, 3 * width + 128), BF16),
            ((tokens, width), BF16),
            ((tokens, 128), F32),
            ((rows, tokens), F32),
            ((pairs, width), BF16),
            ((pairs, emb), F32),
            ((pairs, width), F32),
            ((pairs, width), F32),
            ((pairs, hidden), F32),
        ],
        [
            pltpu.VMEM((tokens, width), BF16),
            pltpu.VMEM((tokens, width), BF16),
            pltpu.VMEM((tokens, width), BF16),
            pltpu.VMEM((tokens, 128), F32),
            pltpu.VMEM((rows, tokens), F32),
            pltpu.VMEM((tokens, width), BF16),
            pltpu.VMEM((tokens, width), BF16),
        ]
        + weights_scratch
        + [
            pltpu.VMEM((rows, tokens), BF16),
            dma((7,)),
            dma((2, chunk_count)),
        ],
        in_hbm=(1, 4, 6, 10, 12, 16),
        out_hbm=(2, 3, 4),
        cost=(10**9, 20 * 10**6),
    )
    turned, spread, keys, hat_rows = call(
        partial(means_kernel, dims),
        (ends, attention_gain, attention_bias, hat, probs, query, triple_weight),
        [
            ((width, lanes), BF16),
            ((rows, width), F32),
            ((rows, width), BF16),
            ((pairs, width), BF16),
        ],
        [
            pltpu.VMEM((width, width), BF16),
            pltpu.VMEM((lanes, width), F32),
            dma((1,)),
        ],
        in_hbm=(6,),
        cost=(10**9, 5 * 10**6),
    )
    early_rows, own_rel = early, unit
    flags = pair_flags.reshape(1, all_pairs)
    for index, stage in enumerate(stages):
        own_parts = exchange(own_rel, "dp", stage)
        if index + 1 < len(stages):
            own_parts, early_rows, turned, spread, keys, hat_rows, flags = lax.optimization_barrier(
                (own_parts, early_rows, turned, spread, keys, hat_rows, flags)
            )
            early_rows = jnp.concatenate(exchange(early_rows, "dp", stage), axis=0)
        own_rel = jnp.concatenate(own_parts, axis=0)
    means_all = lax.all_to_all(turned, "dp", 0, 0, tiled=True).reshape(count, slice_width, lanes)
    other_rel = lax.ppermute(own_rel, "tower", [(0, 1), (1, 0)])
    early_pieces = exchange(early_rows, "dp", stages[-1])
    (
        loss,
        hits,
        scale,
        grad_all,
        late,
        queries,
        back,
        values,
        rows_one,
        rows_mid,
    ) = call(
        partial(loss_kernel, dims + (stages,)),
        (
            own_rel,
            other_rel,
            flags,
            logit_scale.reshape(1, 1),
            loss_scale.reshape(1, 1),
            attention_gain,
            attention_bias,
            triple_weight,
            triple_bias,
            mixer_weight,
            feed_gain,
            widen_weight,
            narrow_weight,
            final_gain,
            embed_weight,
            hat,
            probs,
            spread,
            keys,
            embedded,
            pooled,
            middle,
            slope,
            hat_rows,
        ),
        [
            ((1, 1), F32),
            ((1, 1), F32),
            ((1, 1), F32),
            ((all_pairs, emb), F32),
            ((width, lanes + (slab_lanes if compact else 0)), BF16),
            ((pairs, width), BF16),
            ((rows, tokens), BF16),
            ((rows, width), BF16),
            ((pairs, width), F32),
            ((pairs, width), F32),
        ],
        [pltpu.VMEM((all_pairs, emb), BF16), pltpu.VMEM((all_pairs, emb), BF16)]
        + weights_scratch
        + [
            pltpu.VMEM((tokens, width), BF16),
            pltpu.VMEM((rows, tokens), F32),
            pltpu.VMEM((pairs, emb), F32),
            pltpu.VMEM((pairs, width), F32),
            pltpu.VMEM((lanes, width), F32),
            pltpu.VMEM((slice_width, slab_lanes), F32),
            dma((5,)),
            dma((2, chunk_count)),
        ],
        in_hbm=(7, 9, 11, 12, 14, 15, 16),
        cost=(10**9, 20 * 10**6),
    )
    early_pieces, late, queries = lax.optimization_barrier((early_pieces, late, queries))
    late_all = lax.all_to_all(late, "dp", 0, 0, tiled=True)
    late_all = late_all.reshape(count, slice_width, late.shape[1])
    late_pieces = []
    if not compact:
        late_pieces = [queries]
        for stage in stages:
            late_pieces = exchange(jnp.concatenate(late_pieces, axis=0), "dp", stage)
    ahead = len(early_pieces)
    vector = ((1, slice_width), F32)
    (
        block_grad,
        ones,
        query_rows,
        value_rows,
        grad_embed,
        grad_narrow,
        grad_widen,
        grad_mixer,
        grad_final_gain,
        grad_final_bias,
        grad_feed_gain,
        grad_feed_bias,
        grad_narrow_bias,
        grad_mixer_bias,
        grad_value_bias,
        grad_widen_bias,
    ) = call(
        partial(
            rows_kernel,
            (pairs, tokens, width, hidden, slice_width, slice_hidden, stages, ahead),
        ),
        tuple(early_pieces)
        + (
            ends,
            hat,
            invert,
            probs,
            back,
            values,
            keys,
            rows_one,
            rows_mid,
            grad_all,
            attention_gain,
            attention_bias,
            triple_weight,
            triple_bias,
            mixer_weight,
            mixer_bias,
            feed_gain,
            feed_bias,
            widen_weight,
            widen_bias,
            narrow_weight,
            final_gain,
            final_bias,
            embed_weight,
        ),
        [
            ((1, tokens, width), F32),
            ((all_pairs, slice_width), BF16),
            ((all_pairs, width), BF16),
            ((all_pairs, width), BF16),
            ((1, slice_width, emb), F32),
            ((1, slice_hidden, width), F32),
            ((1, slice_hidden, width), F32),
            ((1, slice_width, width), F32),
        ]
        + [vector] * 7
        + [((1, slice_hidden), F32)],
        [pltpu.VMEM((width, width), BF16)]
        + weights_scratch[1:]
        + [
            pltpu.VMEM((8, width), F32),
            pltpu.VMEM((tokens, width), BF16),
            pltpu.VMEM((tokens, 128), F32),
            pltpu.VMEM((rows, tokens), F32),
            pltpu.VMEM((2 * rows + 3 * pairs, tokens), BF16),
            pltpu.VMEM((2 * rows + 3 * pairs, width), BF16),
            pltpu.VMEM((tokens, width), F32),
            dma((6,)),
            dma((2, chunk_count)),
            dma((-(-tokens // NORM_ROWS),)),
        ],
        in_hbm=tuple(ahead + index for index in (1, 2, 3, 12, 14, 18, 20, 23)),
        out_hbm=(0,),
        cost=(3 * 10**9, 10 * 10**6),
    )
    grad_triple, grad_gain, grad_bias, grad_triple_bias = call(
        partial(last_kernel, (pairs, width, hidden, slice_width, stages, len(late_pieces))),
        tuple(late_pieces)
        + (late_all, means_all, ones, query_rows, value_rows, grad_value_bias),
        [
            ((1, 3, slice_width, width), F32),
            vector,
            vector,
            ((1, 2, slice_width), F32),
        ],
        [
            pltpu.VMEM((width // HEAD * slice_width, all_pairs), BF16),
            pltpu.VMEM((width // HEAD * slice_width, all_pairs), BF16),
            pltpu.VMEM((width, all_pairs), BF16),
            pltpu.VMEM((slice_width, lanes), F32),
            pltpu.VMEM((8, width), F32),
        ],
        cost=(10**9, 10 * 10**6),
    )
    return (
        loss[0, 0],
        hits[0, 0],
        block_grad,
        grad_gain,
        grad_bias,
        grad_triple,
        grad_triple_bias,
        grad_mixer,
        grad_mixer_bias,
        grad_feed_gain,
        grad_feed_bias,
        jnp.swapaxes(grad_widen, 1, 2),
        grad_widen_bias,
        grad_narrow,
        grad_narrow_bias,
        grad_final_gain,
        grad_final_bias,
        grad_embed,
        scale[0, 0],
    )


def solution(mesh):
    in_specs = (
        P("tower", "dp", None),
        P("dp", None),
        P("dp"),
        P(),
        P("tower", None),
        P("tower", None),
        P("tower", None, None, None),
        P("tower", None, None),
        P("tower", None, None),
        P("tower", None),
        P("tower", None),
        P("tower", None),
        P("tower", None, None),
        P("tower", None),
        P("tower", None, None),
        P("tower", None),
        P("tower", None),
        P("tower", None),
        P("tower", None, None),
        P(),
        P(),
    )
    out_specs = (
        P(),
        P(),
        P("tower", "dp", None),
        P("tower", "dp"),
        P("tower", "dp"),
        P("tower", None, "dp", None),
        P("tower", None, "dp"),
        P("tower", "dp", None),
        P("tower", "dp"),
        P("tower", "dp"),
        P("tower", "dp"),
        P("tower", None, "dp"),
        P("tower", "dp"),
        P("tower", "dp", None),
        P("tower", "dp"),
        P("tower", "dp"),
        P("tower", "dp"),
        P("tower", "dp", None),
        P(),
    )
    return jax.shard_map(body, mesh=mesh, in_specs=in_specs, out_specs=out_specs, check_vma=False)
```

```python
from functools import partial

import jax
import jax.numpy as jnp
from jax import lax
from jax.experimental import pallas as pl
from jax.experimental.pallas import tpu as pltpu
from jax.sharding import PartitionSpec as P

D_TXT = 512
MLP_TXT = 2048
HEAD = 64
IMG_TOK = 50
CTX = 77
F32 = jnp.float32
BF16 = jnp.bfloat16
VMEM_LIMIT = 62 * 1024 * 1024
CHUNK = 1024
NORM_ROWS = 272
PROJECT_ROWS = 1088


def dot_dims(left, right, left_dim, right_dim, precision=None):
    return lax.dot_general(
        left,
        right,
        (((left_dim,), (right_dim,)), ((), ())),
        preferred_element_type=F32,
        precision=precision,
    )


def mm(left, right):
    return dot_dims(left, right, 1, 0)


def mm_nt(left, right):
    return dot_dims(left, right, 1, 1)


def mm_tn(left, right):
    return dot_dims(left, right, 0, 0)


def iota(shape, dim):
    return lax.broadcasted_iota(jnp.int32, shape, dim)


def sigmoid(rows):
    return 1.0 / (1.0 + jnp.exp(-rows))


def one_hot(condition):
    return condition.astype(F32).astype(BF16)


def normed(rows, mask, width):
    mean = jnp.sum(rows * mask, axis=-1, keepdims=True) / width
    centre = (rows - mean) * mask
    invert = lax.rsqrt(jnp.sum(centre * centre, axis=-1, keepdims=True) / width + 1e-05)
    return centre * invert, invert


def norm_back(rows_hat, invert, gain, upward, mask, width):
    scaled = upward * gain
    mean = jnp.sum(scaled, axis=-1, keepdims=True) / width
    along = jnp.sum(scaled * rows_hat, axis=-1, keepdims=True) / width
    return invert * (scaled - mean * mask - rows_hat * along)


def sums_of(rows):
    return jnp.sum(rows, axis=0, keepdims=True)


def head_mask(rows, pairs, width):
    row = iota((rows, width), 0)
    first = lax.shift_right_logical(iota((rows, width), 1), 6) * pairs
    return (row >= first) & (row < first + pairs)


def repeat_rows(rows, pairs):
    row = iota((rows, pairs), 0)
    return one_hot(lax.rem(row, pairs) == iota((rows, pairs), 1))


def tower_sizes(full_width, full_hidden):
    is_text = lax.axis_index("tower") != 0
    width = jnp.where(is_text, D_TXT, full_width)
    mask = (iota((1, full_width), 1) < width).astype(F32)
    return is_text, width.astype(F32), mask


def fetch(source, target, semaphore):
    copy = pltpu.make_async_copy(source, target, semaphore)
    copy.start()
    return copy


def three_parts(rows):
    parts = []
    for _ in range(3):
        part = rows.astype(BF16).astype(F32)
        parts.append(part)
        rows = rows - part
    return jnp.concatenate(parts, axis=0).astype(BF16)


def over_tokens(tokens, size, step):
    for at in range(0, tokens, size):
        step(at, min(size, tokens - at))


def across(lane_sums, full_width):
    return jnp.concatenate([lane_sums] * (full_width // 128), axis=1)


def pooled_spots(ends_ref, is_text, pairs, copies):
    pair = lax.rem(iota((copies * pairs, pairs), 0), pairs)
    ends = jnp.where(pair == iota((copies * pairs, pairs), 1), ends_ref[...], 0).astype(F32)
    ends = jnp.sum(ends, axis=1, keepdims=True)
    firsts = (lax.rem(iota((copies * pairs, 1), 0), pairs) * IMG_TOK).astype(F32)
    return jnp.where(is_text, ends, firsts)


def embed_back(embedded, grad_unit):
    inv_norm = lax.rsqrt(jnp.sum(embedded * embedded, axis=-1, keepdims=True) + 1e-06)
    along = jnp.sum(embedded * grad_unit, axis=-1, keepdims=True)
    return (inv_norm * grad_unit - inv_norm * inv_norm * inv_norm * embedded * along).astype(BF16)


class Hidden:
    def __init__(self, widen_hbm, narrow_hbm, s_widen, s_narrow, sems, chunks):
        self.pairs = (
            (lambda at: widen_hbm.at[0, :, pl.ds(at, CHUNK)], lambda at: s_widen.at[:, pl.ds(at, CHUNK)]),
            (lambda at: narrow_hbm.at[0, pl.ds(at, CHUNK), :], lambda at: s_narrow.at[pl.ds(at, CHUNK), :]),
        )
        self.sems = sems
        self.chunks = chunks

    def copy(self, which, chunk):
        source, target = self.pairs[which]
        at = chunk * CHUNK
        if not isinstance(at, int):
            at = pl.multiple_of(at, CHUNK)
        return pltpu.make_async_copy(source(at), target(at), self.sems.at[which, chunk])

    def start(self, order):
        for chunk in range(self.chunks):
            for which in order:
                self.copy(which, chunk).start()

    def wait(self, chunk):
        self.copy(0, chunk).wait()
        self.copy(1, chunk).wait()

    def each(self, step):
        for chunk in range(self.chunks):
            self.wait(chunk)
            step(slice(chunk * CHUNK, (chunk + 1) * CHUNK))


def attend_kernel(
    dims,
    ends_ref,
    x_hbm,
    ag,
    ab,
    triple_hbm,
    triple_bias,
    wo_hbm,
    bo,
    fg,
    fb,
    ww_hbm,
    bw,
    wn_hbm,
    bn,
    lg,
    lb,
    we_hbm,
    unit_ref,
    early_ref,
    hat_hbm,
    inv_hbm,
    probs_hbm,
    query_ref,
    embedded_ref,
    pooled_ref,
    middle_ref,
    slope_ref,
    s_x,
    s_one,
    s_hat,
    s_inv,
    s_probs,
    s_key,
    s_value,
    s_triple,
    s_wo,
    s_ww,
    s_wn,
    s_we,
    s_low,
    sems,
    hidden_sems,
):
    pairs, tokens, full_width, full_hidden = dims
    is_text, width, mask = tower_sizes(full_width, full_hidden)
    rows = full_width // HEAD * pairs
    get_x = fetch(x_hbm.at[0], s_x, sems.at[0])
    get_triple = fetch(triple_hbm.at[0], s_triple, sems.at[1])
    gain, shift = ag[...] * mask, ab[...] * mask
    ones = one_hot((iota((full_width, 128), 0)).astype(F32) < width)
    hidden = Hidden(ww_hbm, wn_hbm, s_ww, s_wn, hidden_sems, full_hidden // CHUNK)
    get_x.wait()
    get_wo = fetch(wo_hbm.at[0], s_wo, sems.at[2])
    hidden.start((0, 1))
    get_we = fetch(we_hbm.at[0], s_we, sems.at[3])

    def norm_rows(at, count):
        here = pl.ds(at, count)
        low = s_x[here, :]
        mean = mm(low, ones) / width
        centre = low.astype(F32) - across(mean, full_width)
        square = centre * centre
        high = square.astype(BF16)
        low = (square - high.astype(F32)).astype(BF16)
        invert = lax.rsqrt((mm(high, ones) + mm(low, ones)) / width + 1e-05)
        hat = centre * across(invert, full_width)
        s_hat[here, :] = hat.astype(BF16)
        s_one[here, :] = (hat * gain + shift).astype(BF16)
        s_inv[here, :] = invert

    over_tokens(tokens, NORM_ROWS, norm_rows)
    put_hat = fetch(s_hat, hat_hbm, sems.at[4])
    put_inv = fetch(s_inv, inv_hbm, sems.at[5])
    pick = one_hot(iota((pairs, tokens), 1).astype(F32) == pooled_spots(ends_ref, is_text, pairs, 1))
    stream_rows = mm(pick, s_x[...]) * mask
    one = mm(pick, s_one[...]).astype(BF16)
    get_triple.wait()
    query = ((mm(one, s_triple[0]) + triple_bias[0, 0:1, :]) * (mask * 0.125)).astype(BF16)
    repeat = repeat_rows(rows, pairs)
    heads = head_mask(rows, pairs, full_width)
    wide = jnp.where(heads, mm(repeat, query), 0.0).astype(BF16)

    def project(at, count):
        here = pl.ds(at, count)
        s_key[here, :] = mm(s_one[here, :], s_triple[1]).astype(BF16)
        s_value[here, :] = (mm(s_one[here, :], s_triple[2]) + triple_bias[0, 1:2, :]).astype(BF16)

    over_tokens(tokens, PROJECT_ROWS, project)
    s_probs[...] = mm_nt(wide, s_key[...])
    last = pooled_spots(ends_ref, is_text, pairs, rows // pairs)
    pair = lax.rem(iota((rows, 1), 0), pairs)
    stops = jnp.where(
        pair - 1 == iota((rows, pairs), 1), ends_ref[...] + 1, 0
    ).astype(F32)
    first = jnp.where(is_text, jnp.sum(stops, axis=1, keepdims=True), last)
    last = jnp.where(is_text, last, last + (IMG_TOK - 1.0))
    step_rows = 48
    for at in range(0, rows, step_rows):
        here = slice(at, at + step_rows)
        place = iota((step_rows, tokens), 1).astype(F32)
        allowed = (place >= first[here]) & (place <= last[here])
        scores = jnp.where(allowed, s_probs[here, :], -1e30)
        powers = jnp.exp(scores - jnp.max(scores, axis=1, keepdims=True))
        probs = powers * (1.0 / jnp.sum(powers, axis=1, keepdims=True))
        s_probs[here, :] = probs
        s_low[here, :] = probs.astype(BF16)
    put_probs = fetch(s_probs, probs_hbm, sems.at[6])
    mixed_wide = mm(s_low[...], s_value[...])
    mixed = mm_tn(repeat, jnp.where(heads, mixed_wide, 0.0).astype(BF16))
    mixed = (mixed * mask).astype(BF16)
    early_ref[:, 0:full_width] = mixed
    early_ref[:, full_width : 2 * full_width] = stream_rows.astype(BF16)
    get_wo.wait()
    middle = stream_rows + mm(mixed, s_wo[...]) + bo[...]
    middle_ref[...] = middle
    mid_hat, _ = normed(middle, mask, width)
    two = ((mid_hat * fg[...] + fb[...]) * mask).astype(BF16)
    pooled_ref[...] = middle + bn[...]
    hidden_width = jnp.where(is_text, MLP_TXT, full_hidden)
    hidden_mask = (iota((1, full_hidden), 1) < hidden_width).astype(F32)

    def forward(at):
        pre = mm(two, s_ww[:, at]) + bw[:, at]
        gate = sigmoid(1.702 * pre)
        active = pre * gate * hidden_mask[:, at]
        slope_ref[:, at] = (gate + 1.702 * active * (1.0 - gate)) * hidden_mask[:, at]
        pooled_ref[...] += mm(active.astype(BF16), s_wn[at, :])

    hidden.each(forward)
    out_hat, out_inv = normed(pooled_ref[...], mask, width)
    early_ref[:, 2 * full_width : 3 * full_width] = out_hat.astype(BF16)
    lane = iota((pairs, 128), 1)
    numbers = jnp.zeros((pairs, 128), F32)
    for place in range(3):
        part = out_inv.astype(BF16).astype(F32)
        numbers = jnp.where(lane == place, part, numbers)
        out_inv = out_inv - part
    early_ref[:, 3 * full_width :] = numbers.astype(BF16)
    three = ((out_hat * lg[...] + lb[...]) * mask).astype(BF16)
    get_we.wait()
    embedded = mm(three, s_we[...])
    embedded_ref[...] = embedded
    unit_ref[...] = (
        embedded * lax.rsqrt(jnp.sum(embedded * embedded, axis=-1, keepdims=True) + 1e-06)
    ).astype(BF16)
    query_ref[...] = query
    for copy in (put_hat, put_inv, put_probs):
        copy.wait()


def means_kernel(
    dims,
    ends_ref,
    ag,
    ab,
    hat_ref,
    probs_ref,
    query_ref,
    triple_hbm,
    turned_ref,
    spread_ref,
    keys_ref,
    hat_rows_ref,
    s_weight,
    s_turn,
    sems,
):
    pairs, tokens, full_width, full_hidden = dims
    is_text, width, mask = tower_sizes(full_width, full_hidden)
    get_weight = fetch(triple_hbm.at[0, 1], s_weight, sems.at[0])
    rows = probs_ref.shape[0]
    low = probs_ref[...].astype(BF16)
    spread = mm(low, hat_ref[...])
    spread_ref[...] = spread
    total = jnp.sum(low.astype(F32), axis=1, keepdims=True)
    s_turn[rows:, :] = jnp.zeros((s_turn.shape[0] - rows, full_width), F32)
    s_turn[0:rows, :] = (spread * ag[...] + total * ab[...]) * mask
    turned_ref[...] = s_turn[...].T.astype(BF16)
    pick = one_hot(iota((pairs, tokens), 1).astype(F32) == pooled_spots(ends_ref, is_text, pairs, 1))
    hat_rows_ref[...] = mm(pick, hat_ref[...]).astype(BF16)
    wide = mm(repeat_rows(rows, pairs), query_ref[...])
    wide = jnp.where(head_mask(rows, pairs, full_width), wide, 0.0).astype(BF16)
    get_weight.wait()
    keys_ref[...] = mm_nt(wide, s_weight[...]).astype(BF16)


def in_order(pieces, stages, pairs, block, at):
    here = lax.axis_index("dp")
    row = at + iota((block, 1), 0)
    owner = lax.div(row, pairs)
    apart = lax.bitwise_xor(owner, here)
    place = jnp.zeros_like(owner)
    weight = 1
    for shift, bits in stages:
        digit = lax.bitwise_and(lax.shift_right_logical(apart, shift), (1 << bits) - 1)
        place = place + digit * weight
        weight = weight << bits
    column = place * pairs + row - owner * pairs
    total = None
    first = 0
    for piece in pieces:
        count = piece.shape[0]
        part = mm(one_hot(iota((block, count), 1) + first == column), piece[...])
        total = part if total is None else total + part
        first += count
    return total.astype(BF16)


def over_blocks(count, step):
    if count == 1:
        step(0)
    else:

        def one(index, carry):
            step(index)
            return carry

        lax.fori_loop(0, count, one, 0)


def block_rows(total):
    return 320 if total % 320 == 0 else total


def loss_kernel(
    dims,
    own_rel,
    other_rel,
    flags_ref,
    logit_scale,
    loss_scale,
    ag,
    ab,
    triple_hbm,
    triple_bias,
    wo_hbm,
    fg,
    ww_hbm,
    wn_hbm,
    lg,
    we_hbm,
    hat_hbm,
    probs_hbm,
    spread_ref,
    keys_ref,
    embedded_ref,
    pooled_ref,
    middle_ref,
    slope_ref,
    hat_rows_ref,
    loss_ref,
    hits_ref,
    scale_ref,
    grad_all_ref,
    late_ref,
    queries_ref,
    back_ref,
    values_ref,
    rows_one_ref,
    rows_mid_ref,
    s_own,
    s_other,
    s_triple,
    s_wo,
    s_ww,
    s_wn,
    s_we,
    s_hat,
    s_probs,
    s_rows,
    s_two,
    s_turn,
    s_slab,
    sems,
    hidden_sems,
):
    pairs, tokens, full_width, full_hidden, stages = dims
    all_pairs = own_rel.shape[0]
    block = block_rows(all_pairs)
    here = lax.axis_index("dp")
    is_text, width, mask = tower_sizes(full_width, full_hidden)
    rows = full_width // HEAD * pairs
    get_we = fetch(we_hbm.at[0], s_we, sems.at[0])
    hidden = Hidden(ww_hbm, wn_hbm, s_ww, s_wn, hidden_sems, full_hidden // CHUNK)
    hidden.start((1, 0))
    get_wo = fetch(wo_hbm.at[0], s_wo, sems.at[1])
    get_triple = fetch(triple_hbm.at[0], s_triple, sems.at[2])
    get_hat = fetch(hat_hbm, s_hat, sems.at[3])
    get_probs = fetch(probs_hbm, s_probs, sems.at[4])

    def place(index):
        at = pl.multiple_of(index * block, block)
        s_own[pl.ds(at, block), :] = in_order([own_rel], stages, pairs, block, at)
        s_other[pl.ds(at, block), :] = in_order([other_rel], stages, pairs, block, at)

    over_blocks(all_pairs // block, place)
    live = (flags_ref[...] > 0).astype(F32)
    live_pairs = jnp.sum(live, axis=1, keepdims=True)
    factor = jnp.exp(logit_scale[...])
    row_weight = loss_scale[...] / (2.0 * live_pairs)
    loss_ref[...] = jnp.zeros_like(loss_ref)
    hits_ref[...] = jnp.zeros_like(hits_ref)
    scale_ref[...] = jnp.zeros_like(scale_ref)
    grad_all_ref[...] = jnp.zeros_like(grad_all_ref)

    def part(index):
        at = pl.multiple_of(index * block, block)
        eye = at + iota((block, all_pairs), 0) == iota((block, all_pairs), 1)
        live_rows = jnp.sum(jnp.where(eye, live, 0.0), axis=1, keepdims=True)

        def one_way(left, right):
            logits = mm_nt(left, right) * factor
            masked = jnp.where(live > 0.5, logits, -1e30)
            peak = jnp.max(masked, axis=1, keepdims=True)
            powers = jnp.exp(masked - peak)
            total = jnp.sum(powers, axis=1, keepdims=True)
            log_total = peak + jnp.log(total)
            matched = jnp.sum(jnp.where(eye, logits, 0.0), axis=1, keepdims=True)
            gap = jnp.where(live_rows > 0.5, log_total - matched, 0.0)
            grads = (
                (powers / total - eye.astype(F32)) * (live_rows * row_weight)
            ).astype(BF16)
            loss = jnp.sum(live_rows * gap, axis=0, keepdims=True)
            hits = jnp.sum(live_rows * jnp.exp(-gap), axis=0, keepdims=True)
            scale = jnp.sum(
                jnp.sum(grads.astype(F32) * logits, axis=1, keepdims=True),
                axis=0,
                keepdims=True,
            )
            return grads, loss, hits, scale

        own = s_own[pl.ds(at, block), :]
        other = s_other[pl.ds(at, block), :]
        grads, loss_one, hits_one, scale_one = one_way(own, s_other[...])
        grad_all_ref[pl.ds(at, block), :] += factor * mm(grads, s_other[...])
        grads, loss_two, hits_two, scale_two = one_way(other, s_own[...])
        grad_all_ref[...] += factor * mm_tn(grads, other)
        loss_ref[...] += loss_one + loss_two
        hits_ref[...] += hits_one + hits_two
        scale_ref[...] += scale_one + scale_two

    over_blocks(all_pairs // block, part)
    loss_ref[...] = loss_ref[...] / (2.0 * live_pairs)
    hits_ref[...] = hits_ref[...] / (2.0 * live_pairs)

    for pair in range(pairs):
        s_rows[pair : pair + 1, :] = grad_all_ref[pl.ds(here * pairs + pair, 1), :]

    gain, shift = ag[...] * mask, ab[...] * mask
    grad_embed = embed_back(embedded_ref[...], s_rows[...])
    get_we.wait()
    grad_three = mm_nt(grad_embed, s_we[...])
    out_hat, out_inv = normed(pooled_ref[...], mask, width)
    grad_pooled = norm_back(out_hat, out_inv, lg[...] * mask, grad_three, mask, width)
    branch = grad_pooled.astype(BF16)
    s_two[...] = jnp.zeros_like(s_two)

    def backward(at):
        grad_active = mm_nt(branch, s_wn[at, :])
        grad_hidden = (grad_active * slope_ref[:, at]).astype(BF16)
        s_two[...] += mm_nt(grad_hidden, s_ww[:, at])

    hidden.each(backward)
    mid_hat, mid_inv = normed(middle_ref[...], mask, width)
    grad_two = s_two[...] * mask
    grad_middle = grad_pooled + norm_back(mid_hat, mid_inv, fg[...] * mask, grad_two, mask, width)
    rows_mid_ref[...] = grad_middle
    attention = grad_middle.astype(BF16)
    get_wo.wait()
    grad_mixed = (mm_nt(attention, s_wo[...]) * mask).astype(BF16)
    repeat = repeat_rows(rows, pairs)
    heads = head_mask(rows, pairs, full_width)
    wide = jnp.where(heads, mm(repeat, grad_mixed), 0.0)
    get_triple.wait()
    along = mm_nt(wide.astype(BF16), s_triple[2])
    values_low = along.astype(BF16)
    values_ref[...] = values_low
    offset = jnp.sum(along * shift, axis=1, keepdims=True) + jnp.sum(
        wide * triple_bias[0, 1:2, :], axis=1, keepdims=True
    )
    get_hat.wait()
    get_probs.wait()
    grad_probs = mm_nt((along * gain).astype(BF16), s_hat[...]) + offset
    probs = s_probs[...]
    inner = jnp.sum(grad_probs * probs, axis=1, keepdims=True)
    back = (probs * (grad_probs - inner)).astype(BF16)
    back_ref[...] = back
    spread = mm(back, s_hat[...])
    total = jnp.sum(back.astype(F32), axis=1, keepdims=True)
    means = (spread * gain + total * shift).astype(BF16)
    query_wide = mm(means, s_triple[1]) * 0.125
    grad_query = mm_tn(repeat, jnp.where(heads, query_wide, 0.0).astype(BF16)).astype(BF16)
    queries_ref[...] = grad_query
    rows_one = mm_nt(grad_query, s_triple[0]) * mask
    rows_one_ref[...] = rows_one
    values_wide = values_low.astype(F32)
    keys_wide = keys_ref[...].astype(F32)
    prob_total = jnp.sum(probs.astype(BF16).astype(F32), axis=1, keepdims=True)
    gain_sum = (
        sums_of(values_wide * spread_ref[...])
        + sums_of(keys_wide * spread)
        + sums_of(rows_one * hat_rows_ref[...].astype(F32))
    ) * mask
    shift_sum = (
        sums_of(values_wide * prob_total) + sums_of(keys_wide * total) + sums_of(rows_one)
    ) * mask
    s_turn[rows:, :] = jnp.zeros((s_turn.shape[0] - rows, full_width), F32)
    s_turn[0:rows, :] = means.astype(F32)
    slot = rows
    for vector in (gain_sum, shift_sum):
        for _ in range(3):
            low = vector.astype(BF16).astype(F32)
            s_turn[slot : slot + 1, :] = low
            vector = vector - low
            slot += 1
    lanes = s_turn.shape[0]
    late_ref[:, 0:lanes] = s_turn[...].T.astype(BF16)
    if late_ref.shape[1] > lanes:
        turned = grad_query.astype(F32).T
        slab = s_slab.shape[0]
        s_slab[...] = jnp.zeros_like(s_slab)
        for place in range(full_width // slab):
            down = slice(place * slab, (place + 1) * slab)
            s_slab[:, place * pairs : (place + 1) * pairs] = turned[down, :]
        slab_low = s_slab[...].astype(BF16)
        for place in range(full_width // slab):
            late_ref[place * slab : (place + 1) * slab, lanes:] = slab_low


def rows_kernel(dims, *refs):
    pairs, tokens, full_width, full_hidden, slice_width, slice_hidden, stages, pieces = dims
    early_hbm = refs[:pieces]
    (
        ends_ref,
        hat_hbm,
        inv_hbm,
        probs_hbm,
        back_ref,
        value_factors_ref,
        keys_ref,
        rows_one_ref,
        rows_mid_ref,
        grad_hbm,
        ag,
        ab,
        triple_hbm,
        triple_bias,
        wo_hbm,
        bo,
        fg,
        fb,
        ww_hbm,
        bw,
        wn_hbm,
        lg,
        lb,
        we_hbm,
        out_hbm,
        ones_ref,
        queries_ref,
        values_ref,
        embed_ref,
        narrow_ref,
        widen_ref,
        mixer_ref,
        final_gain_ref,
        final_bias_ref,
        feed_gain_ref,
        feed_bias_ref,
        narrow_bias_ref,
        mixer_bias_ref,
        value_bias_ref,
        widen_bias_ref,
        s_triple,
        s_wo,
        s_ww,
        s_wn,
        s_we,
        s_vectors,
        s_hat,
        s_inv,
        s_probs,
        s_left,
        s_right,
        s_early,
        grad_ref,
        s_out,
        s_total,
        s_active,
        s_hidden,
        sems,
        hidden_sems,
        out_sems,
    ) = refs[pieces:]
    all_pairs = grad_ref.shape[0]
    block = block_rows(all_pairs)
    here = lax.axis_index("dp")
    is_text, width, mask = tower_sizes(full_width, full_hidden)
    get_probs = fetch(probs_hbm, s_probs, sems.at[3])
    get_hat = fetch(hat_hbm, s_hat, sems.at[4])
    get_inv = fetch(inv_hbm, s_inv, sems.at[5])
    get_grad = fetch(grad_hbm, grad_ref, sems.at[6])
    height = s_early.shape[0] // pieces
    early = [s_early.at[pl.ds(place * height, height), :] for place in range(pieces)]
    get_early = [fetch(early_hbm[place], early[place], sems.at[7 + place]) for place in range(pieces)]
    get_wo = fetch(wo_hbm.at[0], s_wo, sems.at[1])
    get_we = fetch(we_hbm.at[0], s_we, sems.at[2])
    hidden = Hidden(ww_hbm, wn_hbm, s_ww, s_wn, hidden_sems, full_hidden // CHUNK)
    hidden.start((0, 1))
    get_triple = fetch(triple_hbm.at[0, 0], s_triple, sems.at[0])
    rows = full_width // HEAD * pairs
    token_gain = ag[...] * mask
    s_left[rows : 2 * rows, :] = back_ref[...]
    s_right[0:rows, :] = value_factors_ref[...]
    s_right[rows : 2 * rows, :] = keys_ref[...]
    spots = pooled_spots(ends_ref, is_text, pairs, 3)
    s_left[2 * rows :, :] = one_hot(iota((3 * pairs, tokens), 1).astype(F32) == spots)
    s_right[2 * rows :, :] = three_parts(rows_one_ref[...])
    middle_parts = three_parts(rows_mid_ref[...])
    ones = one_hot(iota((full_width, 128), 0).astype(F32) < width)
    get_probs.wait()
    s_left[0:rows, :] = s_probs[...].astype(BF16)
    get_hat.wait()
    get_inv.wait()

    def put(at, count):
        spot = pl.ds(at, count)
        return pltpu.make_async_copy(
            s_out.at[spot, :], out_hbm.at[0, spot, :], out_sems.at[at // NORM_ROWS]
        )

    def norm_rows(at, count):
        spot = pl.ds(at, count)
        upward = mm_tn(s_left[:, spot], s_right[...])
        hat = s_hat[spot, :].astype(F32)
        scaled = upward * token_gain
        mean = mm(scaled.astype(BF16), ones) / width
        along = mm((scaled * hat).astype(BF16), ones) / width
        s_out[spot, :] = across(s_inv[spot, :], full_width) * (
            scaled - (across(mean, full_width) + hat * across(along, full_width)) * mask
        ) + mm_tn(s_left[2 * rows :, spot], middle_parts)
        put(at, count).start()

    over_tokens(tokens, NORM_ROWS, norm_rows)
    for ref in (embed_ref, narrow_ref, widen_ref, mixer_ref, widen_bias_ref, s_vectors):
        ref[...] = jnp.zeros_like(ref)
    lane = iota((full_width, slice_width), 0)
    pick = one_hot(
        (lane == here * slice_width + iota((full_width, slice_width), 1))
        & (lane.astype(F32) < width)
    )
    hidden_width = jnp.where(is_text, MLP_TXT, full_hidden)
    gain, shift = lg[...] * mask, lb[...] * mask
    feed_gain = fg[...] * mask
    get_wo.wait()
    get_we.wait()
    get_grad.wait()
    for copy in get_early:
        copy.wait()

    def part(index):
        at = pl.multiple_of(index * block, block)
        here_rows = pl.ds(at, block)
        arrived = in_order(early, stages, pairs, block, at)
        mixed = arrived[:, 0:full_width]
        stream_rows = arrived[:, full_width : 2 * full_width].astype(F32)
        out_hat = arrived[:, 2 * full_width : 3 * full_width].astype(F32)
        out_inv = jnp.sum(arrived[:, 3 * full_width :].astype(F32), axis=1, keepdims=True)
        three = (out_hat * gain + shift).astype(BF16)
        grad_embed = embed_back(mm(three, s_we[...]), grad_ref[here_rows, :])
        embed_ref[0] += mm_tn(mm(three, pick).astype(BF16), grad_embed)
        grad_three = mm_nt(grad_embed, s_we[...])
        s_vectors[0:1, :] += sums_of(grad_three * out_hat)
        s_vectors[1:2, :] += sums_of(grad_three)
        grad_pooled = norm_back(out_hat, out_inv, gain, grad_three, mask, width)
        branch = grad_pooled.astype(BF16)
        s_vectors[2:3, :] += sums_of(branch.astype(F32))
        middle = stream_rows + mm(mixed, s_wo[...]) + bo[...]
        mid_hat, mid_inv = normed(middle, mask, width)
        two = ((mid_hat * fg[...] + fb[...]) * mask).astype(BF16)
        s_total[...] = jnp.zeros_like(s_total)
        s_active[...] = jnp.zeros_like(s_active)
        s_hidden[...] = jnp.zeros_like(s_hidden)

        def through(chunk, carry):
            first = pl.multiple_of(chunk * CHUNK, CHUNK)
            lanes = pl.ds(first, CHUNK)
            if all_pairs == block:
                hidden.wait(chunk)
            pre = mm(two, s_ww[:, lanes]) + bw[:, lanes]
            gate = sigmoid(1.702 * pre)
            active = pre * gate
            there = (first + iota((1, CHUNK), 1) < hidden_width).astype(F32)
            slope = (gate + 1.702 * active * (1.0 - gate)) * there
            grad_hidden = (mm_nt(branch, s_wn[lanes, :]) * slope).astype(BF16)
            s_total[...] += mm_nt(grad_hidden, s_ww[:, lanes])
            row = first + iota((CHUNK, slice_hidden), 0)
            chosen = one_hot(
                (row == here * slice_hidden + iota((CHUNK, slice_hidden), 1))
                & (row < hidden_width)
            )
            s_active[...] += mm(active.astype(BF16), chosen)
            s_hidden[...] += mm(grad_hidden, chosen)
            return carry

        lax.fori_loop(0, full_hidden // CHUNK, through, 0)
        grad_two, active_slice, hidden_slice = s_total[...], s_active[...], s_hidden[...]
        narrow_ref[0] += mm_tn(active_slice.astype(BF16), branch)
        widen_ref[0] += mm_tn(hidden_slice.astype(BF16), two)
        widen_bias_ref[...] += sums_of(hidden_slice)
        s_vectors[3:4, :] += sums_of(grad_two * mid_hat)
        s_vectors[4:5, :] += sums_of(grad_two)
        grad_middle = grad_pooled + norm_back(mid_hat, mid_inv, feed_gain, grad_two, mask, width)
        attention = grad_middle.astype(BF16)
        s_vectors[5:6, :] += sums_of(attention.astype(F32))
        mixer_ref[0] += mm_tn(mm(mixed, pick).astype(BF16), attention)
        grad_mixed = (mm_nt(attention, s_wo[...]) * mask).astype(BF16)
        values_ref[here_rows, :] = grad_mixed
        s_vectors[6:7, :] += sums_of(grad_mixed.astype(F32))
        rows_hat, _ = normed(stream_rows, mask, width)
        one = ((rows_hat * ag[...] + ab[...]) * mask).astype(BF16)
        ones_ref[here_rows, :] = mm(one, pick).astype(BF16)
        if all_pairs == block:
            get_triple.wait()
        query = (mm(one, s_triple[...]) + triple_bias[0, 0:1, :]) * mask
        queries_ref[here_rows, :] = query.astype(BF16)

    if all_pairs != block:
        get_triple.wait()
        for chunk in range(full_hidden // CHUNK):
            hidden.wait(chunk)
    over_blocks(all_pairs // block, part)
    over_tokens(tokens, NORM_ROWS, lambda at, count: put(at, count).wait())
    vectors = dot_dims(s_vectors[...], pick.astype(F32), 1, 0, lax.Precision.HIGHEST)
    for slot, ref in enumerate(
        (
            final_gain_ref,
            final_bias_ref,
            narrow_bias_ref,
            feed_gain_ref,
            feed_bias_ref,
            mixer_bias_ref,
            value_bias_ref,
        )
    ):
        ref[...] = vectors[slot : slot + 1, :]


def last_kernel(dims, *refs):
    pairs, full_width, full_hidden, slice_width, stages, pieces = dims
    arrived = refs[:pieces]
    (
        late_ref,
        means_ref,
        ones_ref,
        queries_ref,
        values_ref,
        value_bias_ref,
        triple_ref,
        gain_ref,
        shift_ref,
        bias_ref,
        s_keys,
        s_means,
        s_turned,
        s_late,
        s_sums,
    ) = refs[pieces:]
    here = lax.axis_index("dp")
    count = late_ref.shape[0]
    lanes = means_ref.shape[2]
    heads = full_width // HEAD
    rows = heads * pairs
    all_pairs = queries_ref.shape[0]
    s_late[...] = jnp.zeros_like(s_late)
    if not arrived:
        for source in range(count):
            now = late_ref[source]
            s_late[...] += now[:, 0:lanes].astype(F32)
            means = means_ref[source]
            across_now = slice(source * pairs, (source + 1) * pairs)
            for head in range(heads):
                down = slice(head * slice_width, (head + 1) * slice_width)
                lane = slice(head * pairs, (head + 1) * pairs)
                s_keys[down, across_now] = now[:, lane]
                s_means[down, across_now] = means[:, lane]
            for slab in range(count):
                down = slice(slab * slice_width, (slab + 1) * slice_width)
                first = lanes + slab * pairs
                s_turned[down, across_now] = now[:, first : first + pairs]
        left = iota((slice_width, 2 * HEAD), 1) < HEAD
        for two in range(heads // 2):
            down = slice(two * 2 * slice_width, (two + 1) * 2 * slice_width)
            lane = slice(two * 2 * HEAD, (two + 1) * 2 * HEAD)
            both = mm(s_keys[down, :], queries_ref[:, lane]) * 0.125
            triple_ref[0, 1, :, lane] = jnp.where(left, both[0:slice_width], both[slice_width:])
            both = mm(s_means[down, :], values_ref[:, lane])
            triple_ref[0, 2, :, lane] = jnp.where(left, both[0:slice_width], both[slice_width:])
        triple_ref[0, 0] = mm(s_turned[...], ones_ref[...]).T
        mine = s_turned[pl.ds(pl.multiple_of(here * slice_width, slice_width), slice_width), :]
        sums = mm_nt(jnp.ones((8, all_pairs), BF16), mine)
    else:
        block = block_rows(all_pairs)
        triple_ref[...] = jnp.zeros_like(triple_ref)
        s_sums[...] = jnp.zeros_like(s_sums)

        def part(index):
            at = pl.multiple_of(index * block, block)
            grad_query = in_order(arrived, stages, pairs, block, at)
            triple_ref[0, 0] += mm_tn(ones_ref[pl.ds(at, block), :], grad_query)
            s_sums[0:1, :] += sums_of(grad_query.astype(F32))

        over_blocks(all_pairs // block, part)
        head = head_mask(lanes, pairs, full_width)

        def one(source, carry):
            now = late_ref[source]
            s_late[...] += now.astype(F32)
            row = iota((lanes, all_pairs), 0)
            column = iota((lanes, all_pairs), 1)
            repeat = one_hot((column == source * pairs + lax.rem(row, pairs)) & (row < rows))
            means = means_ref[source]
            for which, left, origin in ((1, now, queries_ref), (2, means, values_ref)):
                wide = jnp.where(head, mm(repeat, origin[...]), 0.0).astype(BF16)
                triple_ref[0, which] += mm(left, wide)
            return carry

        lax.fori_loop(0, count, one, 0)
        triple_ref[0, 1] = triple_ref[0, 1] * 0.125
        pick = (
            iota((full_width, slice_width), 0)
            == here * slice_width + iota((full_width, slice_width), 1)
        ).astype(F32)
        sums = dot_dims(s_sums[...], pick, 1, 0, lax.Precision.HIGHEST)
    lane = iota((8, lanes), 1)
    row = iota((8, lanes), 0)
    slot = rows + row * 3
    chosen = ((lane >= slot) & (lane < slot + 3) & (row < 2)).astype(F32)
    from_late = dot_dims(chosen, s_late[...], 1, 1, lax.Precision.HIGHEST)
    gain_ref[...] = from_late[0:1, :]
    shift_ref[...] = from_late[1:2, :]
    bias_ref[0, 0:1, :] = sums[0:1, :]
    bias_ref[0, 1:2, :] = value_bias_ref[...]


def stages_of(count):
    bits = count.bit_length() - 1
    stages = []
    while bits > 0:
        take = 2 if bits >= 2 else 1
        bits -= take
        stages.append((bits, take))
    return tuple(stages)


def exchange(block, axis, stage):
    count = lax.axis_size(axis)
    shift, bits = stage
    parts = [block]
    for apart in range(1, 1 << bits):
        route = [(low, low ^ (apart << shift)) for low in range(count)]
        parts.append(lax.ppermute(block, axis, route))
    return parts


def call(
    kernel, ins, outs, scratch, in_hbm=(), out_hbm=(), cost=None, kept=(), limit=VMEM_LIMIT
):
    vmem = pl.BlockSpec(memory_space=pltpu.VMEM)
    anywhere = pl.BlockSpec(memory_space=pl.ANY)
    specs = [anywhere if index in in_hbm else vmem for index in range(len(ins))]
    out_specs = [anywhere if index in out_hbm else vmem for index in range(len(outs))]
    if kept:
        ins = [
            pltpu.with_memory_space_constraint(
                array, pltpu.VMEM if index in kept else pltpu.HBM
            )
            for index, array in enumerate(ins)
        ]
    flops, moved = cost
    return pl.pallas_call(
        kernel,
        out_shape=[jax.ShapeDtypeStruct(shape, kind) for shape, kind in outs],
        in_specs=specs,
        out_specs=out_specs,
        scratch_shapes=scratch,
        compiler_params=pltpu.CompilerParams(vmem_limit_bytes=limit),
        cost_estimate=pl.CostEstimate(flops=flops, bytes_accessed=moved, transcendentals=0),
    )(*ins)


def body(
    block_input,
    segments,
    caption_ends,
    pair_flags,
    attention_gain,
    attention_bias,
    triple_weight,
    triple_bias,
    mixer_weight,
    mixer_bias,
    feed_gain,
    feed_bias,
    widen_weight,
    widen_bias,
    narrow_weight,
    narrow_bias,
    final_gain,
    final_bias,
    embed_weight,
    logit_scale,
    loss_scale,
):
    tokens, width = block_input.shape[1:]
    hidden = widen_weight.shape[2]
    emb = embed_weight.shape[2]
    pairs = caption_ends.shape[0]
    count = lax.axis_size("dp")
    all_pairs = pair_flags.shape[0]
    heads = width // HEAD
    rows = heads * pairs
    lanes = -(-(rows + 12) // 128) * 128
    slice_width = width // count
    slice_hidden = hidden // count
    stages = stages_of(count)
    compact = count <= 16 and slice_width % 16 == 0
    slab_lanes = -(-all_pairs // 128) * 128
    ends = caption_ends.reshape(1, pairs)
    dma = pltpu.SemaphoreType.DMA
    weights_scratch = [
        pltpu.VMEM((3, width, width), BF16),
        pltpu.VMEM((width, width), BF16),
        pltpu.VMEM((width, hidden), BF16),
        pltpu.VMEM((hidden, width), BF16),
        pltpu.VMEM((width, emb), BF16),
    ]
    dims = (pairs, tokens, width, hidden)
    chunk_count = hidden // CHUNK
    (
        unit,
        early,
        hat,
        invert,
        probs,
        query,
        embedded,
        pooled,
        middle,
        slope,
    ) = call(
        partial(attend_kernel, dims),
        (
            ends,
            block_input,
            attention_gain,
            attention_bias,
            triple_weight,
            triple_bias,
            mixer_weight,
            mixer_bias,
            feed_gain,
            feed_bias,
            widen_weight,
            widen_bias,
            narrow_weight,
            narrow_bias,
            final_gain,
            final_bias,
            embed_weight,
        ),
        [
            ((pairs, emb), BF16),
            ((pairs, 3 * width + 128), BF16),
            ((tokens, width), BF16),
            ((tokens, 128), F32),
            ((rows, tokens), F32),
            ((pairs, width), BF16),
            ((pairs, emb), F32),
            ((pairs, width), F32),
            ((pairs, width), F32),
            ((pairs, hidden), F32),
        ],
        [
            pltpu.VMEM((tokens, width), BF16),
            pltpu.VMEM((tokens, width), BF16),
            pltpu.VMEM((tokens, width), BF16),
            pltpu.VMEM((tokens, 128), F32),
            pltpu.VMEM((rows, tokens), F32),
            pltpu.VMEM((tokens, width), BF16),
            pltpu.VMEM((tokens, width), BF16),
        ]
        + weights_scratch
        + [
            pltpu.VMEM((rows, tokens), BF16),
            dma((7,)),
            dma((2, chunk_count)),
        ],
        in_hbm=(1, 4, 6, 10, 12, 16),
        out_hbm=(2, 3, 4),
        cost=(10**9, 20 * 10**6),
    )
    turned, spread, keys, hat_rows = call(
        partial(means_kernel, dims),
        (ends, attention_gain, attention_bias, hat, probs, query, triple_weight),
        [
            ((width, lanes), BF16),
            ((rows, width), F32),
            ((rows, width), BF16),
            ((pairs, width), BF16),
        ],
        [
            pltpu.VMEM((width, width), BF16),
            pltpu.VMEM((lanes, width), F32),
            dma((1,)),
        ],
        in_hbm=(6,),
        cost=(10**9, 5 * 10**6),
    )
    early_rows, own_rel = early, unit
    flags = pair_flags.reshape(1, all_pairs)
    for index, stage in enumerate(stages):
        own_parts = exchange(own_rel, "dp", stage)
        if index + 1 < len(stages):
            own_parts, early_rows, turned, spread, keys, hat_rows, flags = lax.optimization_barrier(
                (own_parts, early_rows, turned, spread, keys, hat_rows, flags)
            )
            early_rows = jnp.concatenate(exchange(early_rows, "dp", stage), axis=0)
        own_rel = jnp.concatenate(own_parts, axis=0)
    means_all = lax.all_to_all(turned, "dp", 0, 0, tiled=True).reshape(count, slice_width, lanes)
    other_rel = lax.ppermute(own_rel, "tower", [(0, 1), (1, 0)])
    early_pieces = exchange(early_rows, "dp", stages[-1])
    (
        loss,
        hits,
        scale,
        grad_all,
        late,
        queries,
        back,
        values,
        rows_one,
        rows_mid,
    ) = call(
        partial(loss_kernel, dims + (stages,)),
        (
            own_rel,
            other_rel,
            flags,
            logit_scale.reshape(1, 1),
            loss_scale.reshape(1, 1),
            attention_gain,
            attention_bias,
            triple_weight,
            triple_bias,
            mixer_weight,
            feed_gain,
            widen_weight,
            narrow_weight,
            final_gain,
            embed_weight,
            hat,
            probs,
            spread,
            keys,
            embedded,
            pooled,
            middle,
            slope,
            hat_rows,
        ),
        [
            ((1, 1), F32),
            ((1, 1), F32),
            ((1, 1), F32),
            ((all_pairs, emb), F32),
            ((width, lanes + (slab_lanes if compact else 0)), BF16),
            ((pairs, width), BF16),
            ((rows, tokens), BF16),
            ((rows, width), BF16),
            ((pairs, width), F32),
            ((pairs, width), F32),
        ],
        [pltpu.VMEM((all_pairs, emb), BF16), pltpu.VMEM((all_pairs, emb), BF16)]
        + weights_scratch
        + [
            pltpu.VMEM((tokens, width), BF16),
            pltpu.VMEM((rows, tokens), F32),
            pltpu.VMEM((pairs, emb), F32),
            pltpu.VMEM((pairs, width), F32),
            pltpu.VMEM((lanes, width), F32),
            pltpu.VMEM((slice_width, slab_lanes), F32),
            dma((5,)),
            dma((2, chunk_count)),
        ],
        in_hbm=(7, 9, 11, 12, 14, 15, 16),
        cost=(10**9, 20 * 10**6),
    )
    early_pieces, late, queries = lax.optimization_barrier((early_pieces, late, queries))
    late_all = lax.all_to_all(late, "dp", 0, 0, tiled=True)
    late_all = late_all.reshape(count, slice_width, late.shape[1])
    late_pieces = []
    if not compact:
        late_pieces = [queries]
        for stage in stages:
            late_pieces = exchange(jnp.concatenate(late_pieces, axis=0), "dp", stage)
    ahead = len(early_pieces)
    vector = ((1, slice_width), F32)
    (
        block_grad,
        ones,
        query_rows,
        value_rows,
        grad_embed,
        grad_narrow,
        grad_widen,
        grad_mixer,
        grad_final_gain,
        grad_final_bias,
        grad_feed_gain,
        grad_feed_bias,
        grad_narrow_bias,
        grad_mixer_bias,
        grad_value_bias,
        grad_widen_bias,
    ) = call(
        partial(
            rows_kernel,
            (pairs, tokens, width, hidden, slice_width, slice_hidden, stages, ahead),
        ),
        tuple(early_pieces)
        + (
            ends,
            hat,
            invert,
            probs,
            back,
            values,
            keys,
            rows_one,
            rows_mid,
            grad_all,
            attention_gain,
            attention_bias,
            triple_weight,
            triple_bias,
            mixer_weight,
            mixer_bias,
            feed_gain,
            feed_bias,
            widen_weight,
            widen_bias,
            narrow_weight,
            final_gain,
            final_bias,
            embed_weight,
        ),
        [
            ((1, tokens, width), F32),
            ((all_pairs, slice_width), BF16),
            ((all_pairs, width), BF16),
            ((all_pairs, width), BF16),
            ((1, slice_width, emb), F32),
            ((1, slice_hidden, width), F32),
            ((1, slice_hidden, width), F32),
            ((1, slice_width, width), F32),
        ]
        + [vector] * 7
        + [((1, slice_hidden), F32)],
        [pltpu.VMEM((width, width), BF16)]
        + weights_scratch[1:]
        + [
            pltpu.VMEM((8, width), F32),
            pltpu.VMEM((tokens, width), BF16),
            pltpu.VMEM((tokens, 128), F32),
            pltpu.VMEM((rows, tokens), F32),
            pltpu.VMEM((2 * rows + 3 * pairs, tokens), BF16),
            pltpu.VMEM((2 * rows + 3 * pairs, width), BF16),
            pltpu.VMEM((all_pairs, 3 * width + 128), BF16),
            pltpu.VMEM((all_pairs, emb), F32),
            pltpu.VMEM((tokens, width), F32),
            pltpu.VMEM((block_rows(all_pairs), width), F32),
            pltpu.VMEM((block_rows(all_pairs), slice_hidden), F32),
            pltpu.VMEM((block_rows(all_pairs), slice_hidden), F32),
            dma((7 + ahead,)),
            dma((2, chunk_count)),
            dma((-(-tokens // NORM_ROWS),)),
        ],
        in_hbm=tuple(range(ahead)) + tuple(ahead + index for index in (1, 2, 3, 9, 12, 14, 18, 20, 23)),
        out_hbm=(0,),
        cost=(3 * 10**9, 10 * 10**6),
    )
    grad_triple, grad_gain, grad_bias, grad_triple_bias = call(
        partial(last_kernel, (pairs, width, hidden, slice_width, stages, len(late_pieces))),
        tuple(late_pieces)
        + (late_all, means_all, ones, query_rows, value_rows, grad_value_bias),
        [
            ((1, 3, slice_width, width), F32),
            vector,
            vector,
            ((1, 2, slice_width), F32),
        ],
        [
            pltpu.VMEM((width // HEAD * slice_width, all_pairs), BF16),
            pltpu.VMEM((width // HEAD * slice_width, all_pairs), BF16),
            pltpu.VMEM((width, all_pairs), BF16),
            pltpu.VMEM((slice_width, lanes), F32),
            pltpu.VMEM((8, width), F32),
        ],
        cost=(10**9, 10 * 10**6),
        kept=(0,) if compact else (),
        limit=32 * 1024 * 1024 if compact else VMEM_LIMIT,
    )
    return (
        loss[0, 0],
        hits[0, 0],
        block_grad,
        grad_gain,
        grad_bias,
        grad_triple,
        grad_triple_bias,
        grad_mixer,
        grad_mixer_bias,
        grad_feed_gain,
        grad_feed_bias,
        jnp.swapaxes(grad_widen, 1, 2),
        grad_widen_bias,
        grad_narrow,
        grad_narrow_bias,
        grad_final_gain,
        grad_final_bias,
        grad_embed,
        scale[0, 0],
    )


def solution(mesh):
    in_specs = (
        P("tower", "dp", None),
        P("dp", None),
        P("dp"),
        P(),
        P("tower", None),
        P("tower", None),
        P("tower", None, None, None),
        P("tower", None, None),
        P("tower", None, None),
        P("tower", None),
        P("tower", None),
        P("tower", None),
        P("tower", None, None),
        P("tower", None),
        P("tower", None, None),
        P("tower", None),
        P("tower", None),
        P("tower", None),
        P("tower", None, None),
        P(),
        P(),
    )
    out_specs = (
        P(),
        P(),
        P("tower", "dp", None),
        P("tower", "dp"),
        P("tower", "dp"),
        P("tower", None, "dp", None),
        P("tower", None, "dp"),
        P("tower", "dp", None),
        P("tower", "dp"),
        P("tower", "dp"),
        P("tower", "dp"),
        P("tower", None, "dp"),
        P("tower", "dp"),
        P("tower", "dp", None),
        P("tower", "dp"),
        P("tower", "dp"),
        P("tower", "dp"),
        P("tower", "dp", None),
        P(),
    )
    return jax.shard_map(body, mesh=mesh, in_specs=in_specs, out_specs=out_specs, check_vma=False)
```

```python
from functools import partial

import jax
import jax.numpy as jnp
from jax import lax
from jax.experimental import pallas as pl
from jax.experimental.pallas import tpu as pltpu
from jax.sharding import PartitionSpec as P

D_TXT = 512
MLP_TXT = 2048
HEAD = 64
IMG_TOK = 50
CTX = 77
F32 = jnp.float32
BF16 = jnp.bfloat16
VMEM_LIMIT = 62 * 1024 * 1024
CHUNK = 1024
NORM_ROWS = 272
PROJECT_ROWS = 1088


def dot_dims(left, right, left_dim, right_dim, precision=None):
    return lax.dot_general(
        left,
        right,
        (((left_dim,), (right_dim,)), ((), ())),
        preferred_element_type=F32,
        precision=precision,
    )


def mm(left, right):
    return dot_dims(left, right, 1, 0)


def mm_nt(left, right):
    return dot_dims(left, right, 1, 1)


def mm_tn(left, right):
    return dot_dims(left, right, 0, 0)


def iota(shape, dim):
    return lax.broadcasted_iota(jnp.int32, shape, dim)


def sigmoid(rows):
    return 1.0 / (1.0 + jnp.exp(-rows))


def one_hot(condition):
    return condition.astype(F32).astype(BF16)


def normed(rows, mask, width):
    mean = jnp.sum(rows * mask, axis=-1, keepdims=True) / width
    centre = (rows - mean) * mask
    invert = lax.rsqrt(jnp.sum(centre * centre, axis=-1, keepdims=True) / width + 1e-05)
    return centre * invert, invert


def norm_back(rows_hat, invert, gain, upward, mask, width):
    scaled = upward * gain
    mean = jnp.sum(scaled, axis=-1, keepdims=True) / width
    along = jnp.sum(scaled * rows_hat, axis=-1, keepdims=True) / width
    return invert * (scaled - mean * mask - rows_hat * along)


def sums_of(rows):
    return jnp.sum(rows, axis=0, keepdims=True)


def head_mask(rows, pairs, width):
    row = iota((rows, width), 0)
    first = lax.shift_right_logical(iota((rows, width), 1), 6) * pairs
    return (row >= first) & (row < first + pairs)


def repeat_rows(rows, pairs):
    row = iota((rows, pairs), 0)
    return one_hot(lax.rem(row, pairs) == iota((rows, pairs), 1))


def tower_sizes(full_width, full_hidden):
    is_text = lax.axis_index("tower") != 0
    width = jnp.where(is_text, D_TXT, full_width)
    mask = (iota((1, full_width), 1) < width).astype(F32)
    return is_text, width.astype(F32), mask


def fetch(source, target, semaphore):
    copy = pltpu.make_async_copy(source, target, semaphore)
    copy.start()
    return copy


def three_parts(rows):
    parts = []
    for _ in range(3):
        part = rows.astype(BF16).astype(F32)
        parts.append(part)
        rows = rows - part
    return jnp.concatenate(parts, axis=0).astype(BF16)


def over_tokens(tokens, size, step):
    for at in range(0, tokens, size):
        step(at, min(size, tokens - at))


def across(lane_sums, full_width):
    return jnp.concatenate([lane_sums] * (full_width // 128), axis=1)


def pooled_spots(ends_ref, is_text, pairs, copies):
    pair = lax.rem(iota((copies * pairs, pairs), 0), pairs)
    ends = jnp.where(pair == iota((copies * pairs, pairs), 1), ends_ref[...], 0).astype(F32)
    ends = jnp.sum(ends, axis=1, keepdims=True)
    firsts = (lax.rem(iota((copies * pairs, 1), 0), pairs) * IMG_TOK).astype(F32)
    return jnp.where(is_text, ends, firsts)


def embed_back(embedded, grad_unit):
    inv_norm = lax.rsqrt(jnp.sum(embedded * embedded, axis=-1, keepdims=True) + 1e-06)
    along = jnp.sum(embedded * grad_unit, axis=-1, keepdims=True)
    return (inv_norm * grad_unit - inv_norm * inv_norm * inv_norm * embedded * along).astype(BF16)


class Hidden:
    def __init__(self, widen_hbm, narrow_hbm, s_widen, s_narrow, sems, chunks):
        self.pairs = (
            (lambda at: widen_hbm.at[0, :, pl.ds(at, CHUNK)], lambda at: s_widen.at[:, pl.ds(at, CHUNK)]),
            (lambda at: narrow_hbm.at[0, pl.ds(at, CHUNK), :], lambda at: s_narrow.at[pl.ds(at, CHUNK), :]),
        )
        self.sems = sems
        self.chunks = chunks

    def copy(self, which, chunk):
        source, target = self.pairs[which]
        at = chunk * CHUNK
        if not isinstance(at, int):
            at = pl.multiple_of(at, CHUNK)
        return pltpu.make_async_copy(source(at), target(at), self.sems.at[which, chunk])

    def start(self, order):
        for chunk in range(self.chunks):
            for which in order:
                self.copy(which, chunk).start()

    def wait(self, chunk):
        self.copy(0, chunk).wait()
        self.copy(1, chunk).wait()

    def each(self, step):
        for chunk in range(self.chunks):
            self.wait(chunk)
            step(slice(chunk * CHUNK, (chunk + 1) * CHUNK))


def attend_kernel(
    dims,
    ends_ref,
    x_hbm,
    ag,
    ab,
    triple_hbm,
    triple_bias,
    wo_hbm,
    bo,
    fg,
    fb,
    ww_hbm,
    bw,
    wn_hbm,
    bn,
    lg,
    lb,
    we_hbm,
    unit_ref,
    early_ref,
    hat_hbm,
    inv_hbm,
    probs_hbm,
    query_ref,
    embedded_ref,
    pooled_ref,
    middle_ref,
    slope_ref,
    s_x,
    s_one,
    s_hat,
    s_inv,
    s_probs,
    s_key,
    s_value,
    s_triple,
    s_wo,
    s_ww,
    s_wn,
    s_we,
    s_low,
    sems,
    hidden_sems,
):
    pairs, tokens, full_width, full_hidden = dims
    is_text, width, mask = tower_sizes(full_width, full_hidden)
    rows = full_width // HEAD * pairs
    get_x = fetch(x_hbm.at[0], s_x, sems.at[0])
    get_triple = fetch(triple_hbm.at[0], s_triple, sems.at[1])
    gain, shift = ag[...] * mask, ab[...] * mask
    ones = one_hot((iota((full_width, 128), 0)).astype(F32) < width)
    hidden = Hidden(ww_hbm, wn_hbm, s_ww, s_wn, hidden_sems, full_hidden // CHUNK)
    get_x.wait()
    get_wo = fetch(wo_hbm.at[0], s_wo, sems.at[2])
    hidden.start((0, 1))
    get_we = fetch(we_hbm.at[0], s_we, sems.at[3])

    def norm_rows(at, count):
        here = pl.ds(at, count)
        low = s_x[here, :]
        mean = mm(low, ones) / width
        centre = low.astype(F32) - across(mean, full_width)
        square = centre * centre
        high = square.astype(BF16)
        low = (square - high.astype(F32)).astype(BF16)
        invert = lax.rsqrt((mm(high, ones) + mm(low, ones)) / width + 1e-05)
        hat = centre * across(invert, full_width)
        s_hat[here, :] = hat.astype(BF16)
        s_one[here, :] = (hat * gain + shift).astype(BF16)
        s_inv[here, :] = invert

    over_tokens(tokens, NORM_ROWS, norm_rows)
    put_hat = fetch(s_hat, hat_hbm, sems.at[4])
    put_inv = fetch(s_inv, inv_hbm, sems.at[5])
    pick = one_hot(iota((pairs, tokens), 1).astype(F32) == pooled_spots(ends_ref, is_text, pairs, 1))
    stream_rows = mm(pick, s_x[...]) * mask
    one = mm(pick, s_one[...]).astype(BF16)
    get_triple.wait()
    query = ((mm(one, s_triple[0]) + triple_bias[0, 0:1, :]) * (mask * 0.125)).astype(BF16)
    repeat = repeat_rows(rows, pairs)
    heads = head_mask(rows, pairs, full_width)
    wide = jnp.where(heads, mm(repeat, query), 0.0).astype(BF16)

    def project(at, count):
        here = pl.ds(at, count)
        s_key[here, :] = mm(s_one[here, :], s_triple[1]).astype(BF16)
        s_value[here, :] = (mm(s_one[here, :], s_triple[2]) + triple_bias[0, 1:2, :]).astype(BF16)

    over_tokens(tokens, PROJECT_ROWS, project)
    s_probs[...] = mm_nt(wide, s_key[...])
    last = pooled_spots(ends_ref, is_text, pairs, rows // pairs)
    pair = lax.rem(iota((rows, 1), 0), pairs)
    stops = jnp.where(
        pair - 1 == iota((rows, pairs), 1), ends_ref[...] + 1, 0
    ).astype(F32)
    first = jnp.where(is_text, jnp.sum(stops, axis=1, keepdims=True), last)
    last = jnp.where(is_text, last, last + (IMG_TOK - 1.0))
    step_rows = 48
    for at in range(0, rows, step_rows):
        here = slice(at, at + step_rows)
        place = iota((step_rows, tokens), 1).astype(F32)
        allowed = (place >= first[here]) & (place <= last[here])
        scores = jnp.where(allowed, s_probs[here, :], -1e30)
        powers = jnp.exp(scores - jnp.max(scores, axis=1, keepdims=True))
        probs = powers * (1.0 / jnp.sum(powers, axis=1, keepdims=True))
        s_low[here, :] = probs.astype(BF16)
    put_probs = fetch(s_low, probs_hbm, sems.at[6])
    mixed_wide = mm(s_low[...], s_value[...])
    mixed = mm_tn(repeat, jnp.where(heads, mixed_wide, 0.0).astype(BF16))
    mixed = (mixed * mask).astype(BF16)
    early_ref[:, 0:full_width] = mixed
    early_ref[:, full_width : 2 * full_width] = stream_rows.astype(BF16)
    get_wo.wait()
    middle = stream_rows + mm(mixed, s_wo[...]) + bo[...]
    middle_ref[...] = middle
    mid_hat, _ = normed(middle, mask, width)
    two = ((mid_hat * fg[...] + fb[...]) * mask).astype(BF16)
    pooled_ref[...] = middle + bn[...]
    hidden_width = jnp.where(is_text, MLP_TXT, full_hidden)
    hidden_mask = (iota((1, full_hidden), 1) < hidden_width).astype(F32)

    def forward(at):
        pre = mm(two, s_ww[:, at]) + bw[:, at]
        gate = sigmoid(1.702 * pre)
        active = pre * gate * hidden_mask[:, at]
        slope_ref[:, at] = (gate + 1.702 * active * (1.0 - gate)) * hidden_mask[:, at]
        pooled_ref[...] += mm(active.astype(BF16), s_wn[at, :])

    hidden.each(forward)
    out_hat, out_inv = normed(pooled_ref[...], mask, width)
    early_ref[:, 2 * full_width : 3 * full_width] = out_hat.astype(BF16)
    lane = iota((pairs, 128), 1)
    numbers = jnp.zeros((pairs, 128), F32)
    for place in range(3):
        part = out_inv.astype(BF16).astype(F32)
        numbers = jnp.where(lane == place, part, numbers)
        out_inv = out_inv - part
    early_ref[:, 3 * full_width :] = numbers.astype(BF16)
    three = ((out_hat * lg[...] + lb[...]) * mask).astype(BF16)
    get_we.wait()
    embedded = mm(three, s_we[...])
    embedded_ref[...] = embedded
    unit_ref[...] = (
        embedded * lax.rsqrt(jnp.sum(embedded * embedded, axis=-1, keepdims=True) + 1e-06)
    ).astype(BF16)
    query_ref[...] = query
    for copy in (put_hat, put_inv, put_probs):
        copy.wait()


def means_kernel(
    dims,
    ends_ref,
    ag,
    ab,
    hat_ref,
    probs_ref,
    query_ref,
    triple_hbm,
    turned_ref,
    spread_ref,
    keys_ref,
    hat_rows_ref,
    s_weight,
    s_turn,
    sems,
):
    pairs, tokens, full_width, full_hidden = dims
    is_text, width, mask = tower_sizes(full_width, full_hidden)
    get_weight = fetch(triple_hbm.at[0, 1], s_weight, sems.at[0])
    rows = probs_ref.shape[0]
    low = probs_ref[...]
    spread = mm(low, hat_ref[...])
    spread_ref[...] = spread.astype(BF16)
    total = jnp.sum(low.astype(F32), axis=1, keepdims=True)
    s_turn[rows:, :] = jnp.zeros((s_turn.shape[0] - rows, full_width), F32)
    s_turn[0:rows, :] = (spread * ag[...] + total * ab[...]) * mask
    turned_ref[...] = s_turn[...].T.astype(BF16)
    pick = one_hot(iota((pairs, tokens), 1).astype(F32) == pooled_spots(ends_ref, is_text, pairs, 1))
    hat_rows_ref[...] = mm(pick, hat_ref[...]).astype(BF16)
    wide = mm(repeat_rows(rows, pairs), query_ref[...])
    wide = jnp.where(head_mask(rows, pairs, full_width), wide, 0.0).astype(BF16)
    get_weight.wait()
    keys_ref[...] = mm_nt(wide, s_weight[...]).astype(BF16)


def in_order(pieces, stages, pairs, block, at):
    here = lax.axis_index("dp")
    row = at + iota((block, 1), 0)
    owner = lax.div(row, pairs)
    apart = lax.bitwise_xor(owner, here)
    place = jnp.zeros_like(owner)
    weight = 1
    for shift, bits in stages:
        digit = lax.bitwise_and(lax.shift_right_logical(apart, shift), (1 << bits) - 1)
        place = place + digit * weight
        weight = weight << bits
    column = place * pairs + row - owner * pairs
    total = None
    first = 0
    for piece in pieces:
        count = piece.shape[0]
        part = mm(one_hot(iota((block, count), 1) + first == column), piece[...])
        total = part if total is None else total + part
        first += count
    return total.astype(BF16)


def over_blocks(count, step):
    if count == 1:
        step(0)
    else:

        def one(index, carry):
            step(index)
            return carry

        lax.fori_loop(0, count, one, 0)


def block_rows(total):
    return 320 if total % 320 == 0 else total


def loss_kernel(
    dims,
    own_rel,
    other_rel,
    flags_ref,
    logit_scale,
    loss_scale,
    ag,
    ab,
    triple_hbm,
    triple_bias,
    wo_hbm,
    fg,
    ww_hbm,
    wn_hbm,
    lg,
    we_hbm,
    hat_hbm,
    probs_hbm,
    spread_ref,
    keys_ref,
    embedded_ref,
    pooled_ref,
    middle_ref,
    slope_ref,
    hat_rows_ref,
    loss_ref,
    hits_ref,
    scale_ref,
    grad_all_ref,
    late_ref,
    queries_ref,
    back_ref,
    values_ref,
    rows_one_ref,
    rows_mid_ref,
    s_own,
    s_other,
    s_triple,
    s_wo,
    s_ww,
    s_wn,
    s_we,
    s_hat,
    s_probs,
    s_rows,
    s_two,
    s_turn,
    s_slab,
    sems,
    hidden_sems,
):
    pairs, tokens, full_width, full_hidden, stages = dims
    all_pairs = own_rel.shape[0]
    block = block_rows(all_pairs)
    here = lax.axis_index("dp")
    is_text, width, mask = tower_sizes(full_width, full_hidden)
    rows = full_width // HEAD * pairs
    get_we = fetch(we_hbm.at[0], s_we, sems.at[0])
    hidden = Hidden(ww_hbm, wn_hbm, s_ww, s_wn, hidden_sems, full_hidden // CHUNK)
    hidden.start((1, 0))
    get_wo = fetch(wo_hbm.at[0], s_wo, sems.at[1])
    get_triple = fetch(triple_hbm.at[0], s_triple, sems.at[2])
    get_hat = fetch(hat_hbm, s_hat, sems.at[3])
    get_probs = fetch(probs_hbm, s_probs, sems.at[4])

    def place(index):
        at = pl.multiple_of(index * block, block)
        s_own[pl.ds(at, block), :] = in_order([own_rel], stages, pairs, block, at)
        s_other[pl.ds(at, block), :] = in_order([other_rel], stages, pairs, block, at)

    over_blocks(all_pairs // block, place)
    live = (flags_ref[...] > 0).astype(F32)
    live_pairs = jnp.sum(live, axis=1, keepdims=True)
    factor = jnp.exp(logit_scale[...])
    row_weight = loss_scale[...] / (2.0 * live_pairs)
    loss_ref[...] = jnp.zeros_like(loss_ref)
    hits_ref[...] = jnp.zeros_like(hits_ref)
    scale_ref[...] = jnp.zeros_like(scale_ref)
    grad_all_ref[...] = jnp.zeros_like(grad_all_ref)

    def part(index):
        at = pl.multiple_of(index * block, block)
        eye = at + iota((block, all_pairs), 0) == iota((block, all_pairs), 1)
        live_rows = jnp.sum(jnp.where(eye, live, 0.0), axis=1, keepdims=True)

        def one_way(left, right):
            logits = mm_nt(left, right) * factor
            masked = jnp.where(live > 0.5, logits, -1e30)
            peak = jnp.max(masked, axis=1, keepdims=True)
            powers = jnp.exp(masked - peak)
            total = jnp.sum(powers, axis=1, keepdims=True)
            log_total = peak + jnp.log(total)
            matched = jnp.sum(jnp.where(eye, logits, 0.0), axis=1, keepdims=True)
            gap = jnp.where(live_rows > 0.5, log_total - matched, 0.0)
            grads = (
                (powers / total - eye.astype(F32)) * (live_rows * row_weight)
            ).astype(BF16)
            loss = jnp.sum(live_rows * gap, axis=0, keepdims=True)
            hits = jnp.sum(live_rows * jnp.exp(-gap), axis=0, keepdims=True)
            scale = jnp.sum(
                jnp.sum(grads.astype(F32) * logits, axis=1, keepdims=True),
                axis=0,
                keepdims=True,
            )
            return grads, loss, hits, scale

        own = s_own[pl.ds(at, block), :]
        other = s_other[pl.ds(at, block), :]
        grads, loss_one, hits_one, scale_one = one_way(own, s_other[...])
        grad_all_ref[pl.ds(at, block), :] += factor * mm(grads, s_other[...])
        grads, loss_two, hits_two, scale_two = one_way(other, s_own[...])
        grad_all_ref[...] += factor * mm_tn(grads, other)
        loss_ref[...] += loss_one + loss_two
        hits_ref[...] += hits_one + hits_two
        scale_ref[...] += scale_one + scale_two

    over_blocks(all_pairs // block, part)
    loss_ref[...] = loss_ref[...] / (2.0 * live_pairs)
    hits_ref[...] = hits_ref[...] / (2.0 * live_pairs)

    for pair in range(pairs):
        s_rows[pair : pair + 1, :] = grad_all_ref[pl.ds(here * pairs + pair, 1), :]

    gain, shift = ag[...] * mask, ab[...] * mask
    grad_embed = embed_back(embedded_ref[...], s_rows[...])
    get_we.wait()
    grad_three = mm_nt(grad_embed, s_we[...])
    out_hat, out_inv = normed(pooled_ref[...], mask, width)
    grad_pooled = norm_back(out_hat, out_inv, lg[...] * mask, grad_three, mask, width)
    branch = grad_pooled.astype(BF16)
    s_two[...] = jnp.zeros_like(s_two)

    def backward(at):
        grad_active = mm_nt(branch, s_wn[at, :])
        grad_hidden = (grad_active * slope_ref[:, at]).astype(BF16)
        s_two[...] += mm_nt(grad_hidden, s_ww[:, at])

    hidden.each(backward)
    mid_hat, mid_inv = normed(middle_ref[...], mask, width)
    grad_two = s_two[...] * mask
    grad_middle = grad_pooled + norm_back(mid_hat, mid_inv, fg[...] * mask, grad_two, mask, width)
    rows_mid_ref[...] = grad_middle
    attention = grad_middle.astype(BF16)
    get_wo.wait()
    grad_mixed = (mm_nt(attention, s_wo[...]) * mask).astype(BF16)
    repeat = repeat_rows(rows, pairs)
    heads = head_mask(rows, pairs, full_width)
    wide = jnp.where(heads, mm(repeat, grad_mixed), 0.0)
    get_triple.wait()
    along = mm_nt(wide.astype(BF16), s_triple[2])
    values_low = along.astype(BF16)
    values_ref[...] = values_low
    offset = jnp.sum(along * shift, axis=1, keepdims=True) + jnp.sum(
        wide * triple_bias[0, 1:2, :], axis=1, keepdims=True
    )
    get_hat.wait()
    get_probs.wait()
    grad_probs = mm_nt((along * gain).astype(BF16), s_hat[...]) + offset
    probs = s_probs[...].astype(F32)
    prob_total = jnp.sum(probs, axis=1, keepdims=True)
    inner = jnp.sum(grad_probs * probs, axis=1, keepdims=True) / prob_total
    back = (probs * (grad_probs - inner)).astype(BF16)
    back_ref[...] = back
    spread = mm(back, s_hat[...])
    total = jnp.sum(back.astype(F32), axis=1, keepdims=True)
    means = (spread * gain + total * shift).astype(BF16)
    query_wide = mm(means, s_triple[1]) * 0.125
    grad_query = mm_tn(repeat, jnp.where(heads, query_wide, 0.0).astype(BF16)).astype(BF16)
    queries_ref[...] = grad_query
    rows_one = mm_nt(grad_query, s_triple[0]) * mask
    rows_one_ref[...] = rows_one
    values_wide = values_low.astype(F32)
    keys_wide = keys_ref[...].astype(F32)
    gain_sum = (
        sums_of(values_wide * spread_ref[...].astype(F32))
        + sums_of(keys_wide * spread)
        + sums_of(rows_one * hat_rows_ref[...].astype(F32))
    ) * mask
    shift_sum = (
        sums_of(values_wide * prob_total) + sums_of(keys_wide * total) + sums_of(rows_one)
    ) * mask
    s_turn[rows:, :] = jnp.zeros((s_turn.shape[0] - rows, full_width), F32)
    s_turn[0:rows, :] = means.astype(F32)
    slot = rows
    for vector in (gain_sum, shift_sum):
        for _ in range(3):
            low = vector.astype(BF16).astype(F32)
            s_turn[slot : slot + 1, :] = low
            vector = vector - low
            slot += 1
    lanes = s_turn.shape[0]
    late_ref[:, 0:lanes] = s_turn[...].T.astype(BF16)
    if late_ref.shape[1] > lanes:
        turned = grad_query.astype(F32).T
        slab = s_slab.shape[0]
        s_slab[...] = jnp.zeros_like(s_slab)
        for place in range(full_width // slab):
            down = slice(place * slab, (place + 1) * slab)
            s_slab[:, place * pairs : (place + 1) * pairs] = turned[down, :]
        slab_low = s_slab[...].astype(BF16)
        for place in range(full_width // slab):
            late_ref[place * slab : (place + 1) * slab, lanes:] = slab_low


def rows_kernel(dims, *refs):
    pairs, tokens, full_width, full_hidden, slice_width, slice_hidden, stages, pieces = dims
    early_hbm = refs[:pieces]
    (
        ends_ref,
        hat_hbm,
        inv_hbm,
        probs_hbm,
        back_ref,
        value_factors_ref,
        keys_ref,
        rows_one_ref,
        rows_mid_ref,
        grad_hbm,
        ag,
        ab,
        triple_hbm,
        triple_bias,
        wo_hbm,
        bo,
        fg,
        fb,
        ww_hbm,
        bw,
        wn_hbm,
        lg,
        lb,
        we_hbm,
        out_hbm,
        ones_ref,
        queries_ref,
        values_ref,
        embed_ref,
        narrow_ref,
        widen_ref,
        mixer_ref,
        final_gain_ref,
        final_bias_ref,
        feed_gain_ref,
        feed_bias_ref,
        narrow_bias_ref,
        mixer_bias_ref,
        value_bias_ref,
        widen_bias_ref,
        s_triple,
        s_wo,
        s_ww,
        s_wn,
        s_we,
        s_vectors,
        s_hat,
        s_inv,
        s_left,
        s_right,
        s_early,
        grad_ref,
        s_out,
        s_total,
        s_active,
        s_hidden,
        sems,
        hidden_sems,
        out_sems,
    ) = refs[pieces:]
    all_pairs = grad_ref.shape[0]
    block = block_rows(all_pairs)
    here = lax.axis_index("dp")
    is_text, width, mask = tower_sizes(full_width, full_hidden)
    get_probs = fetch(probs_hbm, s_left.at[pl.ds(0, full_width // HEAD * pairs), :], sems.at[3])
    get_hat = fetch(hat_hbm, s_hat, sems.at[4])
    get_inv = fetch(inv_hbm, s_inv, sems.at[5])
    get_grad = fetch(grad_hbm, grad_ref, sems.at[6])
    height = s_early.shape[0] // pieces
    early = [s_early.at[pl.ds(place * height, height), :] for place in range(pieces)]
    get_early = [fetch(early_hbm[place], early[place], sems.at[7 + place]) for place in range(pieces)]
    get_wo = fetch(wo_hbm.at[0], s_wo, sems.at[1])
    get_we = fetch(we_hbm.at[0], s_we, sems.at[2])
    hidden = Hidden(ww_hbm, wn_hbm, s_ww, s_wn, hidden_sems, full_hidden // CHUNK)
    hidden.start((0, 1))
    get_triple = fetch(triple_hbm.at[0, 0], s_triple, sems.at[0])
    rows = full_width // HEAD * pairs
    token_gain = ag[...] * mask
    s_left[rows : 2 * rows, :] = back_ref[...]
    s_right[0:rows, :] = value_factors_ref[...]
    s_right[rows : 2 * rows, :] = keys_ref[...]
    spots = pooled_spots(ends_ref, is_text, pairs, 3)
    s_left[2 * rows :, :] = one_hot(iota((3 * pairs, tokens), 1).astype(F32) == spots)
    s_right[2 * rows :, :] = three_parts(rows_one_ref[...])
    middle_parts = three_parts(rows_mid_ref[...])
    ones = one_hot(iota((full_width, 128), 0).astype(F32) < width)
    get_probs.wait()
    get_hat.wait()
    get_inv.wait()

    def put(at, count):
        spot = pl.ds(at, count)
        return pltpu.make_async_copy(
            s_out.at[spot, :], out_hbm.at[0, spot, :], out_sems.at[at // NORM_ROWS]
        )

    def norm_rows(at, count):
        spot = pl.ds(at, count)
        upward = mm_tn(s_left[:, spot], s_right[...])
        hat = s_hat[spot, :].astype(F32)
        scaled = upward * token_gain
        mean = mm(scaled.astype(BF16), ones) / width
        along = mm((scaled * hat).astype(BF16), ones) / width
        s_out[spot, :] = across(s_inv[spot, :], full_width) * (
            scaled - (across(mean, full_width) + hat * across(along, full_width)) * mask
        ) + mm_tn(s_left[2 * rows :, spot], middle_parts)
        put(at, count).start()

    over_tokens(tokens, NORM_ROWS, norm_rows)
    for ref in (embed_ref, narrow_ref, widen_ref, mixer_ref, widen_bias_ref, s_vectors):
        ref[...] = jnp.zeros_like(ref)
    lane = iota((full_width, slice_width), 0)
    pick = one_hot(
        (lane == here * slice_width + iota((full_width, slice_width), 1))
        & (lane.astype(F32) < width)
    )
    hidden_width = jnp.where(is_text, MLP_TXT, full_hidden)
    gain, shift = lg[...] * mask, lb[...] * mask
    feed_gain = fg[...] * mask
    get_wo.wait()
    get_we.wait()
    get_grad.wait()
    for copy in get_early:
        copy.wait()

    def part(index):
        at = pl.multiple_of(index * block, block)
        here_rows = pl.ds(at, block)
        arrived = in_order(early, stages, pairs, block, at)
        mixed = arrived[:, 0:full_width]
        stream_rows = arrived[:, full_width : 2 * full_width].astype(F32)
        out_hat = arrived[:, 2 * full_width : 3 * full_width].astype(F32)
        out_inv = jnp.sum(arrived[:, 3 * full_width :].astype(F32), axis=1, keepdims=True)
        three = (out_hat * gain + shift).astype(BF16)
        grad_embed = embed_back(mm(three, s_we[...]), grad_ref[here_rows, :])
        embed_ref[0] += mm_tn(mm(three, pick).astype(BF16), grad_embed)
        grad_three = mm_nt(grad_embed, s_we[...])
        s_vectors[0:1, :] += sums_of(grad_three * out_hat)
        s_vectors[1:2, :] += sums_of(grad_three)
        grad_pooled = norm_back(out_hat, out_inv, gain, grad_three, mask, width)
        branch = grad_pooled.astype(BF16)
        s_vectors[2:3, :] += sums_of(branch.astype(F32))
        middle = stream_rows + mm(mixed, s_wo[...]) + bo[...]
        mid_hat, mid_inv = normed(middle, mask, width)
        two = ((mid_hat * fg[...] + fb[...]) * mask).astype(BF16)
        s_total[...] = jnp.zeros_like(s_total)
        s_active[...] = jnp.zeros_like(s_active)
        s_hidden[...] = jnp.zeros_like(s_hidden)

        def through(chunk, carry):
            first = pl.multiple_of(chunk * CHUNK, CHUNK)
            lanes = pl.ds(first, CHUNK)
            if all_pairs == block:
                hidden.wait(chunk)
            pre = mm(two, s_ww[:, lanes]) + bw[:, lanes]
            gate = sigmoid(1.702 * pre)
            active = pre * gate
            there = (first + iota((1, CHUNK), 1) < hidden_width).astype(F32)
            slope = (gate + 1.702 * active * (1.0 - gate)) * there
            grad_hidden = (mm_nt(branch, s_wn[lanes, :]) * slope).astype(BF16)
            s_total[...] += mm_nt(grad_hidden, s_ww[:, lanes])
            row = first + iota((CHUNK, slice_hidden), 0)
            chosen = one_hot(
                (row == here * slice_hidden + iota((CHUNK, slice_hidden), 1))
                & (row < hidden_width)
            )
            s_active[...] += mm(active.astype(BF16), chosen)
            s_hidden[...] += mm(grad_hidden, chosen)
            return carry

        lax.fori_loop(0, full_hidden // CHUNK, through, 0)
        grad_two, active_slice, hidden_slice = s_total[...], s_active[...], s_hidden[...]
        narrow_ref[0] += mm_tn(active_slice.astype(BF16), branch)
        widen_ref[0] += mm_tn(hidden_slice.astype(BF16), two)
        widen_bias_ref[...] += sums_of(hidden_slice)
        s_vectors[3:4, :] += sums_of(grad_two * mid_hat)
        s_vectors[4:5, :] += sums_of(grad_two)
        grad_middle = grad_pooled + norm_back(mid_hat, mid_inv, feed_gain, grad_two, mask, width)
        attention = grad_middle.astype(BF16)
        s_vectors[5:6, :] += sums_of(attention.astype(F32))
        mixer_ref[0] += mm_tn(mm(mixed, pick).astype(BF16), attention)
        grad_mixed = (mm_nt(attention, s_wo[...]) * mask).astype(BF16)
        values_ref[here_rows, :] = grad_mixed
        s_vectors[6:7, :] += sums_of(grad_mixed.astype(F32))
        rows_hat, _ = normed(stream_rows, mask, width)
        one = ((rows_hat * ag[...] + ab[...]) * mask).astype(BF16)
        ones_ref[here_rows, :] = mm(one, pick).astype(BF16)
        if all_pairs == block:
            get_triple.wait()
        query = (mm(one, s_triple[...]) + triple_bias[0, 0:1, :]) * mask
        queries_ref[here_rows, :] = query.astype(BF16)

    if all_pairs != block:
        get_triple.wait()
        for chunk in range(full_hidden // CHUNK):
            hidden.wait(chunk)
    over_blocks(all_pairs // block, part)
    over_tokens(tokens, NORM_ROWS, lambda at, count: put(at, count).wait())
    vectors = dot_dims(s_vectors[...], pick.astype(F32), 1, 0, lax.Precision.HIGHEST)
    for slot, ref in enumerate(
        (
            final_gain_ref,
            final_bias_ref,
            narrow_bias_ref,
            feed_gain_ref,
            feed_bias_ref,
            mixer_bias_ref,
            value_bias_ref,
        )
    ):
        ref[...] = vectors[slot : slot + 1, :]


def last_kernel(dims, *refs):
    pairs, full_width, full_hidden, slice_width, stages, pieces = dims
    arrived = refs[:pieces]
    (
        late_ref,
        means_ref,
        ones_ref,
        queries_ref,
        values_ref,
        value_bias_ref,
        triple_ref,
        gain_ref,
        shift_ref,
        bias_ref,
        s_keys,
        s_means,
        s_turned,
        s_late,
        s_sums,
    ) = refs[pieces:]
    here = lax.axis_index("dp")
    count = late_ref.shape[0]
    lanes = means_ref.shape[2]
    heads = full_width // HEAD
    rows = heads * pairs
    all_pairs = queries_ref.shape[0]
    s_late[...] = jnp.zeros_like(s_late)
    if not arrived:
        sources = range(count)
        for source in sources:
            s_late[...] += late_ref[source, :, 0:lanes].astype(F32)
        for head in range(heads):
            down = slice(head * slice_width, (head + 1) * slice_width)
            lane = slice(head * pairs, (head + 1) * pairs)
            s_keys[down, :] = jnp.concatenate([late_ref[source, :, lane] for source in sources], axis=1)
            s_means[down, :] = jnp.concatenate([means_ref[source, :, lane] for source in sources], axis=1)
        for slab in sources:
            down = slice(slab * slice_width, (slab + 1) * slice_width)
            lane = slice(lanes + slab * pairs, lanes + (slab + 1) * pairs)
            s_turned[down, :] = jnp.concatenate([late_ref[source, :, lane] for source in sources], axis=1)
        left = iota((slice_width, 2 * HEAD), 1) < HEAD
        for two in range(heads // 2):
            down = slice(two * 2 * slice_width, (two + 1) * 2 * slice_width)
            lane = slice(two * 2 * HEAD, (two + 1) * 2 * HEAD)
            both = mm(s_keys[down, :], queries_ref[:, lane]) * 0.125
            triple_ref[0, 1, :, lane] = jnp.where(left, both[0:slice_width], both[slice_width:])
            both = mm(s_means[down, :], values_ref[:, lane])
            triple_ref[0, 2, :, lane] = jnp.where(left, both[0:slice_width], both[slice_width:])
        triple_ref[0, 0] = mm(s_turned[...], ones_ref[...]).T
        mine = s_turned[pl.ds(pl.multiple_of(here * slice_width, slice_width), slice_width), :]
        sums = mm_nt(jnp.ones((8, all_pairs), BF16), mine)
    else:
        block = block_rows(all_pairs)
        triple_ref[...] = jnp.zeros_like(triple_ref)
        s_sums[...] = jnp.zeros_like(s_sums)

        def part(index):
            at = pl.multiple_of(index * block, block)
            grad_query = in_order(arrived, stages, pairs, block, at)
            triple_ref[0, 0] += mm_tn(ones_ref[pl.ds(at, block), :], grad_query)
            s_sums[0:1, :] += sums_of(grad_query.astype(F32))

        over_blocks(all_pairs // block, part)
        head = head_mask(lanes, pairs, full_width)

        def one(source, carry):
            now = late_ref[source]
            s_late[...] += now.astype(F32)
            row = iota((lanes, all_pairs), 0)
            column = iota((lanes, all_pairs), 1)
            repeat = one_hot((column == source * pairs + lax.rem(row, pairs)) & (row < rows))
            means = means_ref[source]
            for which, left, origin in ((1, now, queries_ref), (2, means, values_ref)):
                wide = jnp.where(head, mm(repeat, origin[...]), 0.0).astype(BF16)
                triple_ref[0, which] += mm(left, wide)
            return carry

        lax.fori_loop(0, count, one, 0)
        triple_ref[0, 1] = triple_ref[0, 1] * 0.125
        pick = (
            iota((full_width, slice_width), 0)
            == here * slice_width + iota((full_width, slice_width), 1)
        ).astype(F32)
        sums = dot_dims(s_sums[...], pick, 1, 0, lax.Precision.HIGHEST)
    lane = iota((8, lanes), 1)
    row = iota((8, lanes), 0)
    slot = rows + row * 3
    chosen = ((lane >= slot) & (lane < slot + 3) & (row < 2)).astype(F32)
    from_late = dot_dims(chosen, s_late[...], 1, 1, lax.Precision.HIGHEST)
    gain_ref[...] = from_late[0:1, :]
    shift_ref[...] = from_late[1:2, :]
    bias_ref[0, 0:1, :] = sums[0:1, :]
    bias_ref[0, 1:2, :] = value_bias_ref[...]


def stages_of(count):
    bits = count.bit_length() - 1
    stages = []
    while bits > 0:
        take = 2 if bits >= 2 else 1
        bits -= take
        stages.append((bits, take))
    return tuple(stages)


def exchange(block, axis, stage):
    count = lax.axis_size(axis)
    shift, bits = stage
    parts = [block]
    for apart in range(1, 1 << bits):
        route = [(low, low ^ (apart << shift)) for low in range(count)]
        parts.append(lax.ppermute(block, axis, route))
    return parts


def call(
    kernel, ins, outs, scratch, in_hbm=(), out_hbm=(), cost=None, kept=(), limit=VMEM_LIMIT
):
    vmem = pl.BlockSpec(memory_space=pltpu.VMEM)
    anywhere = pl.BlockSpec(memory_space=pl.ANY)
    specs = [anywhere if index in in_hbm else vmem for index in range(len(ins))]
    out_specs = [anywhere if index in out_hbm else vmem for index in range(len(outs))]
    if kept:
        ins = [
            pltpu.with_memory_space_constraint(
                array, pltpu.VMEM if index in kept else pltpu.HBM
            )
            for index, array in enumerate(ins)
        ]
    flops, moved = cost
    return pl.pallas_call(
        kernel,
        out_shape=[jax.ShapeDtypeStruct(shape, kind) for shape, kind in outs],
        in_specs=specs,
        out_specs=out_specs,
        scratch_shapes=scratch,
        compiler_params=pltpu.CompilerParams(vmem_limit_bytes=limit),
        cost_estimate=pl.CostEstimate(flops=flops, bytes_accessed=moved, transcendentals=0),
    )(*ins)


def body(
    block_input,
    segments,
    caption_ends,
    pair_flags,
    attention_gain,
    attention_bias,
    triple_weight,
    triple_bias,
    mixer_weight,
    mixer_bias,
    feed_gain,
    feed_bias,
    widen_weight,
    widen_bias,
    narrow_weight,
    narrow_bias,
    final_gain,
    final_bias,
    embed_weight,
    logit_scale,
    loss_scale,
):
    tokens, width = block_input.shape[1:]
    hidden = widen_weight.shape[2]
    emb = embed_weight.shape[2]
    pairs = caption_ends.shape[0]
    count = lax.axis_size("dp")
    all_pairs = pair_flags.shape[0]
    heads = width // HEAD
    rows = heads * pairs
    lanes = -(-(rows + 12) // 128) * 128
    slice_width = width // count
    slice_hidden = hidden // count
    stages = stages_of(count)
    compact = count <= 16 and slice_width % 16 == 0
    slab_lanes = -(-all_pairs // 128) * 128
    ends = caption_ends.reshape(1, pairs)
    dma = pltpu.SemaphoreType.DMA
    weights_scratch = [
        pltpu.VMEM((3, width, width), BF16),
        pltpu.VMEM((width, width), BF16),
        pltpu.VMEM((width, hidden), BF16),
        pltpu.VMEM((hidden, width), BF16),
        pltpu.VMEM((width, emb), BF16),
    ]
    dims = (pairs, tokens, width, hidden)
    chunk_count = hidden // CHUNK
    (
        unit,
        early,
        hat,
        invert,
        probs,
        query,
        embedded,
        pooled,
        middle,
        slope,
    ) = call(
        partial(attend_kernel, dims),
        (
            ends,
            block_input,
            attention_gain,
            attention_bias,
            triple_weight,
            triple_bias,
            mixer_weight,
            mixer_bias,
            feed_gain,
            feed_bias,
            widen_weight,
            widen_bias,
            narrow_weight,
            narrow_bias,
            final_gain,
            final_bias,
            embed_weight,
        ),
        [
            ((pairs, emb), BF16),
            ((pairs, 3 * width + 128), BF16),
            ((tokens, width), BF16),
            ((tokens, 128), F32),
            ((rows, tokens), BF16),
            ((pairs, width), BF16),
            ((pairs, emb), F32),
            ((pairs, width), F32),
            ((pairs, width), F32),
            ((pairs, hidden), F32),
        ],
        [
            pltpu.VMEM((tokens, width), BF16),
            pltpu.VMEM((tokens, width), BF16),
            pltpu.VMEM((tokens, width), BF16),
            pltpu.VMEM((tokens, 128), F32),
            pltpu.VMEM((rows, tokens), F32),
            pltpu.VMEM((tokens, width), BF16),
            pltpu.VMEM((tokens, width), BF16),
        ]
        + weights_scratch
        + [
            pltpu.VMEM((rows, tokens), BF16),
            dma((7,)),
            dma((2, chunk_count)),
        ],
        in_hbm=(1, 4, 6, 10, 12, 16),
        out_hbm=(2, 3, 4),
        cost=(10**9, 20 * 10**6),
    )
    turned, spread, keys, hat_rows = call(
        partial(means_kernel, dims),
        (ends, attention_gain, attention_bias, hat, probs, query, triple_weight),
        [
            ((width, lanes), BF16),
            ((rows, width), BF16),
            ((rows, width), BF16),
            ((pairs, width), BF16),
        ],
        [
            pltpu.VMEM((width, width), BF16),
            pltpu.VMEM((lanes, width), F32),
            dma((1,)),
        ],
        in_hbm=(6,),
        cost=(10**9, 5 * 10**6),
    )
    early_rows, own_rel = early, unit
    flags = pair_flags.reshape(1, all_pairs)
    for index, stage in enumerate(stages):
        own_parts = exchange(own_rel, "dp", stage)
        if index + 1 < len(stages):
            own_parts, early_rows, turned, spread, keys, hat_rows, flags = lax.optimization_barrier(
                (own_parts, early_rows, turned, spread, keys, hat_rows, flags)
            )
            early_rows = jnp.concatenate(exchange(early_rows, "dp", stage), axis=0)
        own_rel = jnp.concatenate(own_parts, axis=0)
    means_all = lax.all_to_all(turned, "dp", 0, 0, tiled=True).reshape(count, slice_width, lanes)
    other_rel = lax.ppermute(own_rel, "tower", [(0, 1), (1, 0)])
    early_pieces = exchange(early_rows, "dp", stages[-1])
    (
        loss,
        hits,
        scale,
        grad_all,
        late,
        queries,
        back,
        values,
        rows_one,
        rows_mid,
    ) = call(
        partial(loss_kernel, dims + (stages,)),
        (
            own_rel,
            other_rel,
            flags,
            logit_scale.reshape(1, 1),
            loss_scale.reshape(1, 1),
            attention_gain,
            attention_bias,
            triple_weight,
            triple_bias,
            mixer_weight,
            feed_gain,
            widen_weight,
            narrow_weight,
            final_gain,
            embed_weight,
            hat,
            probs,
            spread,
            keys,
            embedded,
            pooled,
            middle,
            slope,
            hat_rows,
        ),
        [
            ((1, 1), F32),
            ((1, 1), F32),
            ((1, 1), F32),
            ((all_pairs, emb), F32),
            ((width, lanes + (slab_lanes if compact else 0)), BF16),
            ((pairs, width), BF16),
            ((rows, tokens), BF16),
            ((rows, width), BF16),
            ((pairs, width), F32),
            ((pairs, width), F32),
        ],
        [pltpu.VMEM((all_pairs, emb), BF16), pltpu.VMEM((all_pairs, emb), BF16)]
        + weights_scratch
        + [
            pltpu.VMEM((tokens, width), BF16),
            pltpu.VMEM((rows, tokens), BF16),
            pltpu.VMEM((pairs, emb), F32),
            pltpu.VMEM((pairs, width), F32),
            pltpu.VMEM((lanes, width), F32),
            pltpu.VMEM((slice_width, slab_lanes), F32),
            dma((5,)),
            dma((2, chunk_count)),
        ],
        in_hbm=(7, 9, 11, 12, 14, 15, 16),
        cost=(10**9, 20 * 10**6),
    )
    early_pieces, late, queries = lax.optimization_barrier((early_pieces, late, queries))
    late_all = lax.all_to_all(late, "dp", 0, 0, tiled=True)
    late_all = late_all.reshape(count, slice_width, late.shape[1])
    late_pieces = []
    if not compact:
        late_pieces = [queries]
        for stage in stages:
            late_pieces = exchange(jnp.concatenate(late_pieces, axis=0), "dp", stage)
    ahead = len(early_pieces)
    vector = ((1, slice_width), F32)
    (
        block_grad,
        ones,
        query_rows,
        value_rows,
        grad_embed,
        grad_narrow,
        grad_widen,
        grad_mixer,
        grad_final_gain,
        grad_final_bias,
        grad_feed_gain,
        grad_feed_bias,
        grad_narrow_bias,
        grad_mixer_bias,
        grad_value_bias,
        grad_widen_bias,
    ) = call(
        partial(
            rows_kernel,
            (pairs, tokens, width, hidden, slice_width, slice_hidden, stages, ahead),
        ),
        tuple(early_pieces)
        + (
            ends,
            hat,
            invert,
            probs,
            back,
            values,
            keys,
            rows_one,
            rows_mid,
            grad_all,
            attention_gain,
            attention_bias,
            triple_weight,
            triple_bias,
            mixer_weight,
            mixer_bias,
            feed_gain,
            feed_bias,
            widen_weight,
            widen_bias,
            narrow_weight,
            final_gain,
            final_bias,
            embed_weight,
        ),
        [
            ((1, tokens, width), F32),
            ((all_pairs, slice_width), BF16),
            ((all_pairs, width), BF16),
            ((all_pairs, width), BF16),
            ((1, slice_width, emb), F32),
            ((1, slice_hidden, width), F32),
            ((1, slice_hidden, width), F32),
            ((1, slice_width, width), F32),
        ]
        + [vector] * 7
        + [((1, slice_hidden), F32)],
        [pltpu.VMEM((width, width), BF16)]
        + weights_scratch[1:]
        + [
            pltpu.VMEM((8, width), F32),
            pltpu.VMEM((tokens, width), BF16),
            pltpu.VMEM((tokens, 128), F32),
            pltpu.VMEM((2 * rows + 3 * pairs, tokens), BF16),
            pltpu.VMEM((2 * rows + 3 * pairs, width), BF16),
            pltpu.VMEM((all_pairs, 3 * width + 128), BF16),
            pltpu.VMEM((all_pairs, emb), F32),
            pltpu.VMEM((tokens, width), F32),
            pltpu.VMEM((block_rows(all_pairs), width), F32),
            pltpu.VMEM((block_rows(all_pairs), slice_hidden), F32),
            pltpu.VMEM((block_rows(all_pairs), slice_hidden), F32),
            dma((7 + ahead,)),
            dma((2, chunk_count)),
            dma((-(-tokens // NORM_ROWS),)),
        ],
        in_hbm=tuple(range(ahead)) + tuple(ahead + index for index in (1, 2, 3, 9, 12, 14, 18, 20, 23)),
        out_hbm=(0,),
        cost=(3 * 10**9, 10 * 10**6),
    )
    grad_triple, grad_gain, grad_bias, grad_triple_bias = call(
        partial(last_kernel, (pairs, width, hidden, slice_width, stages, len(late_pieces))),
        tuple(late_pieces)
        + (late_all, means_all, ones, query_rows, value_rows, grad_value_bias),
        [
            ((1, 3, slice_width, width), F32),
            vector,
            vector,
            ((1, 2, slice_width), F32),
        ],
        [
            pltpu.VMEM((width // HEAD * slice_width, all_pairs), BF16),
            pltpu.VMEM((width // HEAD * slice_width, all_pairs), BF16),
            pltpu.VMEM((width, all_pairs), BF16),
            pltpu.VMEM((slice_width, lanes), F32),
            pltpu.VMEM((8, width), F32),
        ],
        cost=(10**9, 10 * 10**6),
        kept=(0,) if compact else (),
        limit=32 * 1024 * 1024 if compact else VMEM_LIMIT,
    )
    return (
        loss[0, 0],
        hits[0, 0],
        block_grad,
        grad_gain,
        grad_bias,
        grad_triple,
        grad_triple_bias,
        grad_mixer,
        grad_mixer_bias,
        grad_feed_gain,
        grad_feed_bias,
        jnp.swapaxes(grad_widen, 1, 2),
        grad_widen_bias,
        grad_narrow,
        grad_narrow_bias,
        grad_final_gain,
        grad_final_bias,
        grad_embed,
        scale[0, 0],
    )


def solution(mesh):
    in_specs = (
        P("tower", "dp", None),
        P("dp", None),
        P("dp"),
        P(),
        P("tower", None),
        P("tower", None),
        P("tower", None, None, None),
        P("tower", None, None),
        P("tower", None, None),
        P("tower", None),
        P("tower", None),
        P("tower", None),
        P("tower", None, None),
        P("tower", None),
        P("tower", None, None),
        P("tower", None),
        P("tower", None),
        P("tower", None),
        P("tower", None, None),
        P(),
        P(),
    )
    out_specs = (
        P(),
        P(),
        P("tower", "dp", None),
        P("tower", "dp"),
        P("tower", "dp"),
        P("tower", None, "dp", None),
        P("tower", None, "dp"),
        P("tower", "dp", None),
        P("tower", "dp"),
        P("tower", "dp"),
        P("tower", "dp"),
        P("tower", None, "dp"),
        P("tower", "dp"),
        P("tower", "dp", None),
        P("tower", "dp"),
        P("tower", "dp"),
        P("tower", "dp"),
        P("tower", "dp", None),
        P(),
    )
    return jax.shard_map(body, mesh=mesh, in_specs=in_specs, out_specs=out_specs, check_vma=False)
```

```python
from functools import partial

import jax
import jax.numpy as jnp
from jax import lax
from jax.experimental import pallas as pl
from jax.experimental.pallas import tpu as pltpu
from jax.sharding import PartitionSpec as P

D_TXT = 512
MLP_TXT = 2048
HEAD = 64
IMG_TOK = 50
CTX = 77
F32 = jnp.float32
BF16 = jnp.bfloat16
VMEM_LIMIT = 62 * 1024 * 1024
CHUNK = 1024
NORM_ROWS = 272
PROJECT_ROWS = 1088


def dot_dims(left, right, left_dim, right_dim, precision=None):
    return lax.dot_general(
        left,
        right,
        (((left_dim,), (right_dim,)), ((), ())),
        preferred_element_type=F32,
        precision=precision,
    )


def mm(left, right):
    return dot_dims(left, right, 1, 0)


def mm_nt(left, right):
    return dot_dims(left, right, 1, 1)


def mm_tn(left, right):
    return dot_dims(left, right, 0, 0)


def iota(shape, dim):
    return lax.broadcasted_iota(jnp.int32, shape, dim)


def sigmoid(rows):
    return 1.0 / (1.0 + jnp.exp(-rows))


def one_hot(condition):
    return condition.astype(F32).astype(BF16)


def normed(rows, mask, width):
    mean = jnp.sum(rows * mask, axis=-1, keepdims=True) / width
    centre = (rows - mean) * mask
    invert = lax.rsqrt(jnp.sum(centre * centre, axis=-1, keepdims=True) / width + 1e-05)
    return centre * invert, invert


def norm_back(rows_hat, invert, gain, upward, mask, width):
    scaled = upward * gain
    mean = jnp.sum(scaled, axis=-1, keepdims=True) / width
    along = jnp.sum(scaled * rows_hat, axis=-1, keepdims=True) / width
    return invert * (scaled - mean * mask - rows_hat * along)


def sums_of(rows):
    return jnp.sum(rows, axis=0, keepdims=True)


def head_mask(rows, pairs, width):
    row = iota((rows, width), 0)
    first = lax.shift_right_logical(iota((rows, width), 1), 6) * pairs
    return (row >= first) & (row < first + pairs)


def repeat_rows(rows, pairs):
    row = iota((rows, pairs), 0)
    return one_hot(lax.rem(row, pairs) == iota((rows, pairs), 1))


def tower_sizes(full_width, full_hidden):
    is_text = lax.axis_index("tower") != 0
    width = jnp.where(is_text, D_TXT, full_width)
    mask = (iota((1, full_width), 1) < width).astype(F32)
    return is_text, width.astype(F32), mask


def fetch(source, target, semaphore):
    copy = pltpu.make_async_copy(source, target, semaphore)
    copy.start()
    return copy


def three_parts(rows):
    parts = []
    for _ in range(3):
        part = rows.astype(BF16).astype(F32)
        parts.append(part)
        rows = rows - part
    return jnp.concatenate(parts, axis=0).astype(BF16)


def over_tokens(tokens, size, step):
    for at in range(0, tokens, size):
        step(at, min(size, tokens - at))


def across(lane_sums, full_width):
    return jnp.concatenate([lane_sums] * (full_width // 128), axis=1)


def pooled_spots(ends_ref, is_text, pairs, copies):
    pair = lax.rem(iota((copies * pairs, pairs), 0), pairs)
    ends = jnp.where(pair == iota((copies * pairs, pairs), 1), ends_ref[...], 0).astype(F32)
    ends = jnp.sum(ends, axis=1, keepdims=True)
    firsts = (lax.rem(iota((copies * pairs, 1), 0), pairs) * IMG_TOK).astype(F32)
    return jnp.where(is_text, ends, firsts)


def embed_back(embedded, grad_unit):
    inv_norm = lax.rsqrt(jnp.sum(embedded * embedded, axis=-1, keepdims=True) + 1e-06)
    along = jnp.sum(embedded * grad_unit, axis=-1, keepdims=True)
    return (inv_norm * grad_unit - inv_norm * inv_norm * inv_norm * embedded * along).astype(BF16)


class Hidden:
    def __init__(self, widen_hbm, narrow_hbm, s_widen, s_narrow, sems, chunks):
        self.pairs = (
            (lambda at: widen_hbm.at[0, :, pl.ds(at, CHUNK)], lambda at: s_widen.at[:, pl.ds(at, CHUNK)]),
            (lambda at: narrow_hbm.at[0, pl.ds(at, CHUNK), :], lambda at: s_narrow.at[pl.ds(at, CHUNK), :]),
        )
        self.sems = sems
        self.chunks = chunks

    def copy(self, which, chunk):
        source, target = self.pairs[which]
        at = chunk * CHUNK
        if not isinstance(at, int):
            at = pl.multiple_of(at, CHUNK)
        return pltpu.make_async_copy(source(at), target(at), self.sems.at[which, chunk])

    def start(self, order):
        for chunk in range(self.chunks):
            for which in order:
                self.copy(which, chunk).start()

    def wait(self, chunk):
        self.copy(0, chunk).wait()
        self.copy(1, chunk).wait()

    def each(self, step):
        for chunk in range(self.chunks):
            self.wait(chunk)
            step(slice(chunk * CHUNK, (chunk + 1) * CHUNK))


def attend_kernel(
    dims,
    ends_ref,
    x_hbm,
    ag,
    ab,
    triple_hbm,
    triple_bias,
    wo_hbm,
    bo,
    fg,
    fb,
    ww_hbm,
    bw,
    wn_hbm,
    bn,
    lg,
    lb,
    we_hbm,
    unit_ref,
    early_ref,
    hat_hbm,
    inv_hbm,
    probs_hbm,
    query_ref,
    embedded_ref,
    pooled_ref,
    middle_ref,
    slope_ref,
    s_x,
    s_one,
    s_hat,
    s_inv,
    s_probs,
    s_key,
    s_value,
    s_triple,
    s_wo,
    s_ww,
    s_wn,
    s_we,
    s_low,
    sems,
    hidden_sems,
):
    pairs, tokens, full_width, full_hidden = dims
    is_text, width, mask = tower_sizes(full_width, full_hidden)
    rows = full_width // HEAD * pairs
    get_x = fetch(x_hbm.at[0], s_x, sems.at[0])
    get_triple = fetch(triple_hbm.at[0], s_triple, sems.at[1])
    gain, shift = ag[...] * mask, ab[...] * mask
    ones = one_hot((iota((full_width, 128), 0)).astype(F32) < width)
    hidden = Hidden(ww_hbm, wn_hbm, s_ww, s_wn, hidden_sems, full_hidden // CHUNK)
    get_x.wait()
    get_wo = fetch(wo_hbm.at[0], s_wo, sems.at[2])
    hidden.start((0, 1))
    get_we = fetch(we_hbm.at[0], s_we, sems.at[3])

    def norm_rows(at, count):
        here = pl.ds(at, count)
        low = s_x[here, :]
        mean = mm(low, ones) / width
        centre = low.astype(F32) - across(mean, full_width)
        square = centre * centre
        high = square.astype(BF16)
        low = (square - high.astype(F32)).astype(BF16)
        invert = lax.rsqrt((mm(high, ones) + mm(low, ones)) / width + 1e-05)
        hat = centre * across(invert, full_width)
        s_hat[here, :] = hat.astype(BF16)
        s_one[here, :] = (hat * gain + shift).astype(BF16)
        s_inv[here, :] = invert

    over_tokens(tokens, NORM_ROWS, norm_rows)
    put_hat = fetch(s_hat, hat_hbm, sems.at[4])
    put_inv = fetch(s_inv, inv_hbm, sems.at[5])
    pick = one_hot(iota((pairs, tokens), 1).astype(F32) == pooled_spots(ends_ref, is_text, pairs, 1))
    stream_rows = mm(pick, s_x[...]) * mask
    one = mm(pick, s_one[...]).astype(BF16)
    get_triple.wait()
    query = ((mm(one, s_triple[0]) + triple_bias[0, 0:1, :]) * (mask * 0.125)).astype(BF16)
    repeat = repeat_rows(rows, pairs)
    heads = head_mask(rows, pairs, full_width)
    wide = jnp.where(heads, mm(repeat, query), 0.0).astype(BF16)

    def project(at, count):
        here = pl.ds(at, count)
        s_key[here, :] = mm(s_one[here, :], s_triple[1]).astype(BF16)
        s_value[here, :] = (mm(s_one[here, :], s_triple[2]) + triple_bias[0, 1:2, :]).astype(BF16)

    over_tokens(tokens, PROJECT_ROWS, project)
    s_probs[...] = mm_nt(wide, s_key[...])
    last = pooled_spots(ends_ref, is_text, pairs, rows // pairs)
    pair = lax.rem(iota((rows, 1), 0), pairs)
    stops = jnp.where(
        pair - 1 == iota((rows, pairs), 1), ends_ref[...] + 1, 0
    ).astype(F32)
    first = jnp.where(is_text, jnp.sum(stops, axis=1, keepdims=True), last)
    last = jnp.where(is_text, last, last + (IMG_TOK - 1.0))
    step_rows = 48
    for at in range(0, rows, step_rows):
        here = slice(at, at + step_rows)
        place = iota((step_rows, tokens), 1).astype(F32)
        allowed = (place >= first[here]) & (place <= last[here])
        scores = jnp.where(allowed, s_probs[here, :], -1e30)
        powers = jnp.exp(scores - jnp.max(scores, axis=1, keepdims=True))
        probs = powers * (1.0 / jnp.sum(powers, axis=1, keepdims=True))
        s_low[here, :] = probs.astype(BF16)
    put_probs = fetch(s_low, probs_hbm, sems.at[6])
    mixed_wide = mm(s_low[...], s_value[...])
    mixed = mm_tn(repeat, jnp.where(heads, mixed_wide, 0.0).astype(BF16))
    mixed = (mixed * mask).astype(BF16)
    early_ref[:, 0:full_width] = mixed
    early_ref[:, full_width : 2 * full_width] = stream_rows.astype(BF16)
    get_wo.wait()
    middle = stream_rows + mm(mixed, s_wo[...]) + bo[...]
    middle_ref[...] = middle
    mid_hat, _ = normed(middle, mask, width)
    two = ((mid_hat * fg[...] + fb[...]) * mask).astype(BF16)
    pooled_ref[...] = middle + bn[...]
    hidden_width = jnp.where(is_text, MLP_TXT, full_hidden)
    hidden_mask = (iota((1, full_hidden), 1) < hidden_width).astype(F32)

    def forward(at):
        pre = mm(two, s_ww[:, at]) + bw[:, at]
        gate = sigmoid(1.702 * pre)
        active = pre * gate * hidden_mask[:, at]
        slope_ref[:, at] = (gate + 1.702 * active * (1.0 - gate)) * hidden_mask[:, at]
        pooled_ref[...] += mm(active.astype(BF16), s_wn[at, :])

    hidden.each(forward)
    out_hat, out_inv = normed(pooled_ref[...], mask, width)
    early_ref[:, 2 * full_width : 3 * full_width] = out_hat.astype(BF16)
    lane = iota((pairs, 128), 1)
    numbers = jnp.zeros((pairs, 128), F32)
    for place in range(3):
        part = out_inv.astype(BF16).astype(F32)
        numbers = jnp.where(lane == place, part, numbers)
        out_inv = out_inv - part
    early_ref[:, 3 * full_width :] = numbers.astype(BF16)
    three = ((out_hat * lg[...] + lb[...]) * mask).astype(BF16)
    get_we.wait()
    embedded = mm(three, s_we[...])
    embedded_ref[...] = embedded
    unit_ref[...] = (
        embedded * lax.rsqrt(jnp.sum(embedded * embedded, axis=-1, keepdims=True) + 1e-06)
    ).astype(BF16)
    query_ref[...] = query
    for copy in (put_hat, put_inv, put_probs):
        copy.wait()


def means_kernel(
    dims,
    ends_ref,
    ag,
    ab,
    hat_ref,
    probs_ref,
    query_ref,
    triple_hbm,
    turned_ref,
    spread_ref,
    keys_ref,
    hat_rows_ref,
    s_weight,
    s_turn,
    sems,
):
    pairs, tokens, full_width, full_hidden = dims
    is_text, width, mask = tower_sizes(full_width, full_hidden)
    get_weight = fetch(triple_hbm.at[0, 1], s_weight, sems.at[0])
    rows = probs_ref.shape[0]
    low = probs_ref[...]
    spread = mm(low, hat_ref[...])
    spread_ref[...] = spread.astype(BF16)
    total = jnp.sum(low.astype(F32), axis=1, keepdims=True)
    s_turn[rows:, :] = jnp.zeros((s_turn.shape[0] - rows, full_width), F32)
    s_turn[0:rows, :] = (spread * ag[...] + total * ab[...]) * mask
    turned_ref[...] = s_turn[...].T.astype(BF16)
    pick = one_hot(iota((pairs, tokens), 1).astype(F32) == pooled_spots(ends_ref, is_text, pairs, 1))
    hat_rows_ref[...] = mm(pick, hat_ref[...]).astype(BF16)
    wide = mm(repeat_rows(rows, pairs), query_ref[...])
    wide = jnp.where(head_mask(rows, pairs, full_width), wide, 0.0).astype(BF16)
    get_weight.wait()
    keys_ref[...] = mm_nt(wide, s_weight[...]).astype(BF16)


def in_order(pieces, stages, pairs, block, at):
    here = lax.axis_index("dp")
    row = at + iota((block, 1), 0)
    owner = lax.div(row, pairs)
    apart = lax.bitwise_xor(owner, here)
    place = jnp.zeros_like(owner)
    weight = 1
    for shift, bits in stages:
        digit = lax.bitwise_and(lax.shift_right_logical(apart, shift), (1 << bits) - 1)
        place = place + digit * weight
        weight = weight << bits
    column = place * pairs + row - owner * pairs
    total = None
    first = 0
    for piece in pieces:
        count = piece.shape[0]
        part = mm(one_hot(iota((block, count), 1) + first == column), piece[...])
        total = part if total is None else total + part
        first += count
    return total.astype(BF16)


def over_blocks(count, step):
    if count == 1:
        step(0)
    else:

        def one(index, carry):
            step(index)
            return carry

        lax.fori_loop(0, count, one, 0)


def block_rows(total):
    return 320 if total % 320 == 0 else total


def loss_kernel(
    dims,
    own_rel,
    other_rel,
    flags_ref,
    logit_scale,
    loss_scale,
    ag,
    ab,
    triple_hbm,
    triple_bias,
    wo_hbm,
    fg,
    ww_hbm,
    wn_hbm,
    lg,
    we_hbm,
    hat_hbm,
    probs_hbm,
    spread_ref,
    keys_ref,
    embedded_ref,
    pooled_ref,
    middle_ref,
    slope_ref,
    hat_rows_ref,
    loss_ref,
    hits_ref,
    scale_ref,
    grad_all_ref,
    late_ref,
    queries_ref,
    back_ref,
    values_ref,
    rows_one_ref,
    rows_mid_ref,
    s_own,
    s_other,
    s_triple,
    s_wo,
    s_ww,
    s_wn,
    s_we,
    s_hat,
    s_probs,
    s_rows,
    s_two,
    s_turn,
    s_slab,
    sems,
    hidden_sems,
):
    pairs, tokens, full_width, full_hidden, stages = dims
    all_pairs = own_rel.shape[0]
    block = block_rows(all_pairs)
    here = lax.axis_index("dp")
    is_text, width, mask = tower_sizes(full_width, full_hidden)
    rows = full_width // HEAD * pairs
    get_we = fetch(we_hbm.at[0], s_we, sems.at[0])
    hidden = Hidden(ww_hbm, wn_hbm, s_ww, s_wn, hidden_sems, full_hidden // CHUNK)
    hidden.start((1, 0))
    get_wo = fetch(wo_hbm.at[0], s_wo, sems.at[1])
    get_triple = fetch(triple_hbm.at[0], s_triple, sems.at[2])
    get_hat = fetch(hat_hbm, s_hat, sems.at[3])
    get_probs = fetch(probs_hbm, s_probs, sems.at[4])

    def place(index):
        at = pl.multiple_of(index * block, block)
        s_own[pl.ds(at, block), :] = in_order([own_rel], stages, pairs, block, at)
        s_other[pl.ds(at, block), :] = in_order([other_rel], stages, pairs, block, at)

    over_blocks(all_pairs // block, place)
    live = (flags_ref[...] > 0).astype(F32)
    live_pairs = jnp.sum(live, axis=1, keepdims=True)
    factor = jnp.exp(logit_scale[...])
    row_weight = loss_scale[...] / (2.0 * live_pairs)
    loss_ref[...] = jnp.zeros_like(loss_ref)
    hits_ref[...] = jnp.zeros_like(hits_ref)
    scale_ref[...] = jnp.zeros_like(scale_ref)
    grad_all_ref[...] = jnp.zeros_like(grad_all_ref)

    def part(index):
        at = pl.multiple_of(index * block, block)
        eye = at + iota((block, all_pairs), 0) == iota((block, all_pairs), 1)
        live_rows = jnp.sum(jnp.where(eye, live, 0.0), axis=1, keepdims=True)

        def one_way(left, right):
            logits = mm_nt(left, right) * factor
            masked = jnp.where(live > 0.5, logits, -1e30)
            peak = jnp.max(masked, axis=1, keepdims=True)
            powers = jnp.exp(masked - peak)
            total = jnp.sum(powers, axis=1, keepdims=True)
            log_total = peak + jnp.log(total)
            matched = jnp.sum(jnp.where(eye, logits, 0.0), axis=1, keepdims=True)
            gap = jnp.where(live_rows > 0.5, log_total - matched, 0.0)
            grads = (
                (powers / total - eye.astype(F32)) * (live_rows * row_weight)
            ).astype(BF16)
            loss = jnp.sum(live_rows * gap, axis=0, keepdims=True)
            hits = jnp.sum(live_rows * jnp.exp(-gap), axis=0, keepdims=True)
            scale = jnp.sum(
                jnp.sum(grads.astype(F32) * logits, axis=1, keepdims=True),
                axis=0,
                keepdims=True,
            )
            return grads, loss, hits, scale

        own = s_own[pl.ds(at, block), :]
        other = s_other[pl.ds(at, block), :]
        grads, loss_one, hits_one, scale_one = one_way(own, s_other[...])
        grad_all_ref[pl.ds(at, block), :] += factor * mm(grads, s_other[...])
        grads, loss_two, hits_two, scale_two = one_way(other, s_own[...])
        grad_all_ref[...] += factor * mm_tn(grads, other)
        loss_ref[...] += loss_one + loss_two
        hits_ref[...] += hits_one + hits_two
        scale_ref[...] += scale_one + scale_two

    over_blocks(all_pairs // block, part)
    loss_ref[...] = loss_ref[...] / (2.0 * live_pairs)
    hits_ref[...] = hits_ref[...] / (2.0 * live_pairs)

    for pair in range(pairs):
        s_rows[pair : pair + 1, :] = grad_all_ref[pl.ds(here * pairs + pair, 1), :]

    gain, shift = ag[...] * mask, ab[...] * mask
    grad_embed = embed_back(embedded_ref[...], s_rows[...])
    get_we.wait()
    grad_three = mm_nt(grad_embed, s_we[...])
    out_hat, out_inv = normed(pooled_ref[...], mask, width)
    grad_pooled = norm_back(out_hat, out_inv, lg[...] * mask, grad_three, mask, width)
    branch = grad_pooled.astype(BF16)
    s_two[...] = jnp.zeros_like(s_two)

    def backward(at):
        grad_active = mm_nt(branch, s_wn[at, :])
        grad_hidden = (grad_active * slope_ref[:, at]).astype(BF16)
        s_two[...] += mm_nt(grad_hidden, s_ww[:, at])

    hidden.each(backward)
    mid_hat, mid_inv = normed(middle_ref[...], mask, width)
    grad_two = s_two[...] * mask
    grad_middle = grad_pooled + norm_back(mid_hat, mid_inv, fg[...] * mask, grad_two, mask, width)
    rows_mid_ref[...] = grad_middle
    attention = grad_middle.astype(BF16)
    get_wo.wait()
    grad_mixed = (mm_nt(attention, s_wo[...]) * mask).astype(BF16)
    repeat = repeat_rows(rows, pairs)
    heads = head_mask(rows, pairs, full_width)
    wide = jnp.where(heads, mm(repeat, grad_mixed), 0.0)
    get_triple.wait()
    along = mm_nt(wide.astype(BF16), s_triple[2])
    values_low = along.astype(BF16)
    values_ref[...] = values_low
    offset = jnp.sum(along * shift, axis=1, keepdims=True) + jnp.sum(
        wide * triple_bias[0, 1:2, :], axis=1, keepdims=True
    )
    get_hat.wait()
    get_probs.wait()
    grad_probs = mm_nt((along * gain).astype(BF16), s_hat[...]) + offset
    probs = s_probs[...].astype(F32)
    prob_total = jnp.sum(probs, axis=1, keepdims=True)
    inner = jnp.sum(grad_probs * probs, axis=1, keepdims=True) / prob_total
    back = (probs * (grad_probs - inner)).astype(BF16)
    back_ref[...] = back
    spread = mm(back, s_hat[...])
    total = jnp.sum(back.astype(F32), axis=1, keepdims=True)
    means = (spread * gain + total * shift).astype(BF16)
    query_wide = mm(means, s_triple[1]) * 0.125
    grad_query = mm_tn(repeat, jnp.where(heads, query_wide, 0.0).astype(BF16)).astype(BF16)
    queries_ref[...] = grad_query
    rows_one = mm_nt(grad_query, s_triple[0]) * mask
    rows_one_ref[...] = rows_one
    values_wide = values_low.astype(F32)
    keys_wide = keys_ref[...].astype(F32)
    gain_sum = (
        sums_of(values_wide * spread_ref[...].astype(F32))
        + sums_of(keys_wide * spread)
        + sums_of(rows_one * hat_rows_ref[...].astype(F32))
    ) * mask
    shift_sum = (
        sums_of(values_wide * prob_total) + sums_of(keys_wide * total) + sums_of(rows_one)
    ) * mask
    s_turn[rows:, :] = jnp.zeros((s_turn.shape[0] - rows, full_width), F32)
    s_turn[0:rows, :] = means.astype(F32)
    slot = rows
    for vector in (gain_sum, shift_sum):
        for _ in range(3):
            low = vector.astype(BF16).astype(F32)
            s_turn[slot : slot + 1, :] = low
            vector = vector - low
            slot += 1
    lanes = s_turn.shape[0]
    late_ref[:, 0:lanes] = s_turn[...].T.astype(BF16)
    if late_ref.shape[1] > lanes:
        turned = grad_query.astype(F32).T
        slab = s_slab.shape[0]
        s_slab[...] = jnp.zeros_like(s_slab)
        for place in range(full_width // slab):
            down = slice(place * slab, (place + 1) * slab)
            s_slab[:, place * pairs : (place + 1) * pairs] = turned[down, :]
        slab_low = s_slab[...].astype(BF16)
        for place in range(full_width // slab):
            late_ref[place * slab : (place + 1) * slab, lanes:] = slab_low


def rows_kernel(dims, *refs):
    pairs, tokens, full_width, full_hidden, slice_width, slice_hidden, stages, pieces = dims
    early_hbm = refs[:pieces]
    (
        ends_ref,
        hat_hbm,
        inv_hbm,
        probs_hbm,
        back_ref,
        value_factors_ref,
        keys_ref,
        rows_one_ref,
        rows_mid_ref,
        means_ref,
        grad_hbm,
        ag,
        ab,
        triple_hbm,
        triple_bias,
        wo_hbm,
        bo,
        fg,
        fb,
        ww_hbm,
        bw,
        wn_hbm,
        lg,
        lb,
        we_hbm,
        out_hbm,
        ones_ref,
        queries_ref,
        values_ref,
        embed_ref,
        narrow_ref,
        widen_ref,
        mixer_ref,
        final_gain_ref,
        final_bias_ref,
        feed_gain_ref,
        feed_bias_ref,
        narrow_bias_ref,
        mixer_bias_ref,
        value_bias_ref,
        widen_bias_ref,
        value_weight_ref,
        s_triple,
        s_wo,
        s_ww,
        s_wn,
        s_we,
        s_vectors,
        s_hat,
        s_inv,
        s_left,
        s_right,
        s_early,
        grad_ref,
        s_out,
        s_total,
        s_active,
        s_hidden,
        s_means,
        sems,
        hidden_sems,
        out_sems,
    ) = refs[pieces:]
    all_pairs = grad_ref.shape[0]
    block = block_rows(all_pairs)
    here = lax.axis_index("dp")
    is_text, width, mask = tower_sizes(full_width, full_hidden)
    get_probs = fetch(probs_hbm, s_left.at[pl.ds(0, full_width // HEAD * pairs), :], sems.at[3])
    get_hat = fetch(hat_hbm, s_hat, sems.at[4])
    get_inv = fetch(inv_hbm, s_inv, sems.at[5])
    get_grad = fetch(grad_hbm, grad_ref, sems.at[6])
    height = s_early.shape[0] // pieces
    early = [s_early.at[pl.ds(place * height, height), :] for place in range(pieces)]
    get_early = [fetch(early_hbm[place], early[place], sems.at[7 + place]) for place in range(pieces)]
    get_wo = fetch(wo_hbm.at[0], s_wo, sems.at[1])
    get_we = fetch(we_hbm.at[0], s_we, sems.at[2])
    hidden = Hidden(ww_hbm, wn_hbm, s_ww, s_wn, hidden_sems, full_hidden // CHUNK)
    hidden.start((0, 1))
    get_triple = fetch(triple_hbm.at[0, 0], s_triple, sems.at[0])
    rows = full_width // HEAD * pairs
    token_gain = ag[...] * mask
    s_left[rows : 2 * rows, :] = back_ref[...]
    s_right[0:rows, :] = value_factors_ref[...]
    s_right[rows : 2 * rows, :] = keys_ref[...]
    spots = pooled_spots(ends_ref, is_text, pairs, 3)
    s_left[2 * rows :, :] = one_hot(iota((3 * pairs, tokens), 1).astype(F32) == spots)
    s_right[2 * rows :, :] = three_parts(rows_one_ref[...])
    middle_parts = three_parts(rows_mid_ref[...])
    ones = one_hot(iota((full_width, 128), 0).astype(F32) < width)
    get_probs.wait()
    get_hat.wait()
    get_inv.wait()

    def put(at, count):
        spot = pl.ds(at, count)
        return pltpu.make_async_copy(
            s_out.at[spot, :], out_hbm.at[0, spot, :], out_sems.at[at // NORM_ROWS]
        )

    def norm_rows(at, count):
        spot = pl.ds(at, count)
        upward = mm_tn(s_left[:, spot], s_right[...])
        hat = s_hat[spot, :].astype(F32)
        scaled = upward * token_gain
        mean = mm(scaled.astype(BF16), ones) / width
        along = mm((scaled * hat).astype(BF16), ones) / width
        s_out[spot, :] = across(s_inv[spot, :], full_width) * (
            scaled - (across(mean, full_width) + hat * across(along, full_width)) * mask
        ) + mm_tn(s_left[2 * rows :, spot], middle_parts)
        put(at, count).start()

    over_tokens(tokens, NORM_ROWS, norm_rows)
    for ref in (embed_ref, narrow_ref, widen_ref, mixer_ref, widen_bias_ref, s_vectors):
        ref[...] = jnp.zeros_like(ref)
    lane = iota((full_width, slice_width), 0)
    pick = one_hot(
        (lane == here * slice_width + iota((full_width, slice_width), 1))
        & (lane.astype(F32) < width)
    )
    hidden_width = jnp.where(is_text, MLP_TXT, full_hidden)
    gain, shift = lg[...] * mask, lb[...] * mask
    feed_gain = fg[...] * mask
    get_wo.wait()
    get_we.wait()
    get_grad.wait()
    for copy in get_early:
        copy.wait()

    def part(index):
        at = pl.multiple_of(index * block, block)
        here_rows = pl.ds(at, block)
        arrived = in_order(early, stages, pairs, block, at)
        mixed = arrived[:, 0:full_width]
        stream_rows = arrived[:, full_width : 2 * full_width].astype(F32)
        out_hat = arrived[:, 2 * full_width : 3 * full_width].astype(F32)
        out_inv = jnp.sum(arrived[:, 3 * full_width :].astype(F32), axis=1, keepdims=True)
        three = (out_hat * gain + shift).astype(BF16)
        grad_embed = embed_back(mm(three, s_we[...]), grad_ref[here_rows, :])
        embed_ref[0] += mm_tn(mm(three, pick).astype(BF16), grad_embed)
        grad_three = mm_nt(grad_embed, s_we[...])
        s_vectors[0:1, :] += sums_of(grad_three * out_hat)
        s_vectors[1:2, :] += sums_of(grad_three)
        grad_pooled = norm_back(out_hat, out_inv, gain, grad_three, mask, width)
        branch = grad_pooled.astype(BF16)
        s_vectors[2:3, :] += sums_of(branch.astype(F32))
        middle = stream_rows + mm(mixed, s_wo[...]) + bo[...]
        mid_hat, mid_inv = normed(middle, mask, width)
        two = ((mid_hat * fg[...] + fb[...]) * mask).astype(BF16)
        s_total[...] = jnp.zeros_like(s_total)
        s_active[...] = jnp.zeros_like(s_active)
        s_hidden[...] = jnp.zeros_like(s_hidden)

        def through(chunk, carry):
            first = pl.multiple_of(chunk * CHUNK, CHUNK)
            lanes = pl.ds(first, CHUNK)
            if all_pairs == block:
                hidden.wait(chunk)
            pre = mm(two, s_ww[:, lanes]) + bw[:, lanes]
            gate = sigmoid(1.702 * pre)
            active = pre * gate
            there = (first + iota((1, CHUNK), 1) < hidden_width).astype(F32)
            slope = (gate + 1.702 * active * (1.0 - gate)) * there
            grad_hidden = (mm_nt(branch, s_wn[lanes, :]) * slope).astype(BF16)
            s_total[...] += mm_nt(grad_hidden, s_ww[:, lanes])
            row = first + iota((CHUNK, slice_hidden), 0)
            chosen = one_hot(
                (row == here * slice_hidden + iota((CHUNK, slice_hidden), 1))
                & (row < hidden_width)
            )
            s_active[...] += mm(active.astype(BF16), chosen)
            s_hidden[...] += mm(grad_hidden, chosen)
            return carry

        lax.fori_loop(0, full_hidden // CHUNK, through, 0)
        grad_two, active_slice, hidden_slice = s_total[...], s_active[...], s_hidden[...]
        narrow_ref[0] += mm_tn(active_slice.astype(BF16), branch)
        widen_ref[0] += mm_tn(hidden_slice.astype(BF16), two)
        widen_bias_ref[...] += sums_of(hidden_slice)
        s_vectors[3:4, :] += sums_of(grad_two * mid_hat)
        s_vectors[4:5, :] += sums_of(grad_two)
        grad_middle = grad_pooled + norm_back(mid_hat, mid_inv, feed_gain, grad_two, mask, width)
        attention = grad_middle.astype(BF16)
        s_vectors[5:6, :] += sums_of(attention.astype(F32))
        mixer_ref[0] += mm_tn(mm(mixed, pick).astype(BF16), attention)
        grad_mixed = (mm_nt(attention, s_wo[...]) * mask).astype(BF16)
        values_ref[here_rows, :] = grad_mixed
        s_vectors[6:7, :] += sums_of(grad_mixed.astype(F32))
        rows_hat, _ = normed(stream_rows, mask, width)
        one = ((rows_hat * ag[...] + ab[...]) * mask).astype(BF16)
        ones_ref[here_rows, :] = mm(one, pick).astype(BF16)
        if all_pairs == block:
            get_triple.wait()
        query = (mm(one, s_triple[...]) + triple_bias[0, 0:1, :]) * mask
        queries_ref[here_rows, :] = query.astype(BF16)

    if all_pairs != block:
        get_triple.wait()
        for chunk in range(full_hidden // CHUNK):
            hidden.wait(chunk)
    over_blocks(all_pairs // block, part)
    over_tokens(tokens, NORM_ROWS, lambda at, count: put(at, count).wait())
    count = means_ref.shape[0]
    if count <= 16 and slice_width % 16 == 0:
        from_heads(
            [means_ref.at[source] for source in range(count)],
            values_ref,
            value_weight_ref,
            s_means,
            pairs,
            slice_width,
        )
    vectors = dot_dims(s_vectors[...], pick.astype(F32), 1, 0, lax.Precision.HIGHEST)
    for slot, ref in enumerate(
        (
            final_gain_ref,
            final_bias_ref,
            narrow_bias_ref,
            feed_gain_ref,
            feed_bias_ref,
            mixer_bias_ref,
            value_bias_ref,
        )
    ):
        ref[...] = vectors[slot : slot + 1, :]


def from_heads(sources, right_ref, out_ref, s_left, pairs, slice_width):
    heads = right_ref.shape[1] // HEAD
    for head in range(heads):
        down = slice(head * slice_width, (head + 1) * slice_width)
        lane = slice(head * pairs, (head + 1) * pairs)
        s_left[down, :] = jnp.concatenate([source[:, lane] for source in sources], axis=1)
    left = iota((slice_width, 2 * HEAD), 1) < HEAD
    for two in range(heads // 2):
        down = slice(two * 2 * slice_width, (two + 1) * 2 * slice_width)
        lane = slice(two * 2 * HEAD, (two + 1) * 2 * HEAD)
        both = mm(s_left[down, :], right_ref[:, lane])
        out_ref[:, lane] = jnp.where(left, both[0:slice_width], both[slice_width:])


def last_kernel(dims, *refs):
    pairs, full_width, full_hidden, slice_width, stages, pieces = dims
    arrived = refs[:pieces]
    (
        late_ref,
        means_ref,
        ones_ref,
        queries_ref,
        values_ref,
        value_bias_ref,
        value_weight_ref,
        triple_ref,
        gain_ref,
        shift_ref,
        bias_ref,
        s_keys,
        s_turned,
        s_late,
        s_sums,
    ) = refs[pieces:]
    here = lax.axis_index("dp")
    count = late_ref.shape[0]
    lanes = -(-(full_width // HEAD * pairs + 12) // 128) * 128
    heads = full_width // HEAD
    rows = heads * pairs
    all_pairs = queries_ref.shape[0]
    s_late[...] = jnp.zeros_like(s_late)
    if not arrived:
        sources = range(count)
        for source in sources:
            s_late[...] += late_ref[source, :, 0:lanes].astype(F32)
        from_heads(
            [late_ref.at[source] for source in sources],
            queries_ref,
            triple_ref.at[0, 1],
            s_keys,
            pairs,
            slice_width,
        )
        triple_ref[0, 1] = triple_ref[0, 1] * 0.125
        triple_ref[0, 2] = value_weight_ref[...]
        for slab in sources:
            down = slice(slab * slice_width, (slab + 1) * slice_width)
            lane = slice(lanes + slab * pairs, lanes + (slab + 1) * pairs)
            s_turned[down, :] = jnp.concatenate([late_ref[source, :, lane] for source in sources], axis=1)
        triple_ref[0, 0] = mm(s_turned[...], ones_ref[...]).T
        mine = s_turned[pl.ds(pl.multiple_of(here * slice_width, slice_width), slice_width), :]
        sums = mm_nt(jnp.ones((8, all_pairs), BF16), mine)
    else:
        block = block_rows(all_pairs)
        triple_ref[...] = jnp.zeros_like(triple_ref)
        s_sums[...] = jnp.zeros_like(s_sums)

        def part(index):
            at = pl.multiple_of(index * block, block)
            grad_query = in_order(arrived, stages, pairs, block, at)
            triple_ref[0, 0] += mm_tn(ones_ref[pl.ds(at, block), :], grad_query)
            s_sums[0:1, :] += sums_of(grad_query.astype(F32))

        over_blocks(all_pairs // block, part)
        head = head_mask(lanes, pairs, full_width)

        def one(source, carry):
            now = late_ref[source]
            s_late[...] += now.astype(F32)
            row = iota((lanes, all_pairs), 0)
            column = iota((lanes, all_pairs), 1)
            repeat = one_hot((column == source * pairs + lax.rem(row, pairs)) & (row < rows))
            means = means_ref[source]
            for which, left, origin in ((1, now, queries_ref), (2, means, values_ref)):
                wide = jnp.where(head, mm(repeat, origin[...]), 0.0).astype(BF16)
                triple_ref[0, which] += mm(left, wide)
            return carry

        lax.fori_loop(0, count, one, 0)
        triple_ref[0, 1] = triple_ref[0, 1] * 0.125
        pick = (
            iota((full_width, slice_width), 0)
            == here * slice_width + iota((full_width, slice_width), 1)
        ).astype(F32)
        sums = dot_dims(s_sums[...], pick, 1, 0, lax.Precision.HIGHEST)
    lane = iota((8, lanes), 1)
    row = iota((8, lanes), 0)
    slot = rows + row * 3
    chosen = ((lane >= slot) & (lane < slot + 3) & (row < 2)).astype(F32)
    from_late = dot_dims(chosen, s_late[...], 1, 1, lax.Precision.HIGHEST)
    gain_ref[...] = from_late[0:1, :]
    shift_ref[...] = from_late[1:2, :]
    bias_ref[0, 0:1, :] = sums[0:1, :]
    bias_ref[0, 1:2, :] = value_bias_ref[...]


def stages_of(count):
    bits = count.bit_length() - 1
    stages = []
    while bits > 0:
        take = 2 if bits >= 2 else 1
        bits -= take
        stages.append((bits, take))
    return tuple(stages)


def exchange(block, axis, stage):
    count = lax.axis_size(axis)
    shift, bits = stage
    parts = [block]
    for apart in range(1, 1 << bits):
        route = [(low, low ^ (apart << shift)) for low in range(count)]
        parts.append(lax.ppermute(block, axis, route))
    return parts


def call(
    kernel, ins, outs, scratch, in_hbm=(), out_hbm=(), cost=None, kept=(), limit=VMEM_LIMIT
):
    vmem = pl.BlockSpec(memory_space=pltpu.VMEM)
    anywhere = pl.BlockSpec(memory_space=pl.ANY)
    specs = [anywhere if index in in_hbm else vmem for index in range(len(ins))]
    out_specs = [anywhere if index in out_hbm else vmem for index in range(len(outs))]
    if kept:
        ins = [
            pltpu.with_memory_space_constraint(
                array, pltpu.VMEM if index in kept else pltpu.HBM
            )
            for index, array in enumerate(ins)
        ]
    flops, moved = cost
    return pl.pallas_call(
        kernel,
        out_shape=[jax.ShapeDtypeStruct(shape, kind) for shape, kind in outs],
        in_specs=specs,
        out_specs=out_specs,
        scratch_shapes=scratch,
        compiler_params=pltpu.CompilerParams(vmem_limit_bytes=limit),
        cost_estimate=pl.CostEstimate(flops=flops, bytes_accessed=moved, transcendentals=0),
    )(*ins)


def body(
    block_input,
    segments,
    caption_ends,
    pair_flags,
    attention_gain,
    attention_bias,
    triple_weight,
    triple_bias,
    mixer_weight,
    mixer_bias,
    feed_gain,
    feed_bias,
    widen_weight,
    widen_bias,
    narrow_weight,
    narrow_bias,
    final_gain,
    final_bias,
    embed_weight,
    logit_scale,
    loss_scale,
):
    tokens, width = block_input.shape[1:]
    hidden = widen_weight.shape[2]
    emb = embed_weight.shape[2]
    pairs = caption_ends.shape[0]
    count = lax.axis_size("dp")
    all_pairs = pair_flags.shape[0]
    heads = width // HEAD
    rows = heads * pairs
    lanes = -(-(rows + 12) // 128) * 128
    slice_width = width // count
    slice_hidden = hidden // count
    stages = stages_of(count)
    compact = count <= 16 and slice_width % 16 == 0
    slab_lanes = -(-all_pairs // 128) * 128
    ends = caption_ends.reshape(1, pairs)
    dma = pltpu.SemaphoreType.DMA
    weights_scratch = [
        pltpu.VMEM((3, width, width), BF16),
        pltpu.VMEM((width, width), BF16),
        pltpu.VMEM((width, hidden), BF16),
        pltpu.VMEM((hidden, width), BF16),
        pltpu.VMEM((width, emb), BF16),
    ]
    dims = (pairs, tokens, width, hidden)
    chunk_count = hidden // CHUNK
    (
        unit,
        early,
        hat,
        invert,
        probs,
        query,
        embedded,
        pooled,
        middle,
        slope,
    ) = call(
        partial(attend_kernel, dims),
        (
            ends,
            block_input,
            attention_gain,
            attention_bias,
            triple_weight,
            triple_bias,
            mixer_weight,
            mixer_bias,
            feed_gain,
            feed_bias,
            widen_weight,
            widen_bias,
            narrow_weight,
            narrow_bias,
            final_gain,
            final_bias,
            embed_weight,
        ),
        [
            ((pairs, emb), BF16),
            ((pairs, 3 * width + 128), BF16),
            ((tokens, width), BF16),
            ((tokens, 128), F32),
            ((rows, tokens), BF16),
            ((pairs, width), BF16),
            ((pairs, emb), F32),
            ((pairs, width), F32),
            ((pairs, width), F32),
            ((pairs, hidden), F32),
        ],
        [
            pltpu.VMEM((tokens, width), BF16),
            pltpu.VMEM((tokens, width), BF16),
            pltpu.VMEM((tokens, width), BF16),
            pltpu.VMEM((tokens, 128), F32),
            pltpu.VMEM((rows, tokens), F32),
            pltpu.VMEM((tokens, width), BF16),
            pltpu.VMEM((tokens, width), BF16),
        ]
        + weights_scratch
        + [
            pltpu.VMEM((rows, tokens), BF16),
            dma((7,)),
            dma((2, chunk_count)),
        ],
        in_hbm=(1, 4, 6, 10, 12, 16),
        out_hbm=(2, 3, 4),
        cost=(10**9, 20 * 10**6),
    )
    turned, spread, keys, hat_rows = call(
        partial(means_kernel, dims),
        (ends, attention_gain, attention_bias, hat, probs, query, triple_weight),
        [
            ((width, lanes), BF16),
            ((rows, width), BF16),
            ((rows, width), BF16),
            ((pairs, width), BF16),
        ],
        [
            pltpu.VMEM((width, width), BF16),
            pltpu.VMEM((lanes, width), F32),
            dma((1,)),
        ],
        in_hbm=(6,),
        cost=(10**9, 5 * 10**6),
    )
    early_rows, own_rel = early, unit
    flags = pair_flags.reshape(1, all_pairs)
    for index, stage in enumerate(stages):
        own_parts = exchange(own_rel, "dp", stage)
        if index + 1 < len(stages):
            own_parts, early_rows, turned, spread, keys, hat_rows = lax.optimization_barrier(
                (own_parts, early_rows, turned, spread, keys, hat_rows)
            )
            early_rows = jnp.concatenate(exchange(early_rows, "dp", stage), axis=0)
        own_rel = jnp.concatenate(own_parts, axis=0)
    means_all = lax.all_to_all(turned, "dp", 0, 0, tiled=True).reshape(count, slice_width, lanes)
    other_rel = lax.ppermute(own_rel, "tower", [(0, 1), (1, 0)])
    early_pieces = exchange(early_rows, "dp", stages[-1])
    (
        loss,
        hits,
        scale,
        grad_all,
        late,
        queries,
        back,
        values,
        rows_one,
        rows_mid,
    ) = call(
        partial(loss_kernel, dims + (stages,)),
        (
            own_rel,
            other_rel,
            flags,
            logit_scale.reshape(1, 1),
            loss_scale.reshape(1, 1),
            attention_gain,
            attention_bias,
            triple_weight,
            triple_bias,
            mixer_weight,
            feed_gain,
            widen_weight,
            narrow_weight,
            final_gain,
            embed_weight,
            hat,
            probs,
            spread,
            keys,
            embedded,
            pooled,
            middle,
            slope,
            hat_rows,
        ),
        [
            ((1, 1), F32),
            ((1, 1), F32),
            ((1, 1), F32),
            ((all_pairs, emb), F32),
            ((width, lanes + (slab_lanes if compact else 0)), BF16),
            ((pairs, width), BF16),
            ((rows, tokens), BF16),
            ((rows, width), BF16),
            ((pairs, width), F32),
            ((pairs, width), F32),
        ],
        [pltpu.VMEM((all_pairs, emb), BF16), pltpu.VMEM((all_pairs, emb), BF16)]
        + weights_scratch
        + [
            pltpu.VMEM((tokens, width), BF16),
            pltpu.VMEM((rows, tokens), BF16),
            pltpu.VMEM((pairs, emb), F32),
            pltpu.VMEM((pairs, width), F32),
            pltpu.VMEM((lanes, width), F32),
            pltpu.VMEM((slice_width, slab_lanes), F32),
            dma((5,)),
            dma((2, chunk_count)),
        ],
        in_hbm=(7, 9, 11, 12, 14, 15, 16),
        cost=(10**9, 20 * 10**6),
    )
    early_pieces, late, queries = lax.optimization_barrier((early_pieces, late, queries))
    late_all = lax.all_to_all(late, "dp", 0, 0, tiled=True)
    late_all = late_all.reshape(count, slice_width, late.shape[1])
    late_pieces = []
    if not compact:
        late_pieces = [queries]
        for stage in stages:
            late_pieces = exchange(jnp.concatenate(late_pieces, axis=0), "dp", stage)
    ahead = len(early_pieces)
    vector = ((1, slice_width), F32)
    (
        block_grad,
        ones,
        query_rows,
        value_rows,
        grad_embed,
        grad_narrow,
        grad_widen,
        grad_mixer,
        grad_final_gain,
        grad_final_bias,
        grad_feed_gain,
        grad_feed_bias,
        grad_narrow_bias,
        grad_mixer_bias,
        grad_value_bias,
        grad_widen_bias,
        grad_value_weight,
    ) = call(
        partial(
            rows_kernel,
            (pairs, tokens, width, hidden, slice_width, slice_hidden, stages, ahead),
        ),
        tuple(early_pieces)
        + (
            ends,
            hat,
            invert,
            probs,
            back,
            values,
            keys,
            rows_one,
            rows_mid,
            means_all,
            grad_all,
            attention_gain,
            attention_bias,
            triple_weight,
            triple_bias,
            mixer_weight,
            mixer_bias,
            feed_gain,
            feed_bias,
            widen_weight,
            widen_bias,
            narrow_weight,
            final_gain,
            final_bias,
            embed_weight,
        ),
        [
            ((1, tokens, width), F32),
            ((all_pairs, slice_width), BF16),
            ((all_pairs, width), BF16),
            ((all_pairs, width), BF16),
            ((1, slice_width, emb), F32),
            ((1, slice_hidden, width), F32),
            ((1, slice_hidden, width), F32),
            ((1, slice_width, width), F32),
        ]
        + [vector] * 7
        + [((1, slice_hidden), F32), ((slice_width, width), F32)],
        [pltpu.VMEM((width, width), BF16)]
        + weights_scratch[1:]
        + [
            pltpu.VMEM((8, width), F32),
            pltpu.VMEM((tokens, width), BF16),
            pltpu.VMEM((tokens, 128), F32),
            pltpu.VMEM((2 * rows + 3 * pairs, tokens), BF16),
            pltpu.VMEM((2 * rows + 3 * pairs, width), BF16),
            pltpu.VMEM((all_pairs, 3 * width + 128), BF16),
            pltpu.VMEM((all_pairs, emb), F32),
            pltpu.VMEM((tokens, width), F32),
            pltpu.VMEM((block_rows(all_pairs), width), F32),
            pltpu.VMEM((block_rows(all_pairs), slice_hidden), F32),
            pltpu.VMEM((block_rows(all_pairs), slice_hidden), F32),
            pltpu.VMEM((width // HEAD * slice_width if compact else 16, all_pairs), BF16),
            dma((7 + ahead,)),
            dma((2, chunk_count)),
            dma((-(-tokens // NORM_ROWS),)),
        ],
        in_hbm=tuple(range(ahead)) + tuple(ahead + index for index in (1, 2, 3, 10, 13, 15, 19, 21, 24)),
        out_hbm=(0,),
        cost=(3 * 10**9, 10 * 10**6),
    )
    grad_triple, grad_gain, grad_bias, grad_triple_bias = call(
        partial(last_kernel, (pairs, width, hidden, slice_width, stages, len(late_pieces))),
        tuple(late_pieces)
        + (late_all, means_all, ones, query_rows, value_rows, grad_value_bias, grad_value_weight),
        [
            ((1, 3, slice_width, width), F32),
            vector,
            vector,
            ((1, 2, slice_width), F32),
        ],
        [
            pltpu.VMEM((width // HEAD * slice_width, all_pairs), BF16),
            pltpu.VMEM((width, all_pairs), BF16),
            pltpu.VMEM((slice_width, lanes), F32),
            pltpu.VMEM((8, width), F32),
        ],
        cost=(10**9, 10 * 10**6),
        in_hbm=(1, 4) if compact else (),
        kept=(0,) if compact else (),
        limit=32 * 1024 * 1024 if compact else VMEM_LIMIT,
    )
    return (
        loss[0, 0],
        hits[0, 0],
        block_grad,
        grad_gain,
        grad_bias,
        grad_triple,
        grad_triple_bias,
        grad_mixer,
        grad_mixer_bias,
        grad_feed_gain,
        grad_feed_bias,
        jnp.swapaxes(grad_widen, 1, 2),
        grad_widen_bias,
        grad_narrow,
        grad_narrow_bias,
        grad_final_gain,
        grad_final_bias,
        grad_embed,
        scale[0, 0],
    )


def solution(mesh):
    in_specs = (
        P("tower", "dp", None),
        P("dp", None),
        P("dp"),
        P(),
        P("tower", None),
        P("tower", None),
        P("tower", None, None, None),
        P("tower", None, None),
        P("tower", None, None),
        P("tower", None),
        P("tower", None),
        P("tower", None),
        P("tower", None, None),
        P("tower", None),
        P("tower", None, None),
        P("tower", None),
        P("tower", None),
        P("tower", None),
        P("tower", None, None),
        P(),
        P(),
    )
    out_specs = (
        P(),
        P(),
        P("tower", "dp", None),
        P("tower", "dp"),
        P("tower", "dp"),
        P("tower", None, "dp", None),
        P("tower", None, "dp"),
        P("tower", "dp", None),
        P("tower", "dp"),
        P("tower", "dp"),
        P("tower", "dp"),
        P("tower", None, "dp"),
        P("tower", "dp"),
        P("tower", "dp", None),
        P("tower", "dp"),
        P("tower", "dp"),
        P("tower", "dp"),
        P("tower", "dp", None),
        P(),
    )
    return jax.shard_map(body, mesh=mesh, in_specs=in_specs, out_specs=out_specs, check_vma=False)
```

```python
from functools import partial

import jax
import jax.numpy as jnp
from jax import lax
from jax.experimental import pallas as pl
from jax.experimental.pallas import tpu as pltpu
from jax.sharding import PartitionSpec as P

D_TXT = 512
MLP_TXT = 2048
HEAD = 64
IMG_TOK = 50
CTX = 77
F32 = jnp.float32
BF16 = jnp.bfloat16
VMEM_LIMIT = 62 * 1024 * 1024
CHUNK = 1024
NORM_ROWS = 272
STREAM_ROWS = 544
PROJECT_ROWS = 1088


def dot_dims(left, right, left_dim, right_dim, precision=None):
    return lax.dot_general(
        left,
        right,
        (((left_dim,), (right_dim,)), ((), ())),
        preferred_element_type=F32,
        precision=precision,
    )


def mm(left, right):
    return dot_dims(left, right, 1, 0)


def mm_nt(left, right):
    return dot_dims(left, right, 1, 1)


def mm_tn(left, right):
    return dot_dims(left, right, 0, 0)


def iota(shape, dim):
    return lax.broadcasted_iota(jnp.int32, shape, dim)


def sigmoid(rows):
    return 1.0 / (1.0 + jnp.exp(-rows))


def one_hot(condition):
    return condition.astype(F32).astype(BF16)


def normed(rows, mask, width):
    mean = jnp.sum(rows * mask, axis=-1, keepdims=True) / width
    centre = (rows - mean) * mask
    invert = lax.rsqrt(jnp.sum(centre * centre, axis=-1, keepdims=True) / width + 1e-05)
    return centre * invert, invert


def norm_back(rows_hat, invert, gain, upward, mask, width):
    scaled = upward * gain
    mean = jnp.sum(scaled, axis=-1, keepdims=True) / width
    along = jnp.sum(scaled * rows_hat, axis=-1, keepdims=True) / width
    return invert * (scaled - mean * mask - rows_hat * along)


def sums_of(rows):
    return jnp.sum(rows, axis=0, keepdims=True)


def head_mask(rows, pairs, width):
    row = iota((rows, width), 0)
    first = lax.shift_right_logical(iota((rows, width), 1), 6) * pairs
    return (row >= first) & (row < first + pairs)


def repeat_rows(rows, pairs):
    row = iota((rows, pairs), 0)
    return one_hot(lax.rem(row, pairs) == iota((rows, pairs), 1))


def tower_sizes(full_width, full_hidden):
    is_text = lax.axis_index("tower") != 0
    width = jnp.where(is_text, D_TXT, full_width)
    mask = (iota((1, full_width), 1) < width).astype(F32)
    return is_text, width.astype(F32), mask


def fetch(source, target, semaphore):
    copy = pltpu.make_async_copy(source, target, semaphore)
    copy.start()
    return copy


def three_parts(rows):
    parts = []
    for _ in range(3):
        part = rows.astype(BF16).astype(F32)
        parts.append(part)
        rows = rows - part
    return jnp.concatenate(parts, axis=0).astype(BF16)


def over_tokens(tokens, size, step):
    for at in range(0, tokens, size):
        step(at, min(size, tokens - at))


def across(lane_sums, full_width):
    return jnp.concatenate([lane_sums] * (full_width // 128), axis=1)


def pooled_spots(ends_ref, is_text, pairs, copies):
    pair = lax.rem(iota((copies * pairs, pairs), 0), pairs)
    ends = jnp.where(pair == iota((copies * pairs, pairs), 1), ends_ref[...], 0).astype(F32)
    ends = jnp.sum(ends, axis=1, keepdims=True)
    firsts = (lax.rem(iota((copies * pairs, 1), 0), pairs) * IMG_TOK).astype(F32)
    return jnp.where(is_text, ends, firsts)


def embed_back(embedded, grad_unit):
    inv_norm = lax.rsqrt(jnp.sum(embedded * embedded, axis=-1, keepdims=True) + 1e-06)
    along = jnp.sum(embedded * grad_unit, axis=-1, keepdims=True)
    return (inv_norm * grad_unit - inv_norm * inv_norm * inv_norm * embedded * along).astype(BF16)


class Hidden:
    def __init__(self, widen_hbm, narrow_hbm, s_widen, s_narrow, sems, chunks):
        self.pairs = (
            (lambda at: widen_hbm.at[0, :, pl.ds(at, CHUNK)], lambda at: s_widen.at[:, pl.ds(at, CHUNK)]),
            (lambda at: narrow_hbm.at[0, pl.ds(at, CHUNK), :], lambda at: s_narrow.at[pl.ds(at, CHUNK), :]),
        )
        self.sems = sems
        self.chunks = chunks

    def copy(self, which, chunk):
        source, target = self.pairs[which]
        at = chunk * CHUNK
        if not isinstance(at, int):
            at = pl.multiple_of(at, CHUNK)
        return pltpu.make_async_copy(source(at), target(at), self.sems.at[which, chunk])

    def start(self, order):
        for chunk in range(self.chunks):
            for which in order:
                self.copy(which, chunk).start()

    def wait(self, chunk):
        self.copy(0, chunk).wait()
        self.copy(1, chunk).wait()

    def each(self, step):
        for chunk in range(self.chunks):
            self.wait(chunk)
            step(slice(chunk * CHUNK, (chunk + 1) * CHUNK))


def attend_kernel(
    dims,
    ends_ref,
    x_hbm,
    ag,
    ab,
    triple_hbm,
    triple_bias,
    wo_hbm,
    bo,
    fg,
    fb,
    ww_hbm,
    bw,
    wn_hbm,
    bn,
    lg,
    lb,
    we_hbm,
    unit_ref,
    early_ref,
    hat_hbm,
    inv_hbm,
    probs_hbm,
    keys_ref,
    embedded_ref,
    pooled_ref,
    middle_ref,
    slope_ref,
    s_x,
    s_one,
    s_hat,
    s_inv,
    s_probs,
    s_key,
    s_value,
    s_triple,
    s_wo,
    s_ww,
    s_wn,
    s_we,
    s_low,
    sems,
    hidden_sems,
):
    pairs, tokens, full_width, full_hidden = dims
    is_text, width, mask = tower_sizes(full_width, full_hidden)
    rows = full_width // HEAD * pairs
    get_x = fetch(x_hbm.at[0], s_x, sems.at[0])
    get_triple = fetch(triple_hbm.at[0], s_triple, sems.at[1])
    gain, shift = ag[...] * mask, ab[...] * mask
    ones = one_hot((iota((full_width, 128), 0)).astype(F32) < width)
    hidden = Hidden(ww_hbm, wn_hbm, s_ww, s_wn, hidden_sems, full_hidden // CHUNK)
    get_x.wait()
    get_wo = fetch(wo_hbm.at[0], s_wo, sems.at[2])
    hidden.start((0, 1))
    get_we = fetch(we_hbm.at[0], s_we, sems.at[3])

    def norm_rows(at, count):
        here = pl.ds(at, count)
        low = s_x[here, :]
        mean = mm(low, ones) / width
        centre = low.astype(F32) - across(mean, full_width)
        square = centre * centre
        high = square.astype(BF16)
        low = (square - high.astype(F32)).astype(BF16)
        invert = lax.rsqrt((mm(high, ones) + mm(low, ones)) / width + 1e-05)
        hat = centre * across(invert, full_width)
        s_hat[here, :] = hat.astype(BF16)
        s_one[here, :] = (hat * gain + shift).astype(BF16)
        s_inv[here, :] = invert

    over_tokens(tokens, NORM_ROWS, norm_rows)
    put_hat = fetch(s_hat, hat_hbm, sems.at[4])
    put_inv = fetch(s_inv, inv_hbm, sems.at[5])
    pick = one_hot(iota((pairs, tokens), 1).astype(F32) == pooled_spots(ends_ref, is_text, pairs, 1))
    stream_rows = mm(pick, s_x[...]) * mask
    one = mm(pick, s_one[...]).astype(BF16)
    get_triple.wait()
    query = ((mm(one, s_triple[0]) + triple_bias[0, 0:1, :]) * (mask * 0.125)).astype(BF16)
    repeat = repeat_rows(rows, pairs)
    heads = head_mask(rows, pairs, full_width)
    wide = jnp.where(heads, mm(repeat, query), 0.0).astype(BF16)

    def project(at, count):
        here = pl.ds(at, count)
        s_key[here, :] = mm(s_one[here, :], s_triple[1]).astype(BF16)
        s_value[here, :] = (mm(s_one[here, :], s_triple[2]) + triple_bias[0, 1:2, :]).astype(BF16)

    over_tokens(tokens, PROJECT_ROWS, project)
    s_probs[...] = mm_nt(wide, s_key[...])
    last = pooled_spots(ends_ref, is_text, pairs, rows // pairs)
    pair = lax.rem(iota((rows, 1), 0), pairs)
    stops = jnp.where(
        pair - 1 == iota((rows, pairs), 1), ends_ref[...] + 1, 0
    ).astype(F32)
    first = jnp.where(is_text, jnp.sum(stops, axis=1, keepdims=True), last)
    last = jnp.where(is_text, last, last + (IMG_TOK - 1.0))
    step_rows = 48
    for at in range(0, rows, step_rows):
        here = slice(at, at + step_rows)
        place = iota((step_rows, tokens), 1).astype(F32)
        allowed = (place >= first[here]) & (place <= last[here])
        scores = jnp.where(allowed, s_probs[here, :], -1e30)
        powers = jnp.exp(scores - jnp.max(scores, axis=1, keepdims=True))
        probs = powers * (1.0 / jnp.sum(powers, axis=1, keepdims=True))
        s_low[here, :] = probs.astype(BF16)
    put_probs = fetch(s_low, probs_hbm, sems.at[6])
    mixed_wide = mm(s_low[...], s_value[...])
    mixed = mm_tn(repeat, jnp.where(heads, mixed_wide, 0.0).astype(BF16))
    mixed = (mixed * mask).astype(BF16)
    early_ref[:, 0:full_width] = mixed
    early_ref[:, full_width : 2 * full_width] = stream_rows.astype(BF16)
    get_wo.wait()
    middle = stream_rows + mm(mixed, s_wo[...]) + bo[...]
    middle_ref[...] = middle
    mid_hat, _ = normed(middle, mask, width)
    two = ((mid_hat * fg[...] + fb[...]) * mask).astype(BF16)
    pooled_ref[...] = middle + bn[...]
    hidden_width = jnp.where(is_text, MLP_TXT, full_hidden)
    hidden_mask = (iota((1, full_hidden), 1) < hidden_width).astype(F32)

    def forward(at):
        pre = mm(two, s_ww[:, at]) + bw[:, at]
        gate = sigmoid(1.702 * pre)
        active = pre * gate * hidden_mask[:, at]
        slope_ref[:, at] = (gate + 1.702 * active * (1.0 - gate)) * hidden_mask[:, at]
        pooled_ref[...] += mm(active.astype(BF16), s_wn[at, :])

    hidden.each(forward)
    out_hat, out_inv = normed(pooled_ref[...], mask, width)
    early_ref[:, 2 * full_width : 3 * full_width] = out_hat.astype(BF16)
    lane = iota((pairs, 128), 1)
    numbers = jnp.zeros((pairs, 128), F32)
    for place in range(3):
        part = out_inv.astype(BF16).astype(F32)
        numbers = jnp.where(lane == place, part, numbers)
        out_inv = out_inv - part
    early_ref[:, 3 * full_width :] = numbers.astype(BF16)
    three = ((out_hat * lg[...] + lb[...]) * mask).astype(BF16)
    get_we.wait()
    embedded = mm(three, s_we[...])
    embedded_ref[...] = embedded
    unit_ref[...] = (
        embedded * lax.rsqrt(jnp.sum(embedded * embedded, axis=-1, keepdims=True) + 1e-06)
    ).astype(BF16)
    keys_ref[...] = mm_nt(wide, s_triple[1]).astype(BF16)
    for copy in (put_hat, put_inv, put_probs):
        copy.wait()


def means_kernel(
    dims,
    ends_ref,
    ag,
    ab,
    hat_ref,
    probs_ref,
    turned_ref,
    spread_ref,
    hat_rows_ref,
    s_turn,
):
    pairs, tokens, full_width, full_hidden = dims
    is_text, width, mask = tower_sizes(full_width, full_hidden)
    rows = probs_ref.shape[0]
    low = probs_ref[...]
    spread = mm(low, hat_ref[...])
    spread_ref[...] = spread.astype(BF16)
    total = jnp.sum(low.astype(F32), axis=1, keepdims=True)
    s_turn[rows:, :] = jnp.zeros((s_turn.shape[0] - rows, full_width), F32)
    s_turn[0:rows, :] = (spread * ag[...] + total * ab[...]) * mask
    turned_ref[...] = s_turn[...].T.astype(BF16)
    pick = one_hot(iota((pairs, tokens), 1).astype(F32) == pooled_spots(ends_ref, is_text, pairs, 1))
    hat_rows_ref[...] = mm(pick, hat_ref[...]).astype(BF16)


def in_order(pieces, stages, pairs, block, at):
    here = lax.axis_index("dp")
    row = at + iota((block, 1), 0)
    owner = lax.div(row, pairs)
    apart = lax.bitwise_xor(owner, here)
    place = jnp.zeros_like(owner)
    weight = 1
    for shift, bits in stages:
        digit = lax.bitwise_and(lax.shift_right_logical(apart, shift), (1 << bits) - 1)
        place = place + digit * weight
        weight = weight << bits
    column = place * pairs + row - owner * pairs
    total = None
    first = 0
    for piece in pieces:
        count = piece.shape[0]
        part = mm(one_hot(iota((block, count), 1) + first == column), piece[...])
        total = part if total is None else total + part
        first += count
    return total.astype(BF16)


def over_blocks(count, step):
    if count == 1:
        step(0)
    else:

        def one(index, carry):
            step(index)
            return carry

        lax.fori_loop(0, count, one, 0)


def block_rows(total):
    return 320 if total % 320 == 0 else total


def loss_kernel(
    dims,
    own_rel,
    other_rel,
    flags_ref,
    logit_scale,
    loss_scale,
    ag,
    ab,
    triple_hbm,
    triple_bias,
    wo_hbm,
    fg,
    ww_hbm,
    wn_hbm,
    lg,
    we_hbm,
    hat_hbm,
    probs_hbm,
    spread_ref,
    keys_ref,
    embedded_ref,
    pooled_ref,
    middle_ref,
    slope_ref,
    hat_rows_ref,
    loss_ref,
    hits_ref,
    scale_ref,
    grad_all_ref,
    late_ref,
    queries_ref,
    back_ref,
    values_ref,
    rows_one_ref,
    rows_mid_ref,
    s_own,
    s_other,
    s_triple,
    s_wo,
    s_ww,
    s_wn,
    s_we,
    s_hat,
    s_probs,
    s_rows,
    s_two,
    s_turn,
    s_slab,
    sems,
    hidden_sems,
):
    pairs, tokens, full_width, full_hidden, stages = dims
    all_pairs = own_rel.shape[0]
    block = block_rows(all_pairs)
    here = lax.axis_index("dp")
    is_text, width, mask = tower_sizes(full_width, full_hidden)
    rows = full_width // HEAD * pairs
    get_we = fetch(we_hbm.at[0], s_we, sems.at[0])
    hidden = Hidden(ww_hbm, wn_hbm, s_ww, s_wn, hidden_sems, full_hidden // CHUNK)
    hidden.start((1, 0))
    get_wo = fetch(wo_hbm.at[0], s_wo, sems.at[1])
    get_triple = fetch(triple_hbm.at[0], s_triple, sems.at[2])
    get_hat = fetch(hat_hbm, s_hat, sems.at[3])
    get_probs = fetch(probs_hbm, s_probs, sems.at[4])

    def place(index):
        at = pl.multiple_of(index * block, block)
        s_own[pl.ds(at, block), :] = in_order([own_rel], stages, pairs, block, at)
        s_other[pl.ds(at, block), :] = in_order([other_rel], stages, pairs, block, at)

    over_blocks(all_pairs // block, place)
    live = (flags_ref[...] > 0).astype(F32)
    live_pairs = jnp.sum(live, axis=1, keepdims=True)
    factor = jnp.exp(logit_scale[...])
    row_weight = loss_scale[...] / (2.0 * live_pairs)
    loss_ref[...] = jnp.zeros_like(loss_ref)
    hits_ref[...] = jnp.zeros_like(hits_ref)
    scale_ref[...] = jnp.zeros_like(scale_ref)
    grad_all_ref[...] = jnp.zeros_like(grad_all_ref)

    def part(index):
        at = pl.multiple_of(index * block, block)
        eye = at + iota((block, all_pairs), 0) == iota((block, all_pairs), 1)
        live_rows = jnp.sum(jnp.where(eye, live, 0.0), axis=1, keepdims=True)

        def one_way(left, right):
            logits = mm_nt(left, right) * factor
            masked = jnp.where(live > 0.5, logits, -1e30)
            peak = jnp.max(masked, axis=1, keepdims=True)
            powers = jnp.exp(masked - peak)
            total = jnp.sum(powers, axis=1, keepdims=True)
            log_total = peak + jnp.log(total)
            matched = jnp.sum(jnp.where(eye, logits, 0.0), axis=1, keepdims=True)
            gap = jnp.where(live_rows > 0.5, log_total - matched, 0.0)
            grads = (
                (powers / total - eye.astype(F32)) * (live_rows * row_weight)
            ).astype(BF16)
            loss = jnp.sum(live_rows * gap, axis=0, keepdims=True)
            hits = jnp.sum(live_rows * jnp.exp(-gap), axis=0, keepdims=True)
            scale = jnp.sum(
                jnp.sum(grads.astype(F32) * logits, axis=1, keepdims=True),
                axis=0,
                keepdims=True,
            )
            return grads, loss, hits, scale

        own = s_own[pl.ds(at, block), :]
        other = s_other[pl.ds(at, block), :]
        grads, loss_one, hits_one, scale_one = one_way(own, s_other[...])
        grad_all_ref[pl.ds(at, block), :] += factor * mm(grads, s_other[...])
        grads, loss_two, hits_two, scale_two = one_way(other, s_own[...])
        grad_all_ref[...] += factor * mm_tn(grads, other)
        loss_ref[...] += loss_one + loss_two
        hits_ref[...] += hits_one + hits_two
        scale_ref[...] += scale_one + scale_two

    over_blocks(all_pairs // block, part)
    loss_ref[...] = loss_ref[...] / (2.0 * live_pairs)
    hits_ref[...] = hits_ref[...] / (2.0 * live_pairs)

    for pair in range(pairs):
        s_rows[pair : pair + 1, :] = grad_all_ref[pl.ds(here * pairs + pair, 1), :]

    gain, shift = ag[...] * mask, ab[...] * mask
    grad_embed = embed_back(embedded_ref[...], s_rows[...])
    get_we.wait()
    grad_three = mm_nt(grad_embed, s_we[...])
    out_hat, out_inv = normed(pooled_ref[...], mask, width)
    grad_pooled = norm_back(out_hat, out_inv, lg[...] * mask, grad_three, mask, width)
    branch = grad_pooled.astype(BF16)
    s_two[...] = jnp.zeros_like(s_two)

    def backward(at):
        grad_active = mm_nt(branch, s_wn[at, :])
        grad_hidden = (grad_active * slope_ref[:, at]).astype(BF16)
        s_two[...] += mm_nt(grad_hidden, s_ww[:, at])

    hidden.each(backward)
    mid_hat, mid_inv = normed(middle_ref[...], mask, width)
    grad_two = s_two[...] * mask
    grad_middle = grad_pooled + norm_back(mid_hat, mid_inv, fg[...] * mask, grad_two, mask, width)
    rows_mid_ref[...] = grad_middle
    attention = grad_middle.astype(BF16)
    get_wo.wait()
    grad_mixed = (mm_nt(attention, s_wo[...]) * mask).astype(BF16)
    repeat = repeat_rows(rows, pairs)
    heads = head_mask(rows, pairs, full_width)
    wide = jnp.where(heads, mm(repeat, grad_mixed), 0.0)
    get_triple.wait()
    along = mm_nt(wide.astype(BF16), s_triple[2])
    values_low = along.astype(BF16)
    values_ref[...] = values_low
    offset = jnp.sum(along * shift, axis=1, keepdims=True) + jnp.sum(
        wide * triple_bias[0, 1:2, :], axis=1, keepdims=True
    )
    get_hat.wait()
    get_probs.wait()
    grad_probs = mm_nt((along * gain).astype(BF16), s_hat[...]) + offset
    probs = s_probs[...].astype(F32)
    prob_total = jnp.sum(probs, axis=1, keepdims=True)
    inner = jnp.sum(grad_probs * probs, axis=1, keepdims=True) / prob_total
    back = (probs * (grad_probs - inner)).astype(BF16)
    back_ref[...] = back
    spread = mm(back, s_hat[...])
    total = jnp.sum(back.astype(F32), axis=1, keepdims=True)
    means = (spread * gain + total * shift).astype(BF16)
    query_wide = mm(means, s_triple[1]) * 0.125
    grad_query = mm_tn(repeat, jnp.where(heads, query_wide, 0.0).astype(BF16)).astype(BF16)
    queries_ref[...] = grad_query
    rows_one = mm_nt(grad_query, s_triple[0]) * mask
    rows_one_ref[...] = rows_one
    values_wide = values_low.astype(F32)
    keys_wide = keys_ref[...].astype(F32)
    gain_sum = (
        sums_of(values_wide * spread_ref[...].astype(F32))
        + sums_of(keys_wide * spread)
        + sums_of(rows_one * hat_rows_ref[...].astype(F32))
    ) * mask
    shift_sum = (
        sums_of(values_wide * prob_total) + sums_of(keys_wide * total) + sums_of(rows_one)
    ) * mask
    s_turn[rows:, :] = jnp.zeros((s_turn.shape[0] - rows, full_width), F32)
    s_turn[0:rows, :] = means.astype(F32)
    slot = rows
    for vector in (gain_sum, shift_sum):
        for _ in range(3):
            low = vector.astype(BF16).astype(F32)
            s_turn[slot : slot + 1, :] = low
            vector = vector - low
            slot += 1
    lanes = s_turn.shape[0]
    late_ref[:, 0:lanes] = s_turn[...].T.astype(BF16)
    if late_ref.shape[1] > lanes:
        turned = grad_query.astype(F32).T
        slab = s_slab.shape[0]
        s_slab[...] = jnp.zeros_like(s_slab)
        for place in range(full_width // slab):
            down = slice(place * slab, (place + 1) * slab)
            s_slab[:, place * pairs : (place + 1) * pairs] = turned[down, :]
        slab_low = s_slab[...].astype(BF16)
        for place in range(full_width // slab):
            late_ref[place * slab : (place + 1) * slab, lanes:] = slab_low


def rows_kernel(dims, *refs):
    pairs, tokens, full_width, full_hidden, slice_width, slice_hidden, stages, pieces = dims
    early_hbm = refs[:pieces]
    (
        ends_ref,
        hat_hbm,
        inv_hbm,
        probs_hbm,
        back_ref,
        value_factors_ref,
        keys_ref,
        rows_one_ref,
        rows_mid_ref,
        means_ref,
        grad_hbm,
        ag,
        ab,
        triple_hbm,
        triple_bias,
        wo_hbm,
        bo,
        fg,
        fb,
        ww_hbm,
        bw,
        wn_hbm,
        lg,
        lb,
        we_hbm,
        out_hbm,
        ones_ref,
        queries_ref,
        values_ref,
        embed_ref,
        narrow_ref,
        widen_ref,
        mixer_ref,
        final_gain_ref,
        final_bias_ref,
        feed_gain_ref,
        feed_bias_ref,
        narrow_bias_ref,
        mixer_bias_ref,
        value_bias_ref,
        widen_bias_ref,
        value_weight_ref,
        s_triple,
        s_wo,
        s_ww,
        s_wn,
        s_we,
        s_vectors,
        s_hat,
        s_inv,
        s_left,
        s_right,
        s_early,
        grad_ref,
        s_out,
        s_total,
        s_active,
        s_hidden,
        s_means,
        sems,
        hidden_sems,
        out_sems,
    ) = refs[pieces:]
    all_pairs = grad_ref.shape[0]
    block = block_rows(all_pairs)
    here = lax.axis_index("dp")
    is_text, width, mask = tower_sizes(full_width, full_hidden)
    get_probs = fetch(probs_hbm, s_left.at[pl.ds(0, full_width // HEAD * pairs), :], sems.at[3])
    get_hat = fetch(hat_hbm, s_hat, sems.at[4])
    get_inv = fetch(inv_hbm, s_inv, sems.at[5])
    get_grad = fetch(grad_hbm, grad_ref, sems.at[6])
    height = s_early.shape[0] // pieces
    early = [s_early.at[pl.ds(place * height, height), :] for place in range(pieces)]
    get_early = [fetch(early_hbm[place], early[place], sems.at[7 + place]) for place in range(pieces)]
    get_wo = fetch(wo_hbm.at[0], s_wo, sems.at[1])
    get_we = fetch(we_hbm.at[0], s_we, sems.at[2])
    hidden = Hidden(ww_hbm, wn_hbm, s_ww, s_wn, hidden_sems, full_hidden // CHUNK)
    hidden.start((0, 1))
    get_triple = fetch(triple_hbm.at[0, 0], s_triple, sems.at[0])
    rows = full_width // HEAD * pairs
    token_gain = ag[...] * mask
    s_left[rows : 2 * rows, :] = back_ref[...]
    s_right[0:rows, :] = value_factors_ref[...]
    s_right[rows : 2 * rows, :] = keys_ref[...]
    spots = pooled_spots(ends_ref, is_text, pairs, 3)
    s_left[2 * rows :, :] = one_hot(iota((3 * pairs, tokens), 1).astype(F32) == spots)
    s_right[2 * rows :, :] = three_parts(rows_one_ref[...])
    middle_parts = three_parts(rows_mid_ref[...])
    ones = one_hot(iota((full_width, 128), 0).astype(F32) < width)
    get_probs.wait()
    get_hat.wait()
    get_inv.wait()

    def put(at, count):
        spot = pl.ds(at, count)
        return pltpu.make_async_copy(
            s_out.at[spot, :], out_hbm.at[0, spot, :], out_sems.at[at // STREAM_ROWS]
        )

    def norm_rows(at, count):
        spot = pl.ds(at, count)
        upward = mm_tn(s_left[:, spot], s_right[...])
        hat = s_hat[spot, :].astype(F32)
        scaled = upward * token_gain
        mean = mm(scaled.astype(BF16), ones) / width
        along = mm((scaled * hat).astype(BF16), ones) / width
        s_out[spot, :] = across(s_inv[spot, :], full_width) * (
            scaled - (across(mean, full_width) + hat * across(along, full_width)) * mask
        ) + mm_tn(s_left[2 * rows :, spot], middle_parts)
        put(at, count).start()

    over_tokens(tokens, STREAM_ROWS, norm_rows)
    for ref in (embed_ref, narrow_ref, widen_ref, mixer_ref, widen_bias_ref, s_vectors):
        ref[...] = jnp.zeros_like(ref)
    lane = iota((full_width, slice_width), 0)
    pick = one_hot(
        (lane == here * slice_width + iota((full_width, slice_width), 1))
        & (lane.astype(F32) < width)
    )
    hidden_width = jnp.where(is_text, MLP_TXT, full_hidden)
    gain, shift = lg[...] * mask, lb[...] * mask
    feed_gain = fg[...] * mask
    get_wo.wait()
    get_we.wait()
    get_grad.wait()
    for copy in get_early:
        copy.wait()

    def part(index):
        at = pl.multiple_of(index * block, block)
        here_rows = pl.ds(at, block)
        arrived = in_order(early, stages, pairs, block, at)
        mixed = arrived[:, 0:full_width]
        stream_rows = arrived[:, full_width : 2 * full_width].astype(F32)
        out_hat = arrived[:, 2 * full_width : 3 * full_width].astype(F32)
        out_inv = jnp.sum(arrived[:, 3 * full_width :].astype(F32), axis=1, keepdims=True)
        three = (out_hat * gain + shift).astype(BF16)
        grad_embed = embed_back(mm(three, s_we[...]), grad_ref[here_rows, :])
        embed_ref[0] += mm_tn(mm(three, pick).astype(BF16), grad_embed)
        grad_three = mm_nt(grad_embed, s_we[...])
        s_vectors[0:1, :] += sums_of(grad_three * out_hat)
        s_vectors[1:2, :] += sums_of(grad_three)
        grad_pooled = norm_back(out_hat, out_inv, gain, grad_three, mask, width)
        branch = grad_pooled.astype(BF16)
        s_vectors[2:3, :] += sums_of(branch.astype(F32))
        middle = stream_rows + mm(mixed, s_wo[...]) + bo[...]
        mid_hat, mid_inv = normed(middle, mask, width)
        two = ((mid_hat * fg[...] + fb[...]) * mask).astype(BF16)
        s_total[...] = jnp.zeros_like(s_total)
        s_active[...] = jnp.zeros_like(s_active)
        s_hidden[...] = jnp.zeros_like(s_hidden)

        def through(chunk, carry):
            first = pl.multiple_of(chunk * CHUNK, CHUNK)
            lanes = pl.ds(first, CHUNK)
            if all_pairs == block:
                hidden.wait(chunk)
            pre = mm(two, s_ww[:, lanes]) + bw[:, lanes]
            gate = sigmoid(1.702 * pre)
            active = pre * gate
            there = (first + iota((1, CHUNK), 1) < hidden_width).astype(F32)
            slope = (gate + 1.702 * active * (1.0 - gate)) * there
            grad_hidden = (mm_nt(branch, s_wn[lanes, :]) * slope).astype(BF16)
            s_total[...] += mm_nt(grad_hidden, s_ww[:, lanes])
            row = first + iota((CHUNK, slice_hidden), 0)
            chosen = one_hot(
                (row == here * slice_hidden + iota((CHUNK, slice_hidden), 1))
                & (row < hidden_width)
            )
            s_active[...] += mm(active.astype(BF16), chosen)
            s_hidden[...] += mm(grad_hidden, chosen)
            return carry

        lax.fori_loop(0, full_hidden // CHUNK, through, 0)
        grad_two, active_slice, hidden_slice = s_total[...], s_active[...], s_hidden[...]
        narrow_ref[0] += mm_tn(active_slice.astype(BF16), branch)
        widen_ref[0] += mm_tn(hidden_slice.astype(BF16), two)
        widen_bias_ref[...] += sums_of(hidden_slice)
        s_vectors[3:4, :] += sums_of(grad_two * mid_hat)
        s_vectors[4:5, :] += sums_of(grad_two)
        grad_middle = grad_pooled + norm_back(mid_hat, mid_inv, feed_gain, grad_two, mask, width)
        attention = grad_middle.astype(BF16)
        s_vectors[5:6, :] += sums_of(attention.astype(F32))
        mixer_ref[0] += mm_tn(mm(mixed, pick).astype(BF16), attention)
        grad_mixed = (mm_nt(attention, s_wo[...]) * mask).astype(BF16)
        values_ref[here_rows, :] = grad_mixed
        s_vectors[6:7, :] += sums_of(grad_mixed.astype(F32))
        rows_hat, _ = normed(stream_rows, mask, width)
        one = ((rows_hat * ag[...] + ab[...]) * mask).astype(BF16)
        ones_ref[here_rows, :] = mm(one, pick).astype(BF16)
        if all_pairs == block:
            get_triple.wait()
        query = (mm(one, s_triple[...]) + triple_bias[0, 0:1, :]) * mask
        queries_ref[here_rows, :] = query.astype(BF16)

    if all_pairs != block:
        get_triple.wait()
        for chunk in range(full_hidden // CHUNK):
            hidden.wait(chunk)
    over_blocks(all_pairs // block, part)
    over_tokens(tokens, STREAM_ROWS, lambda at, count: put(at, count).wait())
    count = means_ref.shape[0]
    if count <= 16 and slice_width % 16 == 0:
        from_heads(
            [means_ref.at[source] for source in range(count)],
            values_ref,
            value_weight_ref,
            s_means,
            pairs,
            slice_width,
        )
    vectors = dot_dims(s_vectors[...], pick.astype(F32), 1, 0, lax.Precision.HIGHEST)
    for slot, ref in enumerate(
        (
            final_gain_ref,
            final_bias_ref,
            narrow_bias_ref,
            feed_gain_ref,
            feed_bias_ref,
            mixer_bias_ref,
            value_bias_ref,
        )
    ):
        ref[...] = vectors[slot : slot + 1, :]


def from_heads(sources, right_ref, out_ref, s_left, pairs, slice_width):
    heads = right_ref.shape[1] // HEAD
    for head in range(heads):
        down = slice(head * slice_width, (head + 1) * slice_width)
        lane = slice(head * pairs, (head + 1) * pairs)
        s_left[down, :] = jnp.concatenate([source[:, lane] for source in sources], axis=1)
    left = iota((slice_width, 2 * HEAD), 1) < HEAD
    for two in range(heads // 2):
        down = slice(two * 2 * slice_width, (two + 1) * 2 * slice_width)
        lane = slice(two * 2 * HEAD, (two + 1) * 2 * HEAD)
        both = mm(s_left[down, :], right_ref[:, lane])
        out_ref[:, lane] = jnp.where(left, both[0:slice_width], both[slice_width:])


def last_kernel(dims, *refs):
    pairs, full_width, full_hidden, slice_width, stages, pieces = dims
    arrived = refs[:pieces]
    (
        late_ref,
        means_ref,
        ones_ref,
        queries_ref,
        values_ref,
        value_bias_ref,
        value_weight_ref,
        triple_ref,
        gain_ref,
        shift_ref,
        bias_ref,
        s_keys,
        s_turned,
        s_late,
        s_sums,
    ) = refs[pieces:]
    here = lax.axis_index("dp")
    count = late_ref.shape[0]
    lanes = -(-(full_width // HEAD * pairs + 12) // 128) * 128
    heads = full_width // HEAD
    rows = heads * pairs
    all_pairs = queries_ref.shape[0]
    s_late[...] = jnp.zeros_like(s_late)
    if not arrived:
        sources = range(count)
        for source in sources:
            s_late[...] += late_ref[source, :, 0:lanes].astype(F32)
        from_heads(
            [late_ref.at[source] for source in sources],
            queries_ref,
            triple_ref.at[0, 1],
            s_keys,
            pairs,
            slice_width,
        )
        triple_ref[0, 1] = triple_ref[0, 1] * 0.125
        triple_ref[0, 2] = value_weight_ref[...]
        for slab in sources:
            down = slice(slab * slice_width, (slab + 1) * slice_width)
            lane = slice(lanes + slab * pairs, lanes + (slab + 1) * pairs)
            s_turned[down, :] = jnp.concatenate([late_ref[source, :, lane] for source in sources], axis=1)
        triple_ref[0, 0] = mm(s_turned[...], ones_ref[...]).T
        mine = s_turned[pl.ds(pl.multiple_of(here * slice_width, slice_width), slice_width), :]
        sums = mm_nt(jnp.ones((8, all_pairs), BF16), mine)
    else:
        block = block_rows(all_pairs)
        triple_ref[...] = jnp.zeros_like(triple_ref)
        s_sums[...] = jnp.zeros_like(s_sums)

        def part(index):
            at = pl.multiple_of(index * block, block)
            grad_query = in_order(arrived, stages, pairs, block, at)
            triple_ref[0, 0] += mm_tn(ones_ref[pl.ds(at, block), :], grad_query)
            s_sums[0:1, :] += sums_of(grad_query.astype(F32))

        over_blocks(all_pairs // block, part)
        head = head_mask(lanes, pairs, full_width)

        def one(source, carry):
            now = late_ref[source]
            s_late[...] += now.astype(F32)
            row = iota((lanes, all_pairs), 0)
            column = iota((lanes, all_pairs), 1)
            repeat = one_hot((column == source * pairs + lax.rem(row, pairs)) & (row < rows))
            means = means_ref[source]
            for which, left, origin in ((1, now, queries_ref), (2, means, values_ref)):
                wide = jnp.where(head, mm(repeat, origin[...]), 0.0).astype(BF16)
                triple_ref[0, which] += mm(left, wide)
            return carry

        lax.fori_loop(0, count, one, 0)
        triple_ref[0, 1] = triple_ref[0, 1] * 0.125
        pick = (
            iota((full_width, slice_width), 0)
            == here * slice_width + iota((full_width, slice_width), 1)
        ).astype(F32)
        sums = dot_dims(s_sums[...], pick, 1, 0, lax.Precision.HIGHEST)
    lane = iota((8, lanes), 1)
    row = iota((8, lanes), 0)
    slot = rows + row * 3
    chosen = ((lane >= slot) & (lane < slot + 3) & (row < 2)).astype(F32)
    from_late = dot_dims(chosen, s_late[...], 1, 1, lax.Precision.HIGHEST)
    gain_ref[...] = from_late[0:1, :]
    shift_ref[...] = from_late[1:2, :]
    bias_ref[0, 0:1, :] = sums[0:1, :]
    bias_ref[0, 1:2, :] = value_bias_ref[...]


def stages_of(count):
    bits = count.bit_length() - 1
    stages = []
    while bits > 0:
        take = 2 if bits >= 2 else 1
        bits -= take
        stages.append((bits, take))
    return tuple(stages)


def exchange(block, axis, stage):
    count = lax.axis_size(axis)
    shift, bits = stage
    parts = [block]
    for apart in range(1, 1 << bits):
        route = [(low, low ^ (apart << shift)) for low in range(count)]
        parts.append(lax.ppermute(block, axis, route))
    return parts


def call(
    kernel, ins, outs, scratch, in_hbm=(), out_hbm=(), cost=None, kept=(), limit=VMEM_LIMIT
):
    vmem = pl.BlockSpec(memory_space=pltpu.VMEM)
    anywhere = pl.BlockSpec(memory_space=pl.ANY)
    specs = [anywhere if index in in_hbm else vmem for index in range(len(ins))]
    out_specs = [anywhere if index in out_hbm else vmem for index in range(len(outs))]
    if kept:
        ins = [
            pltpu.with_memory_space_constraint(
                array, pltpu.VMEM if index in kept else pltpu.HBM
            )
            for index, array in enumerate(ins)
        ]
    flops, moved = cost
    return pl.pallas_call(
        kernel,
        out_shape=[jax.ShapeDtypeStruct(shape, kind) for shape, kind in outs],
        in_specs=specs,
        out_specs=out_specs,
        scratch_shapes=scratch,
        compiler_params=pltpu.CompilerParams(vmem_limit_bytes=limit),
        cost_estimate=pl.CostEstimate(flops=flops, bytes_accessed=moved, transcendentals=0),
    )(*ins)


def body(
    block_input,
    segments,
    caption_ends,
    pair_flags,
    attention_gain,
    attention_bias,
    triple_weight,
    triple_bias,
    mixer_weight,
    mixer_bias,
    feed_gain,
    feed_bias,
    widen_weight,
    widen_bias,
    narrow_weight,
    narrow_bias,
    final_gain,
    final_bias,
    embed_weight,
    logit_scale,
    loss_scale,
):
    tokens, width = block_input.shape[1:]
    hidden = widen_weight.shape[2]
    emb = embed_weight.shape[2]
    pairs = caption_ends.shape[0]
    count = lax.axis_size("dp")
    all_pairs = pair_flags.shape[0]
    heads = width // HEAD
    rows = heads * pairs
    lanes = -(-(rows + 12) // 128) * 128
    slice_width = width // count
    slice_hidden = hidden // count
    stages = stages_of(count)
    compact = count <= 16 and slice_width % 16 == 0
    slab_lanes = -(-all_pairs // 128) * 128
    ends = caption_ends.reshape(1, pairs)
    dma = pltpu.SemaphoreType.DMA
    weights_scratch = [
        pltpu.VMEM((3, width, width), BF16),
        pltpu.VMEM((width, width), BF16),
        pltpu.VMEM((width, hidden), BF16),
        pltpu.VMEM((hidden, width), BF16),
        pltpu.VMEM((width, emb), BF16),
    ]
    dims = (pairs, tokens, width, hidden)
    chunk_count = hidden // CHUNK
    (
        unit,
        early,
        hat,
        invert,
        probs,
        keys,
        embedded,
        pooled,
        middle,
        slope,
    ) = call(
        partial(attend_kernel, dims),
        (
            ends,
            block_input,
            attention_gain,
            attention_bias,
            triple_weight,
            triple_bias,
            mixer_weight,
            mixer_bias,
            feed_gain,
            feed_bias,
            widen_weight,
            widen_bias,
            narrow_weight,
            narrow_bias,
            final_gain,
            final_bias,
            embed_weight,
        ),
        [
            ((pairs, emb), BF16),
            ((pairs, 3 * width + 128), BF16),
            ((tokens, width), BF16),
            ((tokens, 128), F32),
            ((rows, tokens), BF16),
            ((rows, width), BF16),
            ((pairs, emb), F32),
            ((pairs, width), F32),
            ((pairs, width), F32),
            ((pairs, hidden), F32),
        ],
        [
            pltpu.VMEM((tokens, width), BF16),
            pltpu.VMEM((tokens, width), BF16),
            pltpu.VMEM((tokens, width), BF16),
            pltpu.VMEM((tokens, 128), F32),
            pltpu.VMEM((rows, tokens), F32),
            pltpu.VMEM((tokens, width), BF16),
            pltpu.VMEM((tokens, width), BF16),
        ]
        + weights_scratch
        + [
            pltpu.VMEM((rows, tokens), BF16),
            dma((7,)),
            dma((2, chunk_count)),
        ],
        in_hbm=(1, 4, 6, 10, 12, 16),
        out_hbm=(2, 3, 4),
        cost=(10**9, 20 * 10**6),
    )
    turned, spread, hat_rows = call(
        partial(means_kernel, dims),
        (ends, attention_gain, attention_bias, hat, probs),
        [
            ((width, lanes), BF16),
            ((rows, width), BF16),
            ((pairs, width), BF16),
        ],
        [
            pltpu.VMEM((lanes, width), F32),
        ],
        cost=(10**9, 5 * 10**6),
    )
    early_rows, own_rel = early, unit
    flags = pair_flags.reshape(1, all_pairs)
    for index, stage in enumerate(stages):
        own_parts = exchange(own_rel, "dp", stage)
        if index + 1 < len(stages):
            own_parts, early_rows, turned, spread, keys, hat_rows = lax.optimization_barrier(
                (own_parts, early_rows, turned, spread, keys, hat_rows)
            )
            early_rows = jnp.concatenate(exchange(early_rows, "dp", stage), axis=0)
        own_rel = jnp.concatenate(own_parts, axis=0)
    means_all = lax.all_to_all(turned, "dp", 0, 0, tiled=True).reshape(count, slice_width, lanes)
    other_rel = lax.ppermute(own_rel, "tower", [(0, 1), (1, 0)])
    early_pieces = exchange(early_rows, "dp", stages[-1])
    (
        loss,
        hits,
        scale,
        grad_all,
        late,
        queries,
        back,
        values,
        rows_one,
        rows_mid,
    ) = call(
        partial(loss_kernel, dims + (stages,)),
        (
            own_rel,
            other_rel,
            flags,
            logit_scale.reshape(1, 1),
            loss_scale.reshape(1, 1),
            attention_gain,
            attention_bias,
            triple_weight,
            triple_bias,
            mixer_weight,
            feed_gain,
            widen_weight,
            narrow_weight,
            final_gain,
            embed_weight,
            hat,
            probs,
            spread,
            keys,
            embedded,
            pooled,
            middle,
            slope,
            hat_rows,
        ),
        [
            ((1, 1), F32),
            ((1, 1), F32),
            ((1, 1), F32),
            ((all_pairs, emb), F32),
            ((width, lanes + (slab_lanes if compact else 0)), BF16),
            ((pairs, width), BF16),
            ((rows, tokens), BF16),
            ((rows, width), BF16),
            ((pairs, width), F32),
            ((pairs, width), F32),
        ],
        [pltpu.VMEM((all_pairs, emb), BF16), pltpu.VMEM((all_pairs, emb), BF16)]
        + weights_scratch
        + [
            pltpu.VMEM((tokens, width), BF16),
            pltpu.VMEM((rows, tokens), BF16),
            pltpu.VMEM((pairs, emb), F32),
            pltpu.VMEM((pairs, width), F32),
            pltpu.VMEM((lanes, width), F32),
            pltpu.VMEM((slice_width, slab_lanes), F32),
            dma((5,)),
            dma((2, chunk_count)),
        ],
        in_hbm=(7, 9, 11, 12, 14, 15, 16),
        cost=(10**9, 20 * 10**6),
    )
    early_pieces, late, queries = lax.optimization_barrier((early_pieces, late, queries))
    late_all = lax.all_to_all(late, "dp", 0, 0, tiled=True)
    late_all = late_all.reshape(count, slice_width, late.shape[1])
    late_pieces = []
    if not compact:
        late_pieces = [queries]
        for stage in stages:
            late_pieces = exchange(jnp.concatenate(late_pieces, axis=0), "dp", stage)
    ahead = len(early_pieces)
    vector = ((1, slice_width), F32)
    (
        block_grad,
        ones,
        query_rows,
        value_rows,
        grad_embed,
        grad_narrow,
        grad_widen,
        grad_mixer,
        grad_final_gain,
        grad_final_bias,
        grad_feed_gain,
        grad_feed_bias,
        grad_narrow_bias,
        grad_mixer_bias,
        grad_value_bias,
        grad_widen_bias,
        grad_value_weight,
    ) = call(
        partial(
            rows_kernel,
            (pairs, tokens, width, hidden, slice_width, slice_hidden, stages, ahead),
        ),
        tuple(early_pieces)
        + (
            ends,
            hat,
            invert,
            probs,
            back,
            values,
            keys,
            rows_one,
            rows_mid,
            means_all,
            grad_all,
            attention_gain,
            attention_bias,
            triple_weight,
            triple_bias,
            mixer_weight,
            mixer_bias,
            feed_gain,
            feed_bias,
            widen_weight,
            widen_bias,
            narrow_weight,
            final_gain,
            final_bias,
            embed_weight,
        ),
        [
            ((1, tokens, width), F32),
            ((all_pairs, slice_width), BF16),
            ((all_pairs, width), BF16),
            ((all_pairs, width), BF16),
            ((1, slice_width, emb), F32),
            ((1, slice_hidden, width), F32),
            ((1, slice_hidden, width), F32),
            ((1, slice_width, width), F32),
        ]
        + [vector] * 7
        + [((1, slice_hidden), F32), ((slice_width, width), F32)],
        [pltpu.VMEM((width, width), BF16)]
        + weights_scratch[1:]
        + [
            pltpu.VMEM((8, width), F32),
            pltpu.VMEM((tokens, width), BF16),
            pltpu.VMEM((tokens, 128), F32),
            pltpu.VMEM((2 * rows + 3 * pairs, tokens), BF16),
            pltpu.VMEM((2 * rows + 3 * pairs, width), BF16),
            pltpu.VMEM((all_pairs, 3 * width + 128), BF16),
            pltpu.VMEM((all_pairs, emb), F32),
            pltpu.VMEM((tokens, width), F32),
            pltpu.VMEM((block_rows(all_pairs), width), F32),
            pltpu.VMEM((block_rows(all_pairs), slice_hidden), F32),
            pltpu.VMEM((block_rows(all_pairs), slice_hidden), F32),
            pltpu.VMEM((width // HEAD * slice_width if compact else 16, all_pairs), BF16),
            dma((7 + ahead,)),
            dma((2, chunk_count)),
            dma((-(-tokens // STREAM_ROWS),)),
        ],
        in_hbm=tuple(range(ahead)) + tuple(ahead + index for index in (1, 2, 3, 10, 13, 15, 19, 21, 24)),
        out_hbm=(0,),
        cost=(3 * 10**9, 10 * 10**6),
    )
    grad_triple, grad_gain, grad_bias, grad_triple_bias = call(
        partial(last_kernel, (pairs, width, hidden, slice_width, stages, len(late_pieces))),
        tuple(late_pieces)
        + (late_all, means_all, ones, query_rows, value_rows, grad_value_bias, grad_value_weight),
        [
            ((1, 3, slice_width, width), F32),
            vector,
            vector,
            ((1, 2, slice_width), F32),
        ],
        [
            pltpu.VMEM((width // HEAD * slice_width, all_pairs), BF16),
            pltpu.VMEM((width, all_pairs), BF16),
            pltpu.VMEM((slice_width, lanes), F32),
            pltpu.VMEM((8, width), F32),
        ],
        cost=(10**9, 10 * 10**6),
        in_hbm=(1, 4) if compact else (),
        kept=(0,) if compact else (),
        limit=32 * 1024 * 1024 if compact else VMEM_LIMIT,
    )
    return (
        loss[0, 0],
        hits[0, 0],
        block_grad,
        grad_gain,
        grad_bias,
        grad_triple,
        grad_triple_bias,
        grad_mixer,
        grad_mixer_bias,
        grad_feed_gain,
        grad_feed_bias,
        jnp.swapaxes(grad_widen, 1, 2),
        grad_widen_bias,
        grad_narrow,
        grad_narrow_bias,
        grad_final_gain,
        grad_final_bias,
        grad_embed,
        scale[0, 0],
    )


def solution(mesh):
    in_specs = (
        P("tower", "dp", None),
        P("dp", None),
        P("dp"),
        P(),
        P("tower", None),
        P("tower", None),
        P("tower", None, None, None),
        P("tower", None, None),
        P("tower", None, None),
        P("tower", None),
        P("tower", None),
        P("tower", None),
        P("tower", None, None),
        P("tower", None),
        P("tower", None, None),
        P("tower", None),
        P("tower", None),
        P("tower", None),
        P("tower", None, None),
        P(),
        P(),
    )
    out_specs = (
        P(),
        P(),
        P("tower", "dp", None),
        P("tower", "dp"),
        P("tower", "dp"),
        P("tower", None, "dp", None),
        P("tower", None, "dp"),
        P("tower", "dp", None),
        P("tower", "dp"),
        P("tower", "dp"),
        P("tower", "dp"),
        P("tower", None, "dp"),
        P("tower", "dp"),
        P("tower", "dp", None),
        P("tower", "dp"),
        P("tower", "dp"),
        P("tower", "dp"),
        P("tower", "dp", None),
        P(),
    )
    return jax.shard_map(body, mesh=mesh, in_specs=in_specs, out_specs=out_specs, check_vma=False)
```
